256 devices in a mesh: group: 8 (over x, y_hi), tensor: 32 (over y_lo, z, core).
Axes of the slice: x: 4, y: 4 (y_hi: 2, y_lo: 2; y = y_hi * 2 + y_lo), z: 8, core: 2. Of those that a mesh axis runs over, the one named last changes fastest.
Arguments:
- learner_hidden_state: bfloat16 [32768, 8192], P(('group', 'tensor')), may hold values from -24 to 24
- learner_cotangent: bfloat16 [32768, 5120], P(('group', 'tensor')), may hold values from -24 to 24
- adapter_down_factor: float32 [8192, 64], P('tensor'), may hold values from -0.0625 to 0.0625
- adapter_up_factor: float32 [64, 5120], replicated, may hold values from -0.078125 to 0.078125
- output_projection: bfloat16 [8192, 5120], P('tensor'), may hold values from -0.0625 to 0.0625
- query_projection: bfloat16 [5120, 8192], P(None, 'tensor'), may hold values from -0.078125 to 0.078125
- key_projection: bfloat16 [5120, 1024], P(None, 'tensor'), may hold values from -0.15625 to 0.15625
- value_projection: bfloat16 [5120, 1024], P(None, 'tensor'), may hold values from -0.078125 to 0.078125
- decoder_layer_input: bfloat16 [4, 32, 5120], P(None, 'group'), may hold values from -6 to 6
- rotated_key_cache: bfloat16 [32, 4096, 1024], P('group', 'tensor'), may hold values from -720 to 720
- value_cache_store: bfloat16 [32, 4096, 1024], P('group', 'tensor'), may hold values from -16 to 16
- cache_fill_length: int32 [32], P('group'), may hold values from 1 to 4096, as said below
- rotary_start_position: int32 [32], P('group'), may hold values from 0 to 8191
- rollout_live_steps: int32 [32], P('group'), may hold values from 1 to 4, as said below
Outputs:
- decoded: bfloat16 [4, 32, 5120], P(None, 'group', 'tensor')
- fresh_down_factor: float32 [8192, 64], P('tensor')
- fresh_up_factor: float32 [64, 5120], P(None, ('group', 'tensor'))
The draws below stay inside these ranges and needn't reach their ends.
Inputs may be any that keep to these rules, and one draw needn't show every extreme that they name: `cache_fill_length`: some rollout's cache holds all 4096 positions. `rollout_live_steps`: some rollout takes all 4 steps.
All inputs are finite; a program needn't handle non-finite values.
Results may differ from the reference program's by a relative error of at most 0.03.
Values may be sent and summed in bfloat16 or wider, within the bound.
A program may use at most 128 MiB of HBM per device.

```python
import math
import jax
import jax.numpy as jnp
from jax import lax

MODEL_WIDTH = 5120
QH = 64
KVH = 8
HD = 128
ADAPTER_RANK = 64
STEPS = 4
QUERY_FEATURES = 8192
KVD = 1024
TOKENS_L = 32768
ROLLOUTS = 32
CTX = 4096


def draw_rotated_key_cache(key, part):
    key = jax.random.fold_in(key, 11)
    base = jnp.clip(2.0 * jax.random.normal(key, (ROLLOUTS, CTX, KVD), jnp.float32), -12.0, 12.0)
    return base.astype(jnp.bfloat16)


def draw_cache_fill_length(key, part):
    key = jax.random.fold_in(key, 21)
    share = jax.random.randint(jax.random.fold_in(key, 1), (ROLLOUTS,), 1, 65)
    length = jnp.maximum(CTX * share * share // 4096, 1)
    chosen = jax.random.randint(jax.random.fold_in(key, 2), (), 0, ROLLOUTS)
    return jnp.where(jnp.arange(ROLLOUTS, dtype=jnp.int32) == chosen, CTX, length).astype(jnp.int32)


def draw_rollout_live_steps(key, part):
    key = jax.random.fold_in(key, 31)
    counts = jax.random.randint(jax.random.fold_in(key, 1), (ROLLOUTS,), 1, STEPS + 1)
    chosen = jax.random.randint(jax.random.fold_in(key, 2), (), 0, ROLLOUTS)
    return jnp.where(jnp.arange(ROLLOUTS, dtype=jnp.int32) == chosen, STEPS, counts).astype(jnp.int32)


def plant(values, rng, smallest, top_value):
    longest = values.shape.index(max(values.shape))
    spots = []
    for shift in (0, 1):
        where = [jax.random.randint(jax.random.fold_in(rng, axis), (), 0, length) for axis, length in enumerate(values.shape)]
        where[longest] = (where[longest] + shift) % values.shape[longest]
        spots.append(tuple(where))
    return values.at[spots[0]].set(smallest).at[spots[1]].set(top_value)


def strengthened(drawn, stream_key, source, target, blocks, factor):
    def block_of(axis_at):
        return (jnp.arange(drawn.shape[axis_at]) // (drawn.shape[axis_at] // blocks)).reshape((-1,) + (1,) * (drawn.ndim - 1 - axis_at))

    first = jax.random.permutation(stream_key, blocks)[block_of(target)]
    other_side = (block_of(target) + blocks // 2) % blocks
    return jnp.where((block_of(source) == first) | (block_of(source) == other_side), factor * drawn, drawn)


def levels(key, extent, pieces, low, high):
    loudness = 1.0
    for dim, shards_of in pieces:
        steps = jax.random.uniform(jax.random.fold_in(jax.random.fold_in(key, 6), dim), (shards_of,), jnp.float32, low / len(pieces), high / len(pieces))
        loudness = loudness * jnp.repeat(jnp.exp(steps), extent[dim] // shards_of).reshape((-1,) + (1,) * (len(extent) - 1 - dim))
    return loudness


def gaussian(rng, dims, deviation, most, cuts=(), kind=jnp.bfloat16):
    drawn = deviation * jax.random.normal(rng, dims, jnp.float32)
    if cuts:
        drawn = drawn * levels(rng, dims, cuts, -0.22, 0.18)
    return jnp.clip(drawn, -most, most).astype(kind)


def noise_with(rng, shape, deviation, reach, split, heavy, kind=jnp.bfloat16):
    array = deviation * jax.random.normal(rng, shape, jnp.float32)
    if split:
        array = array * levels(rng, shape, split, -0.22, 0.18)
    return jnp.clip(strengthened(array, jax.random.fold_in(rng, 3), *heavy), -reach, reach).astype(kind)


def setup_inputs(seed: int = 0) -> dict:
    splits = jax.random.split(jax.random.key(seed), 15)
    learner_hidden_state = noise_with(splits[0], (TOKENS_L, QUERY_FEATURES), 1.0, 24.0, ((0, 256),), (0, 1, 256, 6.0))
    learner_cotangent = noise_with(splits[1], (TOKENS_L, MODEL_WIDTH), 1.0, 24.0, ((0, 256),), (0, 1, 256, 6.0))
    adapter_down_factor = gaussian(splits[2], (QUERY_FEATURES, ADAPTER_RANK), QUERY_FEATURES ** -0.5, 0.0625, ((0, 32),), jnp.float32)
    adapter_up_factor = gaussian(splits[3], (ADAPTER_RANK, MODEL_WIDTH), MODEL_WIDTH ** -0.5, 0.078125, (), jnp.float32)
    output_projection = gaussian(splits[4], (QUERY_FEATURES, MODEL_WIDTH), QUERY_FEATURES ** -0.5, 0.0625, ((0, 32),))
    query_projection = gaussian(splits[5], (MODEL_WIDTH, QUERY_FEATURES), MODEL_WIDTH ** -0.5, 0.078125, ((1, 32),))
    key_projection = gaussian(splits[6], (MODEL_WIDTH, KVD), (MODEL_WIDTH // 4) ** -0.5, 0.15625, ((1, 32),))
    value_projection = gaussian(splits[7], (MODEL_WIDTH, KVD), MODEL_WIDTH ** -0.5, 0.078125, ((1, 32),))
    decoder_layer_input = gaussian(splits[8], (STEPS, ROLLOUTS, MODEL_WIDTH), 1.0, 6.0, ((1, 8),))
    rotated_key_cache = draw_rotated_key_cache(jax.random.fold_in(splits[14], 71), 0)
    value_cache_store = gaussian(splits[10], (ROLLOUTS, CTX, KVD), 3.0, 16.0, ((0, 8), (1, 32)))
    cache_fill_length = draw_cache_fill_length(jax.random.fold_in(splits[14], 71), 0)
    rotary_start_position = plant(jax.random.randint(splits[12], (ROLLOUTS,), 0, 2 * CTX), jax.random.fold_in(splits[12], 1), 0, (2 * CTX) - 1).astype(jnp.int32)
    rollout_live_steps = draw_rollout_live_steps(jax.random.fold_in(splits[14], 71), 0)
    return {"learner_hidden_state": learner_hidden_state, "learner_cotangent": learner_cotangent, "adapter_down_factor": adapter_down_factor, "adapter_up_factor": adapter_up_factor, "output_projection": output_projection, "query_projection": query_projection, "key_projection": key_projection, "value_projection": value_projection, "decoder_layer_input": decoder_layer_input, "rotated_key_cache": rotated_key_cache, "value_cache_store": value_cache_store, "cache_fill_length": cache_fill_length, "rotary_start_position": rotary_start_position, "rollout_live_steps": rollout_live_steps}


adapter_scale = 0.01
rate_numerator = 50.0
rope_theta = 1000000.0
masked_score = -1e+30

def reduce_over_rows(left, right):
    return lax.dot_general(left, right, (((0,), (0,)), ((), ())), preferred_element_type=jnp.float32)

def rotate(vectors, positions):
    half = vectors.shape[-1] // 2
    freqs = jnp.exp(-math.log(rope_theta) * jnp.arange(half, dtype=jnp.float32) * (2.0 / vectors.shape[-1]))
    angles = positions.astype(jnp.float32)[..., None] * freqs
    cosine = jnp.concatenate([jnp.cos(angles)] * 2, axis=-1)[..., None, :]
    sine = jnp.concatenate([jnp.sin(angles)] * 2, axis=-1)[..., None, :]
    turned = jnp.concatenate([-vectors[..., half:], vectors[..., :half]], axis=-1)
    return vectors * cosine + turned * sine

def reference(learner_hidden_state, learner_cotangent, adapter_down_factor, adapter_up_factor, output_projection, query_projection, key_projection, value_projection, decoder_layer_input, rotated_key_cache, value_cache_store, cache_fill_length, rotary_start_position, rollout_live_steps):
    step_rate = rate_numerator / math.sqrt(TOKENS_L)
    down_factor_slice = adapter_down_factor.astype(jnp.bfloat16)
    up_factor_slice = adapter_up_factor.astype(jnp.bfloat16)
    reduced_partial = jnp.dot(learner_hidden_state, down_factor_slice, preferred_element_type=jnp.float32).astype(jnp.bfloat16)
    up_gradient = adapter_scale * reduce_over_rows(reduced_partial, learner_cotangent)
    backward_result = lax.dot_general(learner_cotangent, up_factor_slice, (((1,), (1,)), ((), ())), preferred_element_type=jnp.float32).astype(jnp.bfloat16)
    down_gradient = adapter_scale * reduce_over_rows(learner_hidden_state, backward_result)
    fresh_down_factor = adapter_down_factor - step_rate * down_gradient
    fresh_up_factor = adapter_up_factor - step_rate * up_gradient
    merged_weight = (output_projection.astype(jnp.float32) + adapter_scale * jnp.dot(fresh_down_factor.astype(jnp.bfloat16), fresh_up_factor.astype(jnp.bfloat16), preferred_element_type=jnp.float32)).astype(jnp.bfloat16)
    steps, rollouts, width = decoder_layer_input.shape
    flat = decoder_layer_input.reshape(steps * rollouts, width)
    queries = jnp.dot(flat, query_projection, preferred_element_type=jnp.float32).astype(jnp.bfloat16)
    new_keys = jnp.dot(flat, key_projection, preferred_element_type=jnp.float32).astype(jnp.bfloat16)
    new_values = jnp.dot(flat, value_projection, preferred_element_type=jnp.float32).astype(jnp.bfloat16)
    order = jnp.arange(steps, dtype=jnp.int32)
    positions = rotary_start_position[None, :] + order[:, None]
    queries = rotate(queries.reshape(steps, rollouts, QH, HD).astype(jnp.float32), positions).astype(jnp.bfloat16)
    new_keys = rotate(new_keys.reshape(steps, rollouts, KVH, HD).astype(jnp.float32), positions).astype(jnp.bfloat16)
    new_values = new_values.reshape(steps, rollouts, KVH, HD)
    inv_root = 1.0 / math.sqrt(HD)

    def attend(item):
        query_row, keys_cached, values_cached, keys_fresh, values_fresh, length = item
        keys = jnp.concatenate([keys_cached.reshape(CTX, KVH, HD), keys_fresh], axis=0).astype(jnp.float32)
        values = jnp.concatenate([values_cached.reshape(CTX, KVH, HD), values_fresh], axis=0).astype(jnp.float32)
        grouped = query_row.reshape(steps, KVH, QH // KVH, HD).astype(jnp.float32)
        scores = jnp.einsum('skgd,ckd->skgc', grouped, keys) * inv_root
        spot = jnp.arange(CTX + steps, dtype=jnp.int32)
        valid = jnp.where(spot[None, :] < CTX, spot[None, :] < length, spot[None, :] - CTX <= order[:, None])
        valid = valid[:, None, None, :]
        scores = jnp.where(valid, scores, masked_score)
        top = lax.optimization_barrier(jnp.max(scores, axis=-1, keepdims=True))
        weights = jnp.where(valid, jnp.exp(scores - top), 0.0)
        total = lax.optimization_barrier(jnp.sum(weights, axis=-1))
        result = jnp.einsum('skgc,ckd->skgd', weights, values) / total[..., None]
        return result.astype(jnp.bfloat16).reshape(steps, QH * HD)
    attended = lax.map(attend, (jnp.transpose(queries, (1, 0, 2, 3)), rotated_key_cache, value_cache_store, jnp.transpose(new_keys, (1, 0, 2, 3)), jnp.transpose(new_values, (1, 0, 2, 3)), cache_fill_length))
    flat_out = jnp.transpose(attended, (1, 0, 2)).reshape(steps * rollouts, QH * HD)
    projected = jnp.dot(flat_out, merged_weight, preferred_element_type=jnp.float32)
    live = (order[:, None] < rollout_live_steps[None, :]).reshape(steps * rollouts, 1)
    decoded = jnp.where(live, projected, 0.0).astype(jnp.bfloat16).reshape(steps, rollouts, MODEL_WIDTH)
    return (decoded, fresh_down_factor, fresh_up_factor)
```

```python
import math

import jax
import jax.numpy as jnp
from jax import lax
from jax.experimental import pallas as pl
from jax.experimental.pallas import tpu as pltpu
from jax.sharding import PartitionSpec as P

MESH = pl.DeviceIdType.MESH
F32 = jnp.float32
BF16 = jnp.bfloat16

adapter_scale = 0.01
rate_numerator = 50.0
rope_theta = 1000000.0
masked_score = -1e30

HD = 128
TOKENS = 32768
STEP_SCALE = adapter_scale * rate_numerator / math.sqrt(TOKENS)
INV_ROOT = 1.0 / math.sqrt(HD)

NN = (((1,), (0,)), ((), ()))
NT = (((1,), (1,)), ((), ()))


def dot(a, b, dims=NN):
    return lax.dot_general(a, b, dims, preferred_element_type=F32)


def rcopy(src, dst, ss, rs, dev):
    return pltpu.make_async_remote_copy(
        src_ref=src, dst_ref=dst, send_sem=ss, recv_sem=rs, device_id=dev, device_id_type=MESH
    )


def loop(n, fn, start=0):
    def step(k, carry):
        fn(k)
        return carry

    lax.fori_loop(start, n, step, 0)


SCRATCH = dict(
    v_down=((64, 256), F32),
    v_x=((4, 4, 5120), BF16),
    x_rows=((16, 5120), F32),
    v_wq=((5120, 256), BF16),
    v_wkv=((64, 5120), BF16),
    v_up=((64, 5120), F32),
    v_cot=((128, 5120), BF16),
    v_hid=((128, 8192), BF16),
    v_wo=((256, 5120), BF16),
    kbuf=((2, 4, 128, 512), BF16),
    vbuf=((2, 4, 128, 512), BF16),
    down_all=((32, 64, 256), BF16),
    q_rot0=((16, 128), F32),
    q_rot1=((16, 128), F32),
    q_rows=((32, 128), F32),
    q_send=((32, 128), BF16),
    q_buf=((16, 32, 128), BF16),
    n_buf=((4, 16, 128), BF16),
    n_send=((16, 128), BF16),
    a_send=((16, 32, 128), BF16),
    a_recv=((16, 32, 128), BF16),
    l_send=((16, 8, 128), F32),
    l_recv=((16, 8, 128), F32),
    g_send1=((2, 16, 64, 256), BF16),
    g_keep=((2, 16, 64, 256), F32),
    g_recv1=((2, 16, 64, 256), BF16),
    g_send2=((2, 8, 128, 256), BF16),
    g_recv2=((2, 8, 128, 256), BF16),
    g_send3=((2, 16, 16, 128), BF16),
    g_recv3=((2, 16, 16, 128), BF16),
    g_send4=((2, 16, 128), F32),
    g_recv4=((2, 8, 16, 128), F32),
    u_tmp=((64, 1280), F32),
    p_rows=((16, 5120), F32),
    fd_pad=((128, 256), BF16),
    fu_pad=((128, 256), BF16),
    fu_rows=((256, 128), F32),
    o_send1=((16, 16, 256), BF16),
    o_keep=((16, 16, 256), F32),
    o_recv1=((16, 16, 256), BF16),
    o_send2=((16, 16, 256), BF16),
    o_recv2=((16, 16, 256), BF16),
    d_rows=((16, 256), F32),
    f_send=((8, 24, 128), F32),
    f_recv=((24, 128), F32),
)
SEMS = dict(
    load=(12,),
    dn_sz=(8,),
    dn_sy=(8,),
    dn_sc=(16,),
    dn_r=(32,),
    kv_s=(2,),
    kv_r=(2,),
    q_s=(16,),
    q_r=(16,),
    n_s=(4,),
    n_r=(4,),
    a_s=(16,),
    a_r=(16,),
    l_s=(16,),
    l_r=(16,),
    g1_s=(2, 4),
    g1_r=(2, 4),
    g2_s=(2, 8),
    g2_r=(2, 8),
    g3_s=(2, 16),
    g3_r=(2, 16),
    g4_s=(2, 8),
    g4_r=(2, 8),
    o1_s=(1,),
    o1_r=(1,),
    o2_s=(16,),
    o2_r=(16,),
    f_s=(8,),
    f_r=(1,),
)


class Names:
    pass


def lanes(shape):
    return lax.broadcasted_iota(jnp.int32, shape, len(shape) - 1)


def sublanes(shape):
    return lax.broadcasted_iota(jnp.int32, shape, len(shape) - 2)


def by_rollout(rollout, ref):
    picked = jnp.where(rollout == 0, ref[0], ref[1])
    picked = jnp.where(rollout == 2, ref[2], picked)
    return jnp.where(rollout == 3, ref[3], picked)


def kernel(
    hid, cot, down, up, wo, wq, wk, wv, x, kc, vc, fill, start, live, dec_out, fd_out, fu_out, *refs
):
    n = Names()
    for name, ref in zip(list(SCRATCH) + ["s_" + key for key in SEMS], refs):
        setattr(n, name, ref)
    t = lax.axis_index("tensor")
    g = lax.axis_index("group")
    c = lax.rem(t, 2)
    i0 = lax.div(t, 2)
    y = lax.div(t, 16)
    z = lax.rem(i0, 8)
    t16 = lax.rem(t, 16)
    sib = {"tensor": t + 1 - 2 * c}
    ypart = {"tensor": lax.rem(t + 16, 32)}

    def tdev(index):
        return {"tensor": index}

    def gdev(index):
        return {"group": index}

    barrier = pltpu.get_barrier_semaphore()
    loop(
        32,
        lambda k: pl.semaphore_signal(
            barrier, inc=1, device_id=tdev(lax.rem(t + k, 32)), device_id_type=MESH
        ),
        1,
    )
    loop(
        8,
        lambda k: pl.semaphore_signal(
            barrier, inc=1, device_id=gdev(lax.rem(g + k, 8)), device_id_type=MESH
        ),
        1,
    )

    own_half = pl.ds(pl.multiple_of(512 * c, 512), 512)
    sib_half = pl.ds(pl.multiple_of(512 * (1 - c), 512), 512)
    loads = dict(
        down=(down, n.v_down),
        x=(x, n.v_x),
        wq=(wq, n.v_wq),
        wk=(wk, n.v_wkv.at[pl.ds(0, 32)]),
        wv=(wv, n.v_wkv.at[pl.ds(32, 32)]),
        up=(up, n.v_up),
        cot=(cot, n.v_cot),
        hid=(hid, n.v_hid),
        k=(kc.at[:, :, own_half], n.kbuf.at[0]),
        v=(vc.at[:, :, own_half], n.vbuf.at[0]),
        wo=(wo, n.v_wo),
    )
    loads = {
        key: pltpu.make_async_copy(src, dst, n.s_load.at[at])
        for at, (key, (src, dst)) in enumerate(loads.items())
    }
    for copy in loads.values():
        copy.start()

    loads["down"].wait()
    n.down_all[t] = n.v_down[...].astype(BF16)

    pl.semaphore_wait(barrier, 38)

    def dn(slot, ss, dev):
        return rcopy(n.down_all.at[slot], n.down_all.at[slot], ss, n.s_dn_r.at[slot], dev)

    def dn_z(k):
        to = y * 16 + lax.rem(z + k, 8) * 2 + c
        return dn(t, n.s_dn_sz.at[k], tdev(to))

    def dn_y(k):
        slot = y * 16 + lax.rem(z + k, 8) * 2 + c
        return dn(slot, n.s_dn_sy.at[k], ypart)

    def dn_c(k):
        slot = lax.rem(y + lax.div(k, 8), 2) * 16 + lax.rem(z + k, 8) * 2 + c
        return dn(slot, n.s_dn_sc.at[k], sib)

    loop(8, lambda k: dn_z(k).start(), 1)
    dn_y(0).start()
    dn_c(0).start()

    kv = [
        rcopy(src.at[:, :, sib_half], dst.at[1], n.s_kv_s.at[at], n.s_kv_r.at[at], sib)
        for at, (src, dst) in enumerate(((kc, n.kbuf), (vc, n.vbuf)))
    ]
    for copy in kv:
        copy.start()

    loads["x"].wait()
    for s in range(4):
        n.x_rows[s * 4 : s * 4 + 4, :] = n.v_x[s].astype(F32)
    xb = n.x_rows[...].astype(BF16)
    row = sublanes((16, HD))
    lane = lanes((16, HD))
    position = (by_rollout(row & 3, start) + (row >> 2)).astype(F32)
    freq = jnp.exp((lane & 63).astype(F32) * (-math.log(rope_theta) * 2.0 / HD))
    angle = position * freq
    cosine = jnp.cos(angle)
    sine = jnp.where(lane < 64, -jnp.sin(angle), jnp.sin(angle))

    def rotate(v):
        v = v.astype(BF16).astype(F32)
        return v * cosine + pltpu.roll(v, 64, 1) * sine

    loads["wq"].wait()
    q = dot(xb, n.v_wq[...])
    for h, rows in enumerate((n.q_rot0, n.q_rot1)):
        rows[...] = rotate(q[:, h * HD : (h + 1) * HD])
        for r in range(4):
            n.q_rows[r * 8 + h * 4 : r * 8 + h * 4 + 4, :] = rows[pl.ds(r, 4, stride=4), :]
    n.q_send[...] = n.q_rows[...].astype(BF16)

    def q_copy(k):
        i = lax.rem(i0 + k, 16)
        return rcopy(n.q_send, n.q_buf.at[t16], n.s_q_s.at[k], n.s_q_r.at[t16], tdev(2 * i + y))

    @pl.when(c != y)
    def _():
        q_copy(0).start()

    loop(16, lambda k: q_copy(k).start(), 1)

    @pl.when(c == y)
    def _():
        n.q_buf[t16] = n.q_send[...]

    loads["wk"].wait()
    loads["wv"].wait()
    nkv = dot(xb, n.v_wkv[...], NT)
    n.n_send[...] = jnp.concatenate([nkv, nkv], axis=1).astype(BF16)
    b4 = lax.rem(t, 4)

    def n_copy(k):
        to = t - b4 + lax.rem(b4 + k, 4)
        return rcopy(n.n_send, n.n_buf.at[b4], n.s_n_s.at[k], n.s_n_r.at[b4], tdev(to))

    loop(4, lambda k: n_copy(k).start(), 1)
    n.n_buf[b4] = n.n_send[...]

    def g1(u, part):
        at = pl.ds(part * 4, 4)
        return rcopy(
            n.g_send1.at[u, at], n.g_recv1.at[u, at], n.s_g1_s.at[u, part], n.s_g1_r.at[u, part], sib
        )

    def g2(u, k):
        j = lax.rem(g + k, 8)
        return rcopy(
            n.g_send2.at[u, j], n.g_recv2.at[u, g], n.s_g2_s.at[u, k], n.s_g2_r.at[u, g], gdev(j)
        )

    def g2_in(u, k):
        j = lax.rem(g + k, 8)
        return rcopy(
            n.g_send2.at[u, j], n.g_recv2.at[u, j], n.s_g2_s.at[u, k], n.s_g2_r.at[u, j], gdev(j)
        )

    def g3(u, k):
        i = lax.rem(i0 + k, 16)
        return rcopy(
            n.g_send3.at[u, i], n.g_recv3.at[u, i0], n.s_g3_s.at[u, k], n.s_g3_r.at[u, i0],
            tdev(2 * i + c),
        )

    def g3_in(u, k):
        i = lax.rem(i0 + k, 16)
        return rcopy(
            n.g_send3.at[u, i], n.g_recv3.at[u, i], n.s_g3_s.at[u, k], n.s_g3_r.at[u, i],
            tdev(2 * i + c),
        )

    def g4(u, k):
        j = lax.rem(g + k, 8)
        return rcopy(
            n.g_send4.at[u], n.g_recv4.at[u, g], n.s_g4_s.at[u, k], n.s_g4_r.at[u, g], gdev(j)
        )

    def g4_in(u, k):
        j = lax.rem(g + k, 8)
        return rcopy(
            n.g_send4.at[u], n.g_recv4.at[u, j], n.s_g4_s.at[u, k], n.s_g4_r.at[u, j], gdev(j)
        )

    def stage2_out(u):
        def part_sum(part):
            g1(u, part).wait_recv()
            for pair in range(2):
                at = part * 4 + pair * 2
                first = n.g_keep[u, at] + n.g_recv1[u, at].astype(F32)
                second = n.g_keep[u, at + 1] + n.g_recv1[u, at + 1].astype(F32)
                rows = pl.ds(pl.multiple_of(at * 8, 16), 16)
                for j in range(8):
                    both = jnp.concatenate(
                        [first[j * 8 : j * 8 + 8], second[j * 8 : j * 8 + 8]], axis=0
                    )
                    n.g_send2[u, j, rows, :] = both.astype(BF16)

        loop(4, part_sum)
        loop(8, lambda k: g2(u, k).start(), 1)

    def stage3_out(u):
        loop(8, lambda k: g2_in(u, k).wait_recv(), 1)
        n.g_recv2[u, g] = n.g_send2[u, g]

        def pair_sum(pair):
            rows = pl.ds(pl.multiple_of(pair * 16, 16), 16)
            total = n.g_recv2[u, 0, rows, :].astype(F32)
            for j in range(1, 8):
                total = total + n.g_recv2[u, j, rows, :].astype(F32)
            for e in range(2):
                piece = total[e * 8 : e * 8 + 8]
                n.g_send3[u, pair * 2 + e] = jnp.concatenate(
                    [piece[:, :128], piece[:, 128:]], axis=0
                ).astype(BF16)

        loop(8, pair_sum)
        loop(16, lambda k: g3(u, k).start(), 1)

    def stage4_out(u):
        loop(16, lambda k: g3_in(u, k).wait_recv(), 1)
        n.g_recv3[u, i0] = n.g_send3[u, i0]
        total = n.g_recv3[u, 0].astype(F32)
        for i in range(1, 16):
            total = total + n.g_recv3[u, i].astype(F32)
        n.g_send4[u] = total
        n.g_recv4[u, g] = total
        loop(8, lambda k: g4(u, k).start(), 1)

    def summed(u):
        loop(8, lambda k: g4_in(u, k).wait_recv(), 1)
        pieces = [n.g_recv4[u, j] for j in range(8)]
        return jnp.concatenate(
            [jnp.concatenate([p[:8], p[8:]], axis=1) for p in pieces], axis=0
        )

    loads["up"].wait()
    loads["cot"].wait()
    back = dot(n.v_up[...].astype(BF16), n.v_cot[...], NT).astype(BF16)
    loads["hid"].wait()

    def down_part(part):
        for e in range(4):
            i = part * 4 + e
            at = pl.multiple_of((2 * i + 1 - c) * 256, 256)
            n.g_send1[0, i] = dot(back, n.v_hid[:, pl.ds(at, 256)]).astype(BF16)
        g1(0, part).start()
        for e in range(4):
            i = part * 4 + e
            at = pl.multiple_of((2 * i + c) * 256, 256)
            n.g_keep[0, i] = dot(back, n.v_hid[:, pl.ds(at, 256)])

    loop(4, down_part)

    def pass_z(k):
        slot = y * 16 + lax.rem(z + k, 8) * 2 + c
        dn(slot, n.s_dn_sz.at[k], sib).wait_recv()
        dn_y(k).start()
        dn_c(k).start()

    loop(8, pass_z, 1)

    stage2_out(0)

    def pass_y(k):
        dn_c(k).wait_recv()
        dn_c(k).start()

    loop(16, pass_y, 8)

    def q_in(k):
        i = lax.rem(t16 + k, 16)
        return rcopy(n.q_send, n.q_buf.at[i], n.s_q_s.at[k], n.s_q_r.at[i], sib)

    @pl.when(c != y)
    def _():
        q_in(0).wait_recv()

    loop(16, lambda k: q_in(k).wait_recv(), 1)
    loads["k"].wait()
    loads["v"].wait()
    for copy in kv:
        copy.wait_recv()

    spot = lanes((32, 256))
    spot = jnp.where(spot < 128, t * 128 + spot, (t + 1 - 2 * c) * 128 + spot - 128)
    tile_lane = lanes((8, 128))

    def attend(kk):
        cols = pl.ds(pl.multiple_of(kk * HD, HD), HD)
        qs = [n.q_buf[kk * 4 + j].astype(F32) for j in range(4)]
        outs, tops, sums = [], [], []
        for r in range(4):
            qr = jnp.concatenate([a[r * 8 : r * 8 + 8] for a in qs], axis=0).astype(BF16)
            keys = jnp.concatenate([n.kbuf[0, r, :, cols], n.kbuf[1, r, :, cols]], axis=0)
            values = jnp.concatenate([n.vbuf[0, r, :, cols], n.vbuf[1, r, :, cols]], axis=0)
            valid = spot < fill[r]
            scores = jnp.where(valid, dot(qr, keys, NT) * INV_ROOT, masked_score)
            top = jnp.max(scores, axis=1, keepdims=True)
            weights = jnp.where(valid, jnp.exp(scores - top), 0.0)
            tops.append(top)
            sums.append(jnp.sum(weights, axis=1, keepdims=True))
            outs.append(dot(weights.astype(BF16), values))
        for j in range(4):
            rows = slice(j * 8, j * 8 + 8)
            n.a_send[kk * 4 + j] = jnp.concatenate([o[rows] for o in outs], axis=0).astype(BF16)
            tile = jnp.zeros((8, 128), F32)
            for r in range(4):
                tile = jnp.where(tile_lane == r, tops[r][rows], tile)
                tile = jnp.where(tile_lane == 64 + r, sums[r][rows], tile)
            n.l_send[kk * 4 + j] = tile

    loop(4, attend)

    def a_copy(k):
        i = lax.rem(t16 + k, 16)
        to = tdev(16 * c + i)
        return (
            rcopy(n.a_send.at[i], n.a_recv.at[i0], n.s_a_s.at[k], n.s_a_r.at[i0], to),
            rcopy(n.l_send.at[i], n.l_recv.at[i0], n.s_l_s.at[k], n.s_l_r.at[i0], to),
        )

    def a_start(k):
        for copy in a_copy(k):
            copy.start()

    @pl.when(c != y)
    def _():
        a_start(0)

    loop(16, a_start, 1)

    @pl.when(c == y)
    def _():
        n.a_recv[i0] = n.a_send[t16]
        n.l_recv[i0] = n.l_send[t16]

    def dn_in(k):
        slot = lax.rem(y + lax.div(k, 8), 2) * 16 + lax.rem(z + k, 8) * 2 + 1 - c
        dn(slot, n.s_dn_sc.at[k], sib).wait_recv()

    loop(16, dn_in)

    def reduce_part(part, total):
        for e in range(4):
            at = part * 4 + e
            cols = pl.ds(pl.multiple_of(at * 256, 256), 256)
            total = total + dot(n.down_all[at], n.v_hid[:, cols], NT)
        return total

    reduced = lax.fori_loop(0, 8, reduce_part, jnp.zeros((64, 128), F32)).astype(BF16)

    def up_part(part):
        n.u_tmp[...] = dot(reduced, n.v_cot[:, pl.ds(pl.multiple_of(part * 1280, 1280), 1280)])
        for pair in range(4):
            both = []
            for e in (pair * 2, pair * 2 + 1):
                at = 160 * e // 128 * 128
                shift = 160 * e - at
                window = n.u_tmp[:, at : at + 256]
                both.append(pltpu.roll(window, 256 - shift, 1) if shift else window)
            n.g_send1[1, part * 4 + pair] = jnp.where(c == 0, both[1], both[0]).astype(BF16)
            n.g_keep[1, part * 4 + pair] = jnp.where(c == 0, both[0], both[1])
        g1(1, part).start()

    loop(4, up_part)

    stage3_out(0)
    stage2_out(1)

    loop(4, lambda k: rcopy(
        n.n_send, n.n_buf.at[lax.rem(b4 + k, 4)], n.s_n_s.at[k], n.s_n_r.at[lax.rem(b4 + k, 4)], sib
    ).wait_recv(), 1)
    fresh = [n.n_buf[j].astype(F32) for j in range(4)]
    quarter = lane >> 5
    new_k = fresh[0]
    new_v = pltpu.roll(fresh[0], 96, 1)
    for j in range(1, 4):
        new_k = jnp.where(quarter == j, pltpu.roll(fresh[j], 32 * j, 1), new_k)
        new_v = jnp.where(quarter == j, pltpu.roll(fresh[j], (32 * j + 96) % 128, 1), new_v)
    new_k = rotate(new_k).astype(BF16)
    new_v = new_v.astype(BF16)
    nrow = sublanes((32, 16))
    ncol = lanes((32, 16))
    new_valid = ((nrow >> 3) == (ncol & 3)) & ((ncol >> 2) <= (nrow & 3))
    new_scores = jnp.where(new_valid, dot(n.q_send[...], new_k, NT) * INV_ROOT, masked_score)
    new_top = jnp.max(new_scores, axis=1, keepdims=True)
    new_weights = jnp.where(new_valid, jnp.exp(new_scores - new_top), 0.0)
    new_sum = jnp.sum(new_weights, axis=1, keepdims=True)
    new_out = dot(new_weights.astype(BF16), new_v)
    new_tile = jnp.zeros((8, 128), F32)
    new_total = jnp.zeros((8, 128), F32)
    for r in range(4):
        rows = slice(r * 8, r * 8 + 8)
        new_tile = jnp.where(tile_lane == r, new_top[rows], new_tile)
        new_total = jnp.where(tile_lane == r, new_sum[rows], new_total)

    def a_in(k):
        i = lax.rem(i0 + k, 16)
        rcopy(n.a_send.at[0], n.a_recv.at[i], n.s_a_s.at[k], n.s_a_r.at[i], sib).wait_recv()
        rcopy(n.l_send.at[0], n.l_recv.at[i], n.s_l_s.at[k], n.s_l_r.at[i], sib).wait_recv()

    @pl.when(c != y)
    def _():
        a_in(0)

    loop(16, a_in, 1)

    peak = lax.fori_loop(0, 16, lambda i, m: jnp.maximum(m, n.l_recv[i]), new_tile)
    scale = jnp.exp(new_tile - peak)

    def join(i, state):
        total, parts = state
        tile = n.l_recv[i]
        scale = jnp.exp(tile - peak)
        part = n.a_recv[i].astype(F32)
        return (
            total + scale * pltpu.roll(tile, 64, 1),
            [acc + part[r * 8 : r * 8 + 8] * scale[:, r : r + 1] for r, acc in enumerate(parts)],
        )

    total, parts = lax.fori_loop(
        0,
        16,
        join,
        (
            scale * new_total,
            [new_out[r * 8 : r * 8 + 8] * scale[:, r : r + 1] for r in range(4)],
        ),
    )
    for r in range(4):
        n.q_rows[r * 8 : r * 8 + 8, :] = parts[r] / total[:, r : r + 1]
    for h, rows in enumerate((n.q_rot0, n.q_rot1)):
        for r in range(4):
            rows[pl.ds(r, 4, stride=4), :] = n.q_rows[r * 8 + h * 4 : r * 8 + h * 4 + 4, :]
    att = jnp.concatenate([n.q_rot0[...], n.q_rot1[...]], axis=1).astype(BF16)
    loads["wo"].wait()
    n.p_rows[...] = dot(att, n.v_wo[...])

    stage4_out(0)
    stage3_out(1)

    fd = n.v_down[...] - STEP_SCALE * summed(0)
    fd_out[...] = fd
    n.fd_pad[0:64, :] = jnp.zeros((64, 256), BF16)
    n.fd_pad[64:128, :] = fd.astype(BF16)
    low = dot(att, n.fd_pad[...], NT)

    o1 = rcopy(n.o_send1, n.o_recv1, n.s_o1_s.at[0], n.s_o1_r.at[0], sib)

    def out_part(part):
        for pair in range(4):
            both = []
            for e in (pair * 2, pair * 2 + 1):
                at = 160 * e // 128 * 128
                shift = 160 * e - at
                base = pl.multiple_of(part * 1280 + at, 128)
                window = n.p_rows[:, pl.ds(base, 256)]
                window = pltpu.roll(window, 256 - shift, 1) if shift else window
                both.append(
                    jnp.concatenate(
                        [window[:, :128], jnp.where(lane < 32, window[:, 128:], low)], axis=1
                    )
                )
            n.o_send1[part * 4 + pair] = jnp.where(c == 0, both[1], both[0]).astype(BF16)
            n.o_keep[part * 4 + pair] = jnp.where(c == 0, both[0], both[1])

    loop(4, out_part)
    o1.start()

    stage4_out(1)

    o1.wait_recv()

    def out_sum(i):
        n.o_send2[i] = (n.o_keep[i] + n.o_recv1[i].astype(F32)).astype(BF16)

    loop(16, out_sum)

    def o2(k):
        i = lax.rem(i0 + k, 16)
        return rcopy(
            n.o_send2.at[i], n.o_recv2.at[i0], n.s_o2_s.at[k], n.s_o2_r.at[i0], tdev(2 * i + c)
        )

    def o2_in(k):
        i = lax.rem(i0 + k, 16)
        return rcopy(
            n.o_send2.at[i], n.o_recv2.at[i], n.s_o2_s.at[k], n.s_o2_r.at[i], tdev(2 * i + c)
        )

    loop(16, lambda k: o2(k).start(), 1)

    first_col = 160 * t
    base = lax.div(first_col, 128) * 128
    up_cols = n.v_up[:, pl.ds(pl.multiple_of(base, 128), 256)]
    up_cols = pltpu.roll(up_cols, lax.rem(256 - (first_col - base), 256), 1)
    fu = up_cols - STEP_SCALE * summed(1)
    n.fu_pad[0:64, :] = jnp.zeros((64, 256), BF16)
    n.fu_pad[64:128, :] = fu.astype(BF16)

    owner = 4 * g + lax.div(t, 8)

    def f_copy(e):
        return rcopy(
            n.f_send.at[e], n.f_recv, n.s_f_s.at[e], n.s_f_r.at[0], tdev(8 * lax.rem(t, 4) + e)
        )

    @pl.when(lax.div(t, 4) == g)
    def _():
        n.fu_rows[...] = jnp.concatenate([fu, fu], axis=0).T
        for e in range(8):
            n.f_send[e] = n.fu_rows[20 * e : 20 * e + 24, :]
        for e in range(8):
            @pl.when(8 * lax.rem(t, 4) + e != t)
            def _():
                f_copy(e).start()

            @pl.when(8 * lax.rem(t, 4) + e == t)
            def _():
                n.f_recv[...] = n.f_send[e]

    loop(16, lambda k: o2_in(k).wait_recv(), 1)
    n.o_recv2[i0] = n.o_send2[i0]
    total = lax.fori_loop(
        1, 16, lambda i, a: a + n.o_recv2[i].astype(F32), n.o_recv2[0].astype(F32)
    )
    low = jnp.where(lane < 64, 0.0, total[:, 128:]).astype(BF16)
    decoded = total + adapter_scale * dot(low, n.fu_pad[...])
    wide_row = sublanes((16, 256))
    alive = (wide_row >> 2) < by_rollout(wide_row & 3, live)
    n.d_rows[...] = jnp.where(alive, decoded, 0.0)
    for s in range(4):
        dec_out[s] = n.d_rows[s * 4 : s * 4 + 4, 0:160].astype(BF16)

    @pl.when(owner != t)
    def _():
        f_copy(0).wait_recv()

    fu_out[...] = n.f_recv[0:20, 0:64]

    loop(8, lambda k: dn_z(k).wait_send(), 1)
    loop(8, lambda k: dn_y(k).wait_send())
    loop(16, lambda k: dn_c(k).wait_send())
    for copy in kv:
        copy.wait_send()
    loop(16, lambda k: q_copy(k).wait_send(), 1)
    loop(4, lambda k: n_copy(k).wait_send(), 1)

    def a_done(k):
        for copy in a_copy(k):
            copy.wait_send()

    loop(16, a_done, 1)

    @pl.when(c != y)
    def _():
        q_copy(0).wait_send()
        a_done(0)

    for u in range(2):
        loop(4, lambda k: g1(u, k).wait_send())
        loop(8, lambda k: g2(u, k).wait_send(), 1)
        loop(16, lambda k: g3(u, k).wait_send(), 1)
        loop(8, lambda k: g4(u, k).wait_send(), 1)
    o1.wait_send()
    loop(16, lambda k: o2(k).wait_send(), 1)

    @pl.when(lax.div(t, 4) == g)
    def _():
        for e in range(8):
            @pl.when(8 * lax.rem(t, 4) + e != t)
            def _():
                f_copy(e).wait_send()


def body(hid, cot, down, up, wo, wq, wk, wv, x, kc, vc, fill, start, live):
    hbm = pl.BlockSpec(memory_space=pl.ANY)
    smem = pl.BlockSpec(memory_space=pltpu.SMEM)
    vmem = pl.BlockSpec(memory_space=pltpu.VMEM)
    dec, fd, fu = pl.pallas_call(
        kernel,
        out_shape=(
            jax.ShapeDtypeStruct((4, 4, 160), BF16),
            jax.ShapeDtypeStruct((64, 256), F32),
            jax.ShapeDtypeStruct((20, 64), F32),
        ),
        in_specs=[hbm] * 11 + [smem] * 3,
        out_specs=(vmem,) * 3,
        scratch_shapes=[pltpu.VMEM(shape, kind) for shape, kind in SCRATCH.values()]
        + [pltpu.SemaphoreType.DMA(shape) for shape in SEMS.values()],
        compiler_params=pltpu.CompilerParams(
            collective_id=0, has_side_effects=True, vmem_limit_bytes=56 * 2**20
        ),
        name="update_and_decode",
    )(hid, cot, down.T, up, wo, wq, wk.T, wv.T, x, kc, vc, fill, start, live)
    return dec, fd.T, fu.T


def solution(mesh):
    return jax.shard_map(
        body,
        mesh=mesh,
        in_specs=(
            P(("group", "tensor"), None),
            P(("group", "tensor"), None),
            P("tensor", None),
            P(),
            P("tensor", None),
            P(None, "tensor"),
            P(None, "tensor"),
            P(None, "tensor"),
            P(None, "group", None),
            P("group", "tensor", None),
            P("group", "tensor", None),
            P("group"),
            P("group"),
            P("group"),
        ),
        out_specs=(P(None, "group", "tensor"), P("tensor", None), P(None, ("group", "tensor"))),
        check_vma=False,
    )
```

```python
import math

import jax
import jax.numpy as jnp
from jax import lax
from jax.experimental import pallas as pl
from jax.experimental.pallas import tpu as pltpu
from jax.sharding import PartitionSpec as P

MESH = pl.DeviceIdType.MESH
F32 = jnp.float32
BF16 = jnp.bfloat16

adapter_scale = 0.01
rate_numerator = 50.0
rope_theta = 1000000.0
masked_score = -1e30

HD = 128
TOKENS = 32768
STEP_SCALE = adapter_scale * rate_numerator / math.sqrt(TOKENS)
INV_ROOT = 1.0 / math.sqrt(HD)

NN = (((1,), (0,)), ((), ()))
NT = (((1,), (1,)), ((), ()))


def dot(a, b, dims=NN):
    return lax.dot_general(a, b, dims, preferred_element_type=F32)


def rcopy(src, dst, ss, rs, dev):
    return pltpu.make_async_remote_copy(
        src_ref=src, dst_ref=dst, send_sem=ss, recv_sem=rs, device_id=dev, device_id_type=MESH
    )


def loop(n, fn, start=0):
    def step(k, carry):
        fn(k)
        return carry

    lax.fori_loop(start, n, step, 0)


SCRATCH = dict(
    v_down=((64, 256), F32),
    v_x=((4, 4, 5120), BF16),
    x_rows=((16, 5120), F32),
    v_wq=((5120, 256), BF16),
    v_wkv=((64, 5120), BF16),
    v_up=((64, 5120), F32),
    v_cot=((128, 5120), BF16),
    cot2=((128, 2560), BF16),
    hid2=((2, 128, 4096), BF16),
    v_wo=((256, 5120), BF16),
    kbuf=((2, 4, 128, 512), BF16),
    vbuf=((2, 4, 128, 512), BF16),
    down_own=((64, 256), BF16),
    down_half=((16, 64, 256), BF16),
    back2=((2, 64, 128), BF16),
    part_send=((64, 256), F32),
    part_recv=((64, 256), F32),
    q_rot0=((16, 128), F32),
    q_rot1=((16, 128), F32),
    q_rows=((32, 128), F32),
    q_send=((32, 128), BF16),
    q_buf=((16, 32, 128), BF16),
    n_buf=((4, 16, 128), BF16),
    n_send=((16, 128), BF16),
    a_send=((16, 32, 128), BF16),
    a_recv=((16, 32, 128), BF16),
    l_send=((16, 8, 128), F32),
    l_recv=((16, 8, 128), F32),
    d_send2=((8, 128, 256), BF16),
    d_recv2=((8, 128, 256), BF16),
    u_send2=((8, 160, 128), BF16),
    u_recv2=((8, 160, 128), BF16),
    g_send3=((2, 16, 16, 128), BF16),
    g_recv3=((2, 16, 16, 128), BF16),
    g_send4=((2, 16, 128), F32),
    g_recv4=((2, 8, 16, 128), F32),
    u_tmp=((64, 1280), F32),
    p_rows=((16, 5120), F32),
    fd_pad=((128, 256), BF16),
    fu_pad=((128, 256), BF16),
    o_send1=((16, 16, 256), BF16),
    o_keep=((16, 16, 256), F32),
    o_recv1=((16, 16, 256), BF16),
    o_send2=((16, 16, 256), BF16),
    o_recv2=((16, 16, 256), BF16),
    d_rows=((16, 256), F32),
    f_send=((8, 8, 128), F32),
    f_recv=((8, 8, 128), F32),
    w_dec=((4, 4, 160), BF16),
    w_fd=((64, 256), F32),
    w_fu=((20, 64), F32),
)
SEMS = dict(
    load=(11,),
    dn_sz=(1,),
    dn_sy=(1,),
    dn_r=(16,),
    sib_s=(4,),
    sib_r=(4,),
    bk=(2,),
    pt=(2,),
    q=(2,),
    n=(2,),
    a=(2,),
    l=(2,),
    g2=(2, 2),
    g3=(2, 2),
    g4=(2, 2),
    o1=(2,),
    o2=(2,),
    f=(2,),
    out=(3,),
)


class Names:
    pass


def lanes(shape):
    return lax.broadcasted_iota(jnp.int32, shape, len(shape) - 1)


def sublanes(shape):
    return lax.broadcasted_iota(jnp.int32, shape, len(shape) - 2)


def by_rollout(rollout, ref):
    picked = jnp.where(rollout == 0, ref[0], ref[1])
    picked = jnp.where(rollout == 2, ref[2], picked)
    return jnp.where(rollout == 3, ref[3], picked)


def kernel(
    hid, cot, down, up, wo, wq, wk, wv, x, kc, vc, fill, start, live, dec_out, fd_out, fu_out, *refs
):
    n = Names()
    for name, ref in zip(list(SCRATCH) + ["s_" + key for key in SEMS], refs):
        setattr(n, name, ref)
    t = lax.axis_index("tensor")
    g = lax.axis_index("group")
    c = lax.rem(t, 2)
    i0 = lax.div(t, 2)
    y = lax.div(t, 16)
    z = lax.rem(i0, 8)
    t16 = lax.rem(t, 16)
    sib = {"tensor": t + 1 - 2 * c}
    other_y = lax.rem(t + 16, 32)
    g_other = g + 1 - 2 * lax.rem(g, 2)
    relays = c == y

    def tdev(index):
        return {"tensor": index}

    def gdev(index):
        return {"group": index}

    def near(k):
        return lax.rem(lax.div(k + 1, 2) * (7 - 6 * lax.rem(k, 2)), 8)

    f_from = 4 * g + lax.div(t, 8)
    f_self = f_from == t

    def f_to(e):
        return {"group": lax.div(t, 4), "tensor": 8 * lax.rem(t, 4) + e}

    def arrived(buf, count, sem):
        part = buf.at[pl.ds(0, count)]
        rcopy(part, part, sem, sem, sib).wait_recv()

    def left(buf, count, sem):
        part = buf.at[pl.ds(0, count)]
        rcopy(part, part, sem, sem, sib).wait_send()

    def arrived_heads(buf, sem):
        @pl.when(relays)
        def _():
            arrived(buf, 15, sem)

        @pl.when(jnp.logical_not(relays))
        def _():
            arrived(buf, 16, sem)

    barrier = pltpu.get_barrier_semaphore()
    loop(
        32,
        lambda k: pl.semaphore_signal(
            barrier, inc=1, device_id=tdev(lax.rem(t + k, 32)), device_id_type=MESH
        ),
        1,
    )
    loop(
        8,
        lambda k: pl.semaphore_signal(
            barrier, inc=1, device_id=gdev(lax.rem(g + k, 8)), device_id_type=MESH
        ),
        1,
    )

    pl.semaphore_signal(
        barrier,
        inc=1,
        device_id={"group": g_other, "tensor": other_y},
        device_id_type=MESH,
    )

    def f_greet(j):
        pl.semaphore_signal(
            barrier, inc=1, device_id={"group": j, "tensor": f_from}, device_id_type=MESH
        )

    loop(8, lambda k: f_greet(lax.rem(g + k, 8)), 1)

    @pl.when(jnp.logical_not(f_self))
    def _():
        f_greet(g)

    def half(size, which):
        return pl.ds(pl.multiple_of(size * which, size), size)

    loads = dict(
        down=(down, n.v_down),
        x=(x, n.v_x),
        wq=(wq, n.v_wq),
        wk=(wk, n.v_wkv.at[pl.ds(0, 32)]),
        wv=(wv, n.v_wkv.at[pl.ds(32, 32)]),
        up=(up, n.v_up),
        cot=(cot, n.v_cot),
        hid=(hid.at[:, half(4096, c)], n.hid2.at[0]),
        k=(kc.at[:, :, half(512, c)], n.kbuf.at[0]),
        v=(vc.at[:, :, half(512, c)], n.vbuf.at[0]),
        wo=(wo, n.v_wo),
    )
    loads = {
        key: pltpu.make_async_copy(src, dst, n.s_load.at[at])
        for at, (key, (src, dst)) in enumerate(loads.items())
    }
    for copy in loads.values():
        copy.start()

    loads["down"].wait()
    n.down_own[...] = n.v_down[...].astype(BF16)

    pl.semaphore_wait(barrier, 47 - f_self.astype(jnp.int32))

    def dn_z(k):
        to = y * 16 + lax.rem(z + near(k), 8) * 2 + y
        return rcopy(
            n.down_own, n.down_half.at[t16], n.s_dn_sz.at[0], n.s_dn_r.at[t16], tdev(to)
        )

    def dn_y(slot, group):
        return rcopy(
            n.down_half.at[slot],
            n.down_half.at[slot],
            n.s_dn_sy.at[0],
            n.s_dn_r.at[slot],
            {"group": group, "tensor": other_y},
        )

    def dn_pass(z_of, core):
        dn_y(z_of * 2 + core, g + core * (g_other - g)).start()

    loop(8, lambda k: dn_z(k).start(), 1)

    @pl.when(relays)
    def _():
        n.down_half[t16] = n.down_own[...]
        dn_pass(z, c)

    @pl.when(jnp.logical_not(relays))
    def _():
        dn_z(0).start()

    pairs = [
        rcopy(src, dst, n.s_sib_s.at[at], n.s_sib_r.at[at], sib)
        for at, (src, dst) in enumerate(
            (
                (hid.at[:, half(4096, 1 - c)], n.hid2.at[1]),
                (kc.at[:, :, half(512, 1 - c)], n.kbuf.at[1]),
                (vc.at[:, :, half(512, 1 - c)], n.vbuf.at[1]),
                (cot.at[:, half(2560, 1 - c)], n.cot2),
            )
        )
    ]
    for copy in pairs:
        copy.start()

    loads["x"].wait()
    for s in range(4):
        n.x_rows[s * 4 : s * 4 + 4, :] = n.v_x[s].astype(F32)
    xb = n.x_rows[...].astype(BF16)
    row = sublanes((16, HD))
    lane = lanes((16, HD))
    position = (by_rollout(row & 3, start) + (row >> 2)).astype(F32)
    freq = jnp.exp((lane & 63).astype(F32) * (-math.log(rope_theta) * 2.0 / HD))
    angle = position * freq
    cosine = jnp.cos(angle)
    sine = jnp.where(lane < 64, -jnp.sin(angle), jnp.sin(angle))

    def rotate(v):
        v = v.astype(BF16).astype(F32)
        return v * cosine + pltpu.roll(v, 64, 1) * sine

    loads["wq"].wait()
    q = dot(xb, n.v_wq[...])
    for h, rows in enumerate((n.q_rot0, n.q_rot1)):
        rows[...] = rotate(q[:, h * HD : (h + 1) * HD])
        for r in range(4):
            n.q_rows[r * 8 + h * 4 : r * 8 + h * 4 + 4, :] = rows[pl.ds(r, 4, stride=4), :]
    n.q_send[...] = n.q_rows[...].astype(BF16)

    def q_copy(k):
        i = lax.rem(i0 + k, 16)
        return rcopy(n.q_send, n.q_buf.at[t16], n.s_q.at[0], n.s_q.at[1], tdev(2 * i + y))

    @pl.when(jnp.logical_not(relays))
    def _():
        q_copy(0).start()

    loop(16, lambda k: q_copy(k).start(), 1)

    @pl.when(relays)
    def _():
        n.q_buf[t16] = n.q_send[...]

    send2 = (n.d_send2, n.u_send2)
    recv2 = (n.d_recv2, n.u_recv2)

    def g2(u, k):
        j = lax.rem(g + k, 8)
        return rcopy(
            send2[u].at[j], recv2[u].at[g], n.s_g2.at[u, 0], n.s_g2.at[u, 1], gdev(j)
        )

    def g3(u, k):
        i = lax.rem(t16 + k, 16)
        return rcopy(
            n.g_send3.at[u, i], n.g_recv3.at[u, i0], n.s_g3.at[u, 0], n.s_g3.at[u, 1],
            tdev(16 * c + i),
        )

    def g4(u, k):
        j = lax.rem(g + k, 8)
        return rcopy(
            n.g_send4.at[u], n.g_recv4.at[u, g], n.s_g4.at[u, 0], n.s_g4.at[u, 1], gdev(j)
        )

    def stack8(first, second, j):
        rows = slice(j * 8, j * 8 + 8)
        return jnp.concatenate([first[rows], second[rows]], axis=0).astype(BF16)

    def stage3_out(u):
        arrived(recv2[u], 7, n.s_g2.at[u, 1])
        recv2[u][g] = send2[u][g]

        def total(row):
            rows = pl.ds(pl.multiple_of(row, 16), 16)
            sums = recv2[u][0, rows, :].astype(F32)
            for j in range(1, 8):
                sums = sums + recv2[u][j, rows, :].astype(F32)
            return sums

        def send(i, low, high):
            n.g_send3[u, i] = jnp.concatenate([low, high], axis=0).astype(BF16)

        def down_sum(pair):
            sums = total(pair * 16)
            for e in range(2):
                piece = sums[e * 8 : e * 8 + 8]
                send(pair * 2 + e, piece[:, :128], piece[:, 128:])

        def up_sum(part):
            rest = total(128 + part * 16)
            for pair in range(4):
                sums = total(part * 64 + pair * 16)
                high = pltpu.roll(rest, 128 - 32 * pair, 1) if pair else rest
                for e in range(2):
                    rows = slice(e * 8, e * 8 + 8)
                    send(part * 8 + pair * 2 + e, sums[rows], high[rows])

        if u == 0:
            loop(8, down_sum)
        else:
            loop(2, up_sum)

        @pl.when(jnp.logical_not(relays))
        def _():
            g3(u, 0).start()

        loop(16, lambda k: g3(u, k).start(), 1)

    def stage4_out(u):
        arrived_heads(n.g_recv3.at[u], n.s_g3.at[u, 1])

        @pl.when(relays)
        def _():
            n.g_recv3[u, i0] = n.g_send3[u, t16]

        total = n.g_recv3[u, 0].astype(F32)
        for i in range(1, 16):
            total = total + n.g_recv3[u, i].astype(F32)
        n.g_send4[u] = total
        n.g_recv4[u, g] = total
        loop(8, lambda k: g4(u, k).start(), 1)
        return total

    def summed(u):
        arrived(n.g_recv4.at[u], 7, n.s_g4.at[u, 1])
        pieces = [n.g_recv4[u, j] for j in range(8)]
        return jnp.concatenate(
            [jnp.concatenate([p[:8], p[8:]], axis=1) for p in pieces], axis=0
        )

    loads["up"].wait()
    loads["cot"].wait()
    n.back2[0] = dot(n.v_up[...].astype(BF16), n.v_cot[...], NT).astype(BF16)
    bk = rcopy(n.back2.at[0], n.back2.at[1], n.s_bk.at[0], n.s_bk.at[1], sib)
    bk.start()

    loads["wk"].wait()
    loads["wv"].wait()
    nkv = dot(xb, n.v_wkv[...], NT)
    n.n_send[...] = jnp.concatenate([nkv, nkv], axis=1).astype(BF16)
    b4 = lax.rem(t, 4)

    def n_copy(k):
        to = t - b4 + lax.rem(b4 + k, 4)
        return rcopy(n.n_send, n.n_buf.at[b4], n.s_n.at[0], n.s_n.at[1], tdev(to))

    loop(4, lambda k: n_copy(k).start(), 1)
    n.n_buf[b4] = n.n_send[...]

    loads["hid"].wait()
    pairs[0].wait_recv()
    bk.wait_recv()

    back = jnp.concatenate([n.back2[0], n.back2[1]], axis=1)

    def down_pair(pair):
        blocks = []
        for e in range(2):
            cols = pl.ds(pl.multiple_of((pair * 2 + e) * 256, 256), 256)
            both = jnp.concatenate([n.hid2[0, :, cols], n.hid2[1, :, cols]], axis=0)
            blocks.append(dot(back, both))
        rows = pl.ds(pl.multiple_of(pair * 16, 16), 16)
        for j in range(8):
            n.d_send2[j, rows, :] = stack8(*blocks, j)

    loop(8, down_pair)
    loop(8, lambda k: g2(0, k).start(), 1)

    def dn_recv(slot):
        dn_y(slot, g).wait_recv()

    @pl.when(relays)
    def _():
        dn_recv(z * 2 + 1 - c)
        dn_pass(z, 1 - c)

        def pass_on(k):
            from_z = lax.rem(z + near(k), 8)
            for core in range(2):
                dn_recv(from_z * 2 + core)
                dn_pass(from_z, core)

        loop(8, pass_on, 1)

    arrived_heads(n.q_buf, n.s_q.at[1])
    loads["k"].wait()
    loads["v"].wait()
    pairs[1].wait_recv()
    pairs[2].wait_recv()

    spot = lanes((32, 256))
    spot = jnp.where(spot < 128, t * 128 + spot, (t + 1 - 2 * c) * 128 + spot - 128)
    tile_lane = lanes((8, 128))

    def attend(kk):
        cols = pl.ds(pl.multiple_of(kk * HD, HD), HD)
        qs = [n.q_buf[kk * 4 + j].astype(F32) for j in range(4)]
        outs, tops, sums = [], [], []
        for r in range(4):
            qr = jnp.concatenate([a[r * 8 : r * 8 + 8] for a in qs], axis=0).astype(BF16)
            keys = jnp.concatenate([n.kbuf[0, r, :, cols], n.kbuf[1, r, :, cols]], axis=0)
            values = jnp.concatenate([n.vbuf[0, r, :, cols], n.vbuf[1, r, :, cols]], axis=0)
            valid = spot < fill[r]
            scores = jnp.where(valid, dot(qr, keys, NT) * INV_ROOT, masked_score)
            top = jnp.max(scores, axis=1, keepdims=True)
            weights = jnp.where(valid, jnp.exp(scores - top), 0.0)
            tops.append(top)
            sums.append(jnp.sum(weights, axis=1, keepdims=True))
            outs.append(dot(weights.astype(BF16), values))
        for j in range(4):
            rows = slice(j * 8, j * 8 + 8)
            n.a_send[kk * 4 + j] = jnp.concatenate([o[rows] for o in outs], axis=0).astype(BF16)
            tile = jnp.zeros((8, 128), F32)
            for r in range(4):
                tile = jnp.where(tile_lane == r, tops[r][rows], tile)
                tile = jnp.where(tile_lane == 64 + r, sums[r][rows], tile)
            n.l_send[kk * 4 + j] = tile

    loop(2, attend)

    @pl.when(jnp.logical_not(relays))
    def _():
        loop(16, dn_recv)

    def reduce_part(part, total):
        for e in range(4):
            at = part * 4 + e
            cols = pl.ds(pl.multiple_of(at * 256, 256), 256)
            both = jnp.concatenate([n.hid2[0, :, cols], n.hid2[1, :, cols]], axis=0)
            total = total + dot(n.down_half[at], both, NT)
        return total

    n.part_send[...] = lax.fori_loop(0, 4, reduce_part, jnp.zeros((64, 256), F32))
    pt = rcopy(n.part_send, n.part_recv, n.s_pt.at[0], n.s_pt.at[1], sib)
    pt.start()

    stage3_out(0)
    loop(4, attend, 2)

    def a_copy(k):
        i = lax.rem(t16 + k, 16)
        to = tdev(16 * c + i)
        return (
            rcopy(n.a_send.at[i], n.a_recv.at[i0], n.s_a.at[0], n.s_a.at[1], to),
            rcopy(n.l_send.at[i], n.l_recv.at[i0], n.s_l.at[0], n.s_l.at[1], to),
        )

    def a_start(k):
        for copy in a_copy(k):
            copy.start()

    @pl.when(jnp.logical_not(relays))
    def _():
        a_start(0)

    loop(16, a_start, 1)

    @pl.when(relays)
    def _():
        n.a_recv[i0] = n.a_send[t16]
        n.l_recv[i0] = n.l_send[t16]

    pt.wait_recv()
    pairs[3].wait_recv()
    reduced = jnp.concatenate(
        [
            n.part_send[:, :128] + n.part_recv[:, 128:],
            n.part_send[:, 128:] + n.part_recv[:, :128],
        ],
        axis=1,
    ).astype(BF16)

    def up_part(part):
        both = jnp.concatenate(
            [
                n.v_cot[:, pl.ds(pl.multiple_of(2560 * c + 1280 * part, 1280), 1280)],
                n.cot2[:, pl.ds(pl.multiple_of(1280 * part, 1280), 1280)],
            ],
            axis=0,
        )
        n.u_tmp[...] = dot(reduced, both)
        rest = [jnp.zeros((64, 128), F32)] * 2
        quarter = lanes((64, 128)) >> 5
        for pair in range(4):
            low = []
            for e in range(2):
                first = 160 * (pair * 2 + e)
                at = first // 128 * 128
                window = n.u_tmp[:, at : at + 256]
                window = pltpu.roll(window, 256 - (first - at), 1) if first > at else window
                low.append(window[:, :128])
                high = pltpu.roll(window[:, 128:], 32 * pair, 1) if pair else window[:, 128:]
                rest[e] = jnp.where(quarter == pair, high, rest[e])
            rows = pl.ds(pl.multiple_of(part * 64 + pair * 16, 16), 16)
            for j in range(8):
                n.u_send2[j, rows, :] = stack8(*low, j)
        rows = pl.ds(pl.multiple_of(128 + part * 16, 16), 16)
        for j in range(8):
            n.u_send2[j, rows, :] = stack8(*rest, j)

    loop(2, up_part)
    loop(8, lambda k: g2(1, k).start(), 1)

    arrived(n.n_buf, 3, n.s_n.at[1])
    fresh = [n.n_buf[j].astype(F32) for j in range(4)]
    quarter = lane >> 5
    new_k = fresh[0]
    new_v = pltpu.roll(fresh[0], 96, 1)
    for j in range(1, 4):
        new_k = jnp.where(quarter == j, pltpu.roll(fresh[j], 32 * j, 1), new_k)
        new_v = jnp.where(quarter == j, pltpu.roll(fresh[j], (32 * j + 96) % 128, 1), new_v)
    new_k = rotate(new_k).astype(BF16)
    new_v = new_v.astype(BF16)
    nrow = sublanes((32, 16))
    ncol = lanes((32, 16))
    new_valid = ((nrow >> 3) == (ncol & 3)) & ((ncol >> 2) <= (nrow & 3))
    new_scores = jnp.where(new_valid, dot(n.q_send[...], new_k, NT) * INV_ROOT, masked_score)
    new_top = jnp.max(new_scores, axis=1, keepdims=True)
    new_weights = jnp.where(new_valid, jnp.exp(new_scores - new_top), 0.0)
    new_sum = jnp.sum(new_weights, axis=1, keepdims=True)
    new_out = dot(new_weights.astype(BF16), new_v)
    new_tile = jnp.zeros((8, 128), F32)
    new_total = jnp.zeros((8, 128), F32)
    for r in range(4):
        rows = slice(r * 8, r * 8 + 8)
        new_tile = jnp.where(tile_lane == r, new_top[rows], new_tile)
        new_total = jnp.where(tile_lane == r, new_sum[rows], new_total)

    stage4_out(0)
    arrived_heads(n.a_recv, n.s_a.at[1])
    arrived_heads(n.l_recv, n.s_l.at[1])

    stage3_out(1)

    peak = lax.fori_loop(0, 16, lambda i, m: jnp.maximum(m, n.l_recv[i]), new_tile)
    scale = jnp.exp(new_tile - peak)

    def join(i, state):
        total, parts = state
        tile = n.l_recv[i]
        scale = jnp.exp(tile - peak)
        part = n.a_recv[i].astype(F32)
        return (
            total + scale * pltpu.roll(tile, 64, 1),
            [acc + part[r * 8 : r * 8 + 8] * scale[:, r : r + 1] for r, acc in enumerate(parts)],
        )

    total, parts = lax.fori_loop(
        0,
        16,
        join,
        (
            scale * new_total,
            [new_out[r * 8 : r * 8 + 8] * scale[:, r : r + 1] for r in range(4)],
        ),
    )
    for r in range(4):
        n.q_rows[r * 8 : r * 8 + 8, :] = parts[r] / total[:, r : r + 1]
    for h, rows in enumerate((n.q_rot0, n.q_rot1)):
        for r in range(4):
            rows[pl.ds(r, 4, stride=4), :] = n.q_rows[r * 8 + h * 4 : r * 8 + h * 4 + 4, :]
    att = jnp.concatenate([n.q_rot0[...], n.q_rot1[...]], axis=1).astype(BF16)
    loads["wo"].wait()
    n.p_rows[...] = dot(att, n.v_wo[...])

    fd = n.v_down[...] - STEP_SCALE * summed(0)
    n.w_fd[...] = fd
    results = [
        pltpu.make_async_copy(src, dst, n.s_out.at[at])
        for at, (src, dst) in enumerate(
            ((n.w_dec, dec_out), (n.w_fd, fd_out), (n.w_fu, fu_out))
        )
    ]
    results[1].start()
    n.fd_pad[0:64, :] = jnp.zeros((64, 256), BF16)
    n.fd_pad[64:128, :] = fd.astype(BF16)
    low = dot(att, n.fd_pad[...], NT)

    o1 = rcopy(n.o_send1, n.o_recv1, n.s_o1.at[0], n.s_o1.at[1], sib)

    def out_part(part):
        for pair in range(4):
            both = []
            for e in (pair * 2, pair * 2 + 1):
                at = 160 * e // 128 * 128
                shift = 160 * e - at
                base = pl.multiple_of(part * 1280 + at, 128)
                window = n.p_rows[:, pl.ds(base, 256)]
                window = pltpu.roll(window, 256 - shift, 1) if shift else window
                both.append(
                    jnp.concatenate(
                        [window[:, :128], jnp.where(lane < 32, window[:, 128:], low)], axis=1
                    )
                )
            n.o_send1[part * 4 + pair] = jnp.where(c == 0, both[1], both[0]).astype(BF16)
            n.o_keep[part * 4 + pair] = jnp.where(c == 0, both[0], both[1])

    loop(4, out_part)
    o1.start()

    o1.wait_recv()

    def out_sum(i):
        n.o_send2[i] = (n.o_keep[i] + n.o_recv1[i].astype(F32)).astype(BF16)

    loop(16, out_sum)

    def o2(k):
        i = lax.rem(i0 + k, 16)
        return rcopy(
            n.o_send2.at[i], n.o_recv2.at[i0], n.s_o2.at[0], n.s_o2.at[1], tdev(2 * i + c)
        )

    loop(16, lambda k: o2(k).start(), 1)

    up_total = stage4_out(1)
    up_total = jnp.concatenate([up_total[:8], up_total[8:]], axis=1)
    for e in range(8):
        n.f_send[e] = pltpu.roll(up_total, (256 - 20 * e) % 256, 1)[:, :128]

    def f_copy(e):
        return rcopy(n.f_send.at[e], n.f_recv.at[g], n.s_f.at[0], n.s_f.at[1], f_to(e))

    f_own = lax.rem(t, 8)

    def f_start(e):
        @pl.when(jnp.logical_not(f_self & (e == f_own)))
        def _():
            f_copy(e).start()

    loop(8, f_start)

    @pl.when(f_self)
    def _():
        n.f_recv[g] = n.f_send[f_own]

    def left_heads(buf, sem):
        @pl.when(relays)
        def _():
            left(buf, 15, sem)

        @pl.when(jnp.logical_not(relays))
        def _():
            left(buf, 16, sem)

    @pl.when(relays)
    def _():
        left(n.down_half, 7, n.s_dn_sz.at[0])
        left(n.down_half, 16, n.s_dn_sy.at[0])

    @pl.when(jnp.logical_not(relays))
    def _():
        left(n.down_half, 8, n.s_dn_sz.at[0])

    left_heads(n.q_buf, n.s_q.at[0])
    left(n.n_buf, 3, n.s_n.at[0])
    for copy in pairs:
        copy.wait_send()
    bk.wait_send()
    pt.wait_send()
    left_heads(n.a_send, n.s_a.at[0])
    left_heads(n.l_send, n.s_l.at[0])
    left(n.d_send2, 7, n.s_g2.at[0, 0])
    left(n.u_send2, 7, n.s_g2.at[1, 0])
    left_heads(n.g_send3.at[0], n.s_g3.at[0, 0])
    left(n.g_recv4.at[0], 7, n.s_g4.at[0, 0])

    first_col = 160 * t
    base = lax.div(first_col, 128) * 128
    up_cols = n.v_up[:, pl.ds(pl.multiple_of(base, 128), 256)]
    up_cols = pltpu.roll(up_cols, lax.rem(256 - (first_col - base), 256), 1)
    fu = up_cols - STEP_SCALE * summed(1)
    n.fu_pad[0:64, :] = jnp.zeros((64, 256), BF16)
    n.fu_pad[64:128, :] = fu.astype(BF16)

    arrived(n.o_recv2, 15, n.s_o2.at[1])
    n.o_recv2[i0] = n.o_send2[i0]
    total = lax.fori_loop(
        1, 16, lambda i, a: a + n.o_recv2[i].astype(F32), n.o_recv2[0].astype(F32)
    )
    low = jnp.where(lane < 64, 0.0, total[:, 128:]).astype(BF16)
    decoded = total + adapter_scale * dot(low, n.fu_pad[...])
    wide_row = sublanes((16, 256))
    alive = (wide_row >> 2) < by_rollout(wide_row & 3, live)
    n.d_rows[...] = jnp.where(alive, decoded, 0.0)
    for s in range(4):
        n.w_dec[s] = n.d_rows[s * 4 : s * 4 + 4, 0:160].astype(BF16)
    results[0].start()

    @pl.when(f_self)
    def _():
        arrived(n.f_recv, 7, n.s_f.at[1])

    @pl.when(jnp.logical_not(f_self))
    def _():
        arrived(n.f_recv, 8, n.s_f.at[1])

    first_col = 640 * g + 20 * t
    base = jnp.minimum(lax.div(first_col, 128) * 128, 5120 - 256)
    up_cols = n.v_up[:, pl.ds(pl.multiple_of(base, 128), 256)]
    up_cols = pltpu.roll(up_cols, lax.rem(256 - (first_col - base), 256), 1)[:, :128]
    sums = jnp.concatenate([n.f_recv[j] for j in range(8)], axis=0)
    piece = up_cols - STEP_SCALE * sums
    n.w_fu[...] = jnp.concatenate([piece, piece], axis=0).T[0:20, 0:64]
    results[2].start()

    left_heads(n.g_send3.at[1], n.s_g3.at[1, 0])
    left(n.g_recv4.at[1], 7, n.s_g4.at[1, 0])
    o1.wait_send()
    left(n.o_send2, 15, n.s_o2.at[0])

    @pl.when(f_self)
    def _():
        left(n.f_send, 7, n.s_f.at[0])

    @pl.when(jnp.logical_not(f_self))
    def _():
        left(n.f_send, 8, n.s_f.at[0])

    for copy in results:
        copy.wait()


def hand_out(dec, fd, fu, dec_out, fd_out, fu_out):
    dec_out[...] = dec[...]
    fd_out[...] = fd[...]
    fu_out[...] = fu[...]


def body(hid, cot, down, up, wo, wq, wk, wv, x, kc, vc, fill, start, live):
    hbm = pl.BlockSpec(memory_space=pl.ANY)
    smem = pl.BlockSpec(memory_space=pltpu.SMEM)
    vmem = pl.BlockSpec(memory_space=pltpu.VMEM)
    shapes = (
        jax.ShapeDtypeStruct((4, 4, 160), BF16),
        jax.ShapeDtypeStruct((64, 256), F32),
        jax.ShapeDtypeStruct((20, 64), F32),
    )
    results = pl.pallas_call(
        kernel,
        out_shape=shapes,
        in_specs=[hbm] * 11 + [smem] * 3,
        out_specs=(hbm,) * 3,
        scratch_shapes=[pltpu.VMEM(shape, kind) for shape, kind in SCRATCH.values()]
        + [pltpu.SemaphoreType.DMA(shape) for shape in SEMS.values()],
        compiler_params=pltpu.CompilerParams(
            collective_id=0, has_side_effects=True, vmem_limit_bytes=56 * 2**20
        ),
        name="update_and_decode",
    )(hid, cot, down.T, up, wo, wq, wk.T, wv.T, x, kc, vc, fill, start, live)
    dec, fd, fu = pl.pallas_call(
        hand_out,
        out_shape=shapes,
        in_specs=[vmem] * 3,
        out_specs=(vmem,) * 3,
        compiler_params=pltpu.CompilerParams(vmem_limit_bytes=56 * 2**20),
        name="hand_out",
    )(*results)
    return dec, fd.T, fu.T


def solution(mesh):
    return jax.shard_map(
        body,
        mesh=mesh,
        in_specs=(
            P(("group", "tensor"), None),
            P(("group", "tensor"), None),
            P("tensor", None),
            P(),
            P("tensor", None),
            P(None, "tensor"),
            P(None, "tensor"),
            P(None, "tensor"),
            P(None, "group", None),
            P("group", "tensor", None),
            P("group", "tensor", None),
            P("group"),
            P("group"),
            P("group"),
        ),
        out_specs=(P(None, "group", "tensor"), P("tensor", None), P(None, ("group", "tensor"))),
        check_vma=False,
    )
```

```python
import math

import jax
import jax.numpy as jnp
from jax import lax
from jax.experimental import pallas as pl
from jax.experimental.pallas import tpu as pltpu
from jax.sharding import PartitionSpec as P

MESH = pl.DeviceIdType.MESH
F32 = jnp.float32
BF16 = jnp.bfloat16

adapter_scale = 0.01
rate_numerator = 50.0
rope_theta = 1000000.0
masked_score = -1e30

HD = 128
TOKENS = 32768
STEP_SCALE = adapter_scale * rate_numerator / math.sqrt(TOKENS)
INV_ROOT = 1.0 / math.sqrt(HD)

NN = (((1,), (0,)), ((), ()))
NT = (((1,), (1,)), ((), ()))


def dot(a, b, dims=NN):
    return lax.dot_general(a, b, dims, preferred_element_type=F32)


def rcopy(src, dst, ss, rs, dev):
    return pltpu.make_async_remote_copy(
        src_ref=src, dst_ref=dst, send_sem=ss, recv_sem=rs, device_id=dev, device_id_type=MESH
    )


def loop(n, fn, start=0):
    def step(k, carry):
        fn(k)
        return carry

    lax.fori_loop(start, n, step, 0)


SCRATCH = dict(
    v_down=((64, 256), F32),
    v_x=((4, 4, 5120), BF16),
    x_rows=((16, 5120), F32),
    v_wq=((5120, 256), BF16),
    v_wkv=((64, 5120), BF16),
    v_up=((64, 5120), F32),
    v_cot=((128, 5120), BF16),
    cot2=((128, 2560), BF16),
    hid2=((2, 128, 4096), BF16),
    v_wo=((256, 5120), BF16),
    kbuf=((2, 4, 128, 512), BF16),
    vbuf=((2, 4, 128, 512), BF16),
    down_own=((64, 256), BF16),
    down_half=((16, 64, 256), BF16),
    back2=((2, 64, 128), BF16),
    part_send=((64, 256), F32),
    part_recv=((64, 256), F32),
    q_rot0=((16, 128), F32),
    q_rot1=((16, 128), F32),
    q_rows=((32, 128), F32),
    q_send=((32, 128), BF16),
    q_buf=((16, 32, 128), BF16),
    n_buf=((4, 16, 128), BF16),
    n_send=((16, 128), BF16),
    a_send=((16, 32, 128), BF16),
    a_recv=((16, 32, 128), BF16),
    l_send=((16, 8, 128), F32),
    l_recv=((16, 8, 128), F32),
    d_send2=((8, 128, 256), BF16),
    d_recv2=((4, 2, 128, 256), BF16),
    u_send2=((8, 160, 128), BF16),
    u_recv2=((4, 2, 160, 128), BF16),
    g_send3=((2, 32, 16, 128), BF16),
    g_recv3=((2, 32, 16, 128), BF16),
    g_send4=((2, 16, 128), F32),
    g_recv4=((2, 8, 16, 128), F32),
    u_tmp=((64, 1280), F32),
    p_rows=((16, 5120), F32),
    fd_pad=((128, 256), BF16),
    fu_pad=((128, 256), BF16),
    o_send1=((16, 16, 256), BF16),
    o_keep=((16, 16, 256), F32),
    o_recv1=((16, 16, 256), BF16),
    o_send2=((16, 16, 256), BF16),
    o_recv2=((16, 16, 256), BF16),
    d_rows=((16, 256), F32),
    f_send=((8, 8, 128), F32),
    f_recv=((8, 8, 128), F32),
    w_dec=((4, 4, 160), BF16),
    w_fd=((64, 256), F32),
    w_fu=((20, 64), F32),
)
SEMS = dict(
    load=(14,),
    dn_sz=(1,),
    dn_sy=(1,),
    dn_r=(16,),
    sib_s=(4,),
    sib_r=(4,),
    bk=(2,),
    pt=(2,),
    q=(2,),
    n=(2,),
    a=(2,),
    l=(2,),
    g2=(2, 2),
    g3=(2, 2),
    g4=(2, 2),
    o1=(2,),
    o2=(2,),
    f=(2,),
    out=(3,),
)


class Names:
    pass


def lanes(shape):
    return lax.broadcasted_iota(jnp.int32, shape, len(shape) - 1)


def sublanes(shape):
    return lax.broadcasted_iota(jnp.int32, shape, len(shape) - 2)


def by_rollout(rollout, ref):
    picked = jnp.where(rollout == 0, ref[0], ref[1])
    picked = jnp.where(rollout == 2, ref[2], picked)
    return jnp.where(rollout == 3, ref[3], picked)


def kernel(
    hid, cot, down, up, wo, wq, wk, wv, x, kc, vc, fill_in, start_in, live_in, dec_out, fd_out, fu_out, *refs
):
    n = Names()
    for name, ref in zip(list(SCRATCH) + ["start", "fill", "live"] + ["s_" + key for key in SEMS], refs):
        setattr(n, name, ref)
    t = lax.axis_index("tensor")
    g = lax.axis_index("group")
    c = lax.rem(t, 2)
    i0 = lax.div(t, 2)
    y = lax.div(t, 16)
    z = lax.rem(i0, 8)
    t16 = lax.rem(t, 16)
    sib = {"tensor": t + 1 - 2 * c}
    other_y = lax.rem(t + 16, 32)
    g_other = g + 1 - 2 * lax.rem(g, 2)
    gx = lax.div(g, 2)
    gy = lax.rem(g, 2)
    relays = c == y

    def tdev(index):
        return {"tensor": index}

    def gdev(index):
        return {"group": index}

    def near(k):
        return lax.rem(lax.div(k + 1, 2) * (7 - 6 * lax.rem(k, 2)), 8)

    def far_z(k):
        return lax.rem(z + near(7 - k), 8)

    def far_core(k):
        return far_z(lax.div(k, 2)) * 2 + lax.rem(c + 1 + k, 2)

    def far_chip(k):
        return lax.rem(y + 1 + k, 2) * 8 + far_z(lax.div(k, 2))

    def far_x(k):
        at = 3 - k
        return lax.rem(gx + lax.div(at + 1, 2) * (3 - 2 * lax.rem(at, 2)), 4)

    def far_group(k):
        return far_x(lax.rem(k, 4)) * 2 + lax.rem(g + 1 - lax.div(k, 4), 2)

    f_from = 4 * g + lax.div(t, 8)
    f_self = f_from == t

    def f_to(e):
        return {"group": lax.div(t, 4), "tensor": 8 * lax.rem(t, 4) + e}

    def half(size, which):
        return pl.ds(pl.multiple_of(size * which, size), size)

    loads = dict(
        down=(down, n.v_down),
        x=(x, n.v_x),
        wq=(wq, n.v_wq),
        wk=(wk, n.v_wkv.at[pl.ds(0, 32)]),
        wv=(wv, n.v_wkv.at[pl.ds(32, 32)]),
        up=(up, n.v_up),
        cot=(cot, n.v_cot),
        hid=(hid.at[:, half(4096, c)], n.hid2.at[0]),
        k=(kc.at[:, :, half(512, c)], n.kbuf.at[0]),
        v=(vc.at[:, :, half(512, c)], n.vbuf.at[0]),
        wo=(wo, n.v_wo),
        start=(start_in, n.start),
        fill=(fill_in, n.fill),
        live=(live_in, n.live),
    )
    loads = {
        key: pltpu.make_async_copy(src, dst, n.s_load.at[at])
        for at, (key, (src, dst)) in enumerate(loads.items())
    }
    for copy in loads.values():
        copy.start()

    def arrived(buf, count, sem):
        part = buf.at[pl.ds(0, count)]
        rcopy(part, part, sem, sem, sib).wait_recv()

    def left(buf, count, sem):
        part = buf.at[pl.ds(0, count)]
        rcopy(part, part, sem, sem, sib).wait_send()

    def arrived_heads(buf, sem, more=0):
        @pl.when(relays)
        def _():
            arrived(buf, 15 + more, sem)

        @pl.when(jnp.logical_not(relays))
        def _():
            arrived(buf, 16 + more, sem)

    barrier = pltpu.get_barrier_semaphore()
    loop(
        32,
        lambda k: pl.semaphore_signal(
            barrier, inc=1, device_id=tdev(lax.rem(t + k, 32)), device_id_type=MESH
        ),
        1,
    )
    loop(
        8,
        lambda k: pl.semaphore_signal(
            barrier, inc=1, device_id=gdev(lax.rem(g + k, 8)), device_id_type=MESH
        ),
        1,
    )

    pl.semaphore_signal(
        barrier,
        inc=1,
        device_id={"group": g_other, "tensor": other_y},
        device_id_type=MESH,
    )

    loop(
        16,
        lambda k: pl.semaphore_signal(
            barrier,
            inc=1,
            device_id={"group": g_other, "tensor": 2 * k + y},
            device_id_type=MESH,
        ),
    )

    def f_greet(j):
        pl.semaphore_signal(
            barrier, inc=1, device_id={"group": j, "tensor": f_from}, device_id_type=MESH
        )

    loop(8, lambda k: f_greet(lax.rem(g + k, 8)), 1)

    @pl.when(jnp.logical_not(f_self))
    def _():
        f_greet(g)

    loads["down"].wait()
    n.down_own[...] = n.v_down[...].astype(BF16)

    pl.semaphore_wait(barrier, 63 - f_self.astype(jnp.int32))

    def dn_z(k):
        to = y * 16 + far_z(k) * 2 + y
        return rcopy(
            n.down_own, n.down_half.at[t16], n.s_dn_sz.at[0], n.s_dn_r.at[t16], tdev(to)
        )

    def dn_y(slot, group):
        return rcopy(
            n.down_half.at[slot],
            n.down_half.at[slot],
            n.s_dn_sy.at[0],
            n.s_dn_r.at[slot],
            {"group": group, "tensor": other_y},
        )

    def dn_pass(z_of, core):
        dn_y(z_of * 2 + core, g + core * (g_other - g)).start()

    loop(7, lambda k: dn_z(k).start())

    @pl.when(relays)
    def _():
        n.down_half[t16] = n.down_own[...]
        dn_pass(z, c)

    @pl.when(jnp.logical_not(relays))
    def _():
        dn_z(7).start()

    pairs = [
        rcopy(src, dst, n.s_sib_s.at[at], n.s_sib_r.at[at], sib)
        for at, (src, dst) in enumerate(
            (
                (hid.at[:, half(4096, 1 - c)], n.hid2.at[1]),
                (kc.at[:, :, half(512, 1 - c)], n.kbuf.at[1]),
                (vc.at[:, :, half(512, 1 - c)], n.vbuf.at[1]),
                (cot.at[:, half(2560, 1 - c)], n.cot2),
            )
        )
    ]
    pairs[0].start()

    loads["x"].wait()
    for s in range(4):
        n.x_rows[s * 4 : s * 4 + 4, :] = n.v_x[s].astype(F32)
    xb = n.x_rows[...].astype(BF16)
    row = sublanes((16, HD))
    lane = lanes((16, HD))
    loads["start"].wait()
    position = (by_rollout(row & 3, n.start) + (row >> 2)).astype(F32)
    freq = jnp.exp((lane & 63).astype(F32) * (-math.log(rope_theta) * 2.0 / HD))
    angle = position * freq
    cosine = jnp.cos(angle)
    sine = jnp.where(lane < 64, -jnp.sin(angle), jnp.sin(angle))

    def rotate(v):
        v = v.astype(BF16).astype(F32)
        return v * cosine + pltpu.roll(v, 64, 1) * sine

    loads["wq"].wait()
    q = dot(xb, n.v_wq[...])
    for h, rows in enumerate((n.q_rot0, n.q_rot1)):
        rows[...] = rotate(q[:, h * HD : (h + 1) * HD])
        for r in range(4):
            n.q_rows[r * 8 + h * 4 : r * 8 + h * 4 + 4, :] = rows[pl.ds(r, 4, stride=4), :]
    n.q_send[...] = n.q_rows[...].astype(BF16)

    send2 = (n.d_send2, n.u_send2)
    recv2 = (n.d_recv2, n.u_recv2)

    def g2(u, k):
        to = far_x(k)
        return rcopy(
            send2[u].at[pl.ds(2 * to, 2)],
            recv2[u].at[gx],
            n.s_g2.at[u, 0],
            n.s_g2.at[u, 1],
            gdev(2 * to + gy),
        )

    def g3(u, half, k):
        i = far_core(k)
        return rcopy(
            n.g_send3.at[u, half * 16 + i],
            n.g_recv3.at[u, gy * 16 + i0],
            n.s_g3.at[u, 0],
            n.s_g3.at[u, 1],
            {"group": 2 * gx + half, "tensor": 16 * c + i},
        )

    def g4(u, k):
        j = far_group(k)
        return rcopy(
            n.g_send4.at[u], n.g_recv4.at[u, g], n.s_g4.at[u, 0], n.s_g4.at[u, 1], gdev(j)
        )

    def stack8(first, second, j):
        rows = slice(j * 8, j * 8 + 8)
        return jnp.concatenate([first[rows], second[rows]], axis=0).astype(BF16)

    def stage3_out(u):
        arrived(recv2[u], 3, n.s_g2.at[u, 1])

        def total(half, row):
            rows = pl.ds(pl.multiple_of(row, 16), 16)
            sums = send2[u][2 * gx + half, rows, :].astype(F32)
            for dx in range(1, 4):
                sums = sums + recv2[u][lax.rem(gx + dx, 4), half, rows, :].astype(F32)
            return sums

        def send(i, low, high):
            n.g_send3[u, i] = jnp.concatenate([low, high], axis=0).astype(BF16)

        def down_sum(pair):
            for half in range(2):
                sums = total(half, pair * 16)
                for e in range(2):
                    piece = sums[e * 8 : e * 8 + 8]
                    send(half * 16 + pair * 2 + e, piece[:, :128], piece[:, 128:])

        def up_sum(part):
            for half in range(2):
                rest = total(half, 128 + part * 16)
                for pair in range(4):
                    sums = total(half, part * 64 + pair * 16)
                    high = pltpu.roll(rest, 128 - 32 * pair, 1) if pair else rest
                    for e in range(2):
                        rows = slice(e * 8, e * 8 + 8)
                        send(half * 16 + part * 8 + pair * 2 + e, sums[rows], high[rows])

        if u == 0:
            loop(8, down_sum)
        else:
            loop(2, up_sum)

        def both(k):
            g3(u, 1 - gy, k).start()
            g3(u, gy, k).start()

        loop(15, both)
        g3(u, 1 - gy, 15).start()

        @pl.when(jnp.logical_not(relays))
        def _():
            g3(u, gy, 15).start()

    def stage4_out(u):
        arrived_heads(n.g_recv3.at[u], n.s_g3.at[u, 1], 16)

        @pl.when(relays)
        def _():
            n.g_recv3[u, gy * 16 + i0] = n.g_send3[u, gy * 16 + t16]

        sums = [n.g_recv3[u, i].astype(F32) for i in range(4)]
        for i in range(4, 32):
            sums[i % 4] = sums[i % 4] + n.g_recv3[u, i].astype(F32)
        total = (sums[0] + sums[1]) + (sums[2] + sums[3])
        n.g_send4[u] = total
        n.g_recv4[u, g] = total
        loop(7, lambda k: g4(u, k).start())
        return total

    def summed(u):
        arrived(n.g_recv4.at[u], 7, n.s_g4.at[u, 1])
        pieces = [n.g_recv4[u, j] for j in range(8)]
        return jnp.concatenate(
            [jnp.concatenate([p[:8], p[8:]], axis=1) for p in pieces], axis=0
        )

    loads["up"].wait()
    loads["cot"].wait()
    n.back2[0] = dot(n.v_up[...].astype(BF16), n.v_cot[...], NT).astype(BF16)
    bk = rcopy(n.back2.at[0], n.back2.at[1], n.s_bk.at[0], n.s_bk.at[1], sib)
    bk.start()

    loads["wk"].wait()
    loads["wv"].wait()
    nkv = dot(xb, n.v_wkv[...], NT)
    n.n_send[...] = jnp.concatenate([nkv, nkv], axis=1).astype(BF16)
    b4 = lax.rem(t, 4)

    def n_copy(k):
        to = t - b4 + lax.rem(b4 + k, 4)
        return rcopy(n.n_send, n.n_buf.at[b4], n.s_n.at[0], n.s_n.at[1], tdev(to))

    loop(4, lambda k: n_copy(k).start(), 1)
    n.n_buf[b4] = n.n_send[...]

    loads["hid"].wait()
    pairs[0].wait_recv()
    bk.wait_recv()

    back = jnp.concatenate([n.back2[0], n.back2[1]], axis=1)

    def down_pair(pair):
        blocks = []
        for e in range(2):
            cols = pl.ds(pl.multiple_of((pair * 2 + e) * 256, 256), 256)
            both = jnp.concatenate([n.hid2[0, :, cols], n.hid2[1, :, cols]], axis=0)
            blocks.append(dot(back, both))
        rows = pl.ds(pl.multiple_of(pair * 16, 16), 16)
        for j in range(8):
            n.d_send2[j, rows, :] = stack8(*blocks, j)

    loop(8, down_pair)

    def q_copy(k):
        to = 2 * far_chip(k) + y
        return rcopy(n.q_send, n.q_buf.at[t16], n.s_q.at[0], n.s_q.at[1], tdev(to))

    @pl.when(jnp.logical_not(relays))
    def _():
        q_copy(15).start()

    loop(15, lambda k: q_copy(k).start())

    @pl.when(relays)
    def _():
        n.q_buf[t16] = n.q_send[...]

    for copy in pairs[1:]:
        copy.start()

    loop(3, lambda k: g2(0, k).start())

    def dn_recv(slot):
        dn_y(slot, g).wait_recv()

    @pl.when(relays)
    def _():
        dn_recv(z * 2 + 1 - c)
        dn_pass(z, 1 - c)

        def pass_on(k):
            from_z = far_z(k)
            for core in range(2):
                dn_recv(from_z * 2 + core)
                dn_pass(from_z, core)

        loop(7, pass_on)

    def reduce_part(part, total):
        for e in range(4):
            at = part * 4 + e
            cols = pl.ds(pl.multiple_of(at * 256, 256), 256)
            both = jnp.concatenate([n.hid2[0, :, cols], n.hid2[1, :, cols]], axis=0)
            total = total + dot(n.down_half[at], both, NT)
        return total

    pt = rcopy(n.part_send, n.part_recv, n.s_pt.at[0], n.s_pt.at[1], sib)

    def reduce():
        n.part_send[...] = lax.fori_loop(0, 4, reduce_part, jnp.zeros((64, 256), F32))
        pt.start()

    @pl.when(relays)
    def _():
        reduce()

    arrived_heads(n.q_buf, n.s_q.at[1])
    loads["fill"].wait()
    loads["k"].wait()
    loads["v"].wait()
    pairs[1].wait_recv()
    pairs[2].wait_recv()

    spot = lanes((32, 256))
    spot = jnp.where(spot < 128, t * 128 + spot, (t + 1 - 2 * c) * 128 + spot - 128)
    tile_lane = lanes((8, 128))

    def send_part(i):
        to = tdev(16 * c + i)
        stays = relays & (i == t16)

        @pl.when(jnp.logical_not(stays))
        def _():
            rcopy(n.a_send.at[i], n.a_recv.at[i0], n.s_a.at[0], n.s_a.at[1], to).start()
            rcopy(n.l_send.at[i], n.l_recv.at[i0], n.s_l.at[0], n.s_l.at[1], to).start()

        @pl.when(stays)
        def _():
            n.a_recv[i0] = n.a_send[i]
            n.l_recv[i0] = n.l_send[i]

    def attend(step):
        kk = lax.rem(step + 2 + lax.div(z, 2), 4)
        cols = pl.ds(pl.multiple_of(kk * HD, HD), HD)
        qs = [n.q_buf[kk * 4 + j].astype(F32) for j in range(4)]
        outs, tops, sums = [], [], []
        for r in range(4):
            qr = jnp.concatenate([a[r * 8 : r * 8 + 8] for a in qs], axis=0).astype(BF16)
            keys = jnp.concatenate([n.kbuf[0, r, :, cols], n.kbuf[1, r, :, cols]], axis=0)
            values = jnp.concatenate([n.vbuf[0, r, :, cols], n.vbuf[1, r, :, cols]], axis=0)
            valid = spot < n.fill[r]
            scores = jnp.where(valid, dot(qr, keys, NT) * INV_ROOT, masked_score)
            top = jnp.max(scores, axis=1, keepdims=True)
            weights = jnp.where(valid, jnp.exp(scores - top), 0.0)
            tops.append(top)
            sums.append(jnp.sum(weights, axis=1, keepdims=True))
            outs.append(dot(weights.astype(BF16), values))
        for j in range(4):
            rows = slice(j * 8, j * 8 + 8)
            n.a_send[kk * 4 + j] = jnp.concatenate([o[rows] for o in outs], axis=0).astype(BF16)
            tile = jnp.zeros((8, 128), F32)
            for r in range(4):
                tile = jnp.where(tile_lane == r, tops[r][rows], tile)
                tile = jnp.where(tile_lane == 64 + r, sums[r][rows], tile)
            n.l_send[kk * 4 + j] = tile
        for j in range(4):
            send_part(kk * 4 + j)

    loop(1, attend)

    stage3_out(0)
    loop(2, attend, 1)

    @pl.when(jnp.logical_not(relays))
    def _():
        loop(16, dn_recv)
        reduce()

    pt.wait_recv()
    pairs[3].wait_recv()
    reduced = jnp.concatenate(
        [
            n.part_send[:, :128] + n.part_recv[:, 128:],
            n.part_send[:, 128:] + n.part_recv[:, :128],
        ],
        axis=1,
    ).astype(BF16)

    def up_part(part):
        both = jnp.concatenate(
            [
                n.v_cot[:, pl.ds(pl.multiple_of(2560 * c + 1280 * part, 1280), 1280)],
                n.cot2[:, pl.ds(pl.multiple_of(1280 * part, 1280), 1280)],
            ],
            axis=0,
        )
        n.u_tmp[...] = dot(reduced, both)
        rest = [jnp.zeros((64, 128), F32)] * 2
        quarter = lanes((64, 128)) >> 5
        for pair in range(4):
            low = []
            for e in range(2):
                first = 160 * (pair * 2 + e)
                at = first // 128 * 128
                window = n.u_tmp[:, at : at + 256]
                window = pltpu.roll(window, 256 - (first - at), 1) if first > at else window
                low.append(window[:, :128])
                high = pltpu.roll(window[:, 128:], 32 * pair, 1) if pair else window[:, 128:]
                rest[e] = jnp.where(quarter == pair, high, rest[e])
            rows = pl.ds(pl.multiple_of(part * 64 + pair * 16, 16), 16)
            for j in range(8):
                n.u_send2[j, rows, :] = stack8(*low, j)
        rows = pl.ds(pl.multiple_of(128 + part * 16, 16), 16)
        for j in range(8):
            n.u_send2[j, rows, :] = stack8(*rest, j)

    loop(2, up_part)
    loop(3, lambda k: g2(1, k).start())

    loop(4, attend, 2)

    arrived(n.n_buf, 3, n.s_n.at[1])
    fresh = [n.n_buf[j].astype(F32) for j in range(4)]
    quarter = lane >> 5
    new_k = fresh[0]
    new_v = pltpu.roll(fresh[0], 96, 1)
    for j in range(1, 4):
        new_k = jnp.where(quarter == j, pltpu.roll(fresh[j], 32 * j, 1), new_k)
        new_v = jnp.where(quarter == j, pltpu.roll(fresh[j], (32 * j + 96) % 128, 1), new_v)
    new_k = rotate(new_k).astype(BF16)
    new_v = new_v.astype(BF16)
    nrow = sublanes((32, 16))
    ncol = lanes((32, 16))
    new_valid = ((nrow >> 3) == (ncol & 3)) & ((ncol >> 2) <= (nrow & 3))
    new_scores = jnp.where(new_valid, dot(n.q_send[...], new_k, NT) * INV_ROOT, masked_score)
    new_top = jnp.max(new_scores, axis=1, keepdims=True)
    new_weights = jnp.where(new_valid, jnp.exp(new_scores - new_top), 0.0)
    new_sum = jnp.sum(new_weights, axis=1, keepdims=True)
    new_out = dot(new_weights.astype(BF16), new_v)
    new_tile = jnp.zeros((8, 128), F32)
    new_total = jnp.zeros((8, 128), F32)
    for r in range(4):
        rows = slice(r * 8, r * 8 + 8)
        new_tile = jnp.where(tile_lane == r, new_top[rows], new_tile)
        new_total = jnp.where(tile_lane == r, new_sum[rows], new_total)

    stage4_out(0)
    stage3_out(1)

    arrived_heads(n.a_recv, n.s_a.at[1])
    arrived_heads(n.l_recv, n.s_l.at[1])

    peak = lax.fori_loop(0, 16, lambda i, m: jnp.maximum(m, n.l_recv[i]), new_tile, unroll=True)
    scale = jnp.exp(new_tile - peak)

    def join(i, state):
        total, parts = state
        tile = n.l_recv[i]
        scale = jnp.exp(tile - peak)
        part = n.a_recv[i].astype(F32)
        return (
            total + scale * pltpu.roll(tile, 64, 1),
            [acc + part[r * 8 : r * 8 + 8] * scale[:, r : r + 1] for r, acc in enumerate(parts)],
        )

    total, parts = lax.fori_loop(
        0,
        16,
        join,
        (
            scale * new_total,
            [new_out[r * 8 : r * 8 + 8] * scale[:, r : r + 1] for r in range(4)],
        ),
        unroll=4,
    )
    for r in range(4):
        n.q_rows[r * 8 : r * 8 + 8, :] = parts[r] / total[:, r : r + 1]
    for h, rows in enumerate((n.q_rot0, n.q_rot1)):
        for r in range(4):
            rows[pl.ds(r, 4, stride=4), :] = n.q_rows[r * 8 + h * 4 : r * 8 + h * 4 + 4, :]
    att = jnp.concatenate([n.q_rot0[...], n.q_rot1[...]], axis=1).astype(BF16)
    loads["wo"].wait()
    n.p_rows[...] = dot(att, n.v_wo[...])

    fd = n.v_down[...] - STEP_SCALE * summed(0)
    n.w_fd[...] = fd
    results = [
        pltpu.make_async_copy(src, dst, n.s_out.at[at])
        for at, (src, dst) in enumerate(
            ((n.w_dec, dec_out), (n.w_fd, fd_out), (n.w_fu, fu_out))
        )
    ]
    results[1].start()
    n.fd_pad[0:64, :] = jnp.zeros((64, 256), BF16)
    n.fd_pad[64:128, :] = fd.astype(BF16)
    low = dot(att, n.fd_pad[...], NT)

    o1 = rcopy(n.o_send1, n.o_recv1, n.s_o1.at[0], n.s_o1.at[1], sib)

    def out_part(part):
        for pair in range(4):
            both = []
            for e in (pair * 2, pair * 2 + 1):
                at = 160 * e // 128 * 128
                shift = 160 * e - at
                base = pl.multiple_of(part * 1280 + at, 128)
                window = n.p_rows[:, pl.ds(base, 256)]
                window = pltpu.roll(window, 256 - shift, 1) if shift else window
                both.append(
                    jnp.concatenate(
                        [window[:, :128], jnp.where(lane < 32, window[:, 128:], low)], axis=1
                    )
                )
            n.o_send1[part * 4 + pair] = jnp.where(c == 0, both[1], both[0]).astype(BF16)
            n.o_keep[part * 4 + pair] = jnp.where(c == 0, both[0], both[1])

    loop(4, out_part)
    o1.start()

    o1.wait_recv()

    def out_sum(i):
        n.o_send2[i] = (n.o_keep[i] + n.o_recv1[i].astype(F32)).astype(BF16)

    loop(16, out_sum)

    def o2(k):
        i = far_chip(k)
        return rcopy(
            n.o_send2.at[i], n.o_recv2.at[i0], n.s_o2.at[0], n.s_o2.at[1], tdev(2 * i + c)
        )

    loop(15, lambda k: o2(k).start())

    up_total = stage4_out(1)
    up_total = jnp.concatenate([up_total[:8], up_total[8:]], axis=1)
    for e in range(8):
        n.f_send[e] = pltpu.roll(up_total, (256 - 20 * e) % 256, 1)[:, :128]

    def f_copy(e):
        return rcopy(n.f_send.at[e], n.f_recv.at[g], n.s_f.at[0], n.s_f.at[1], f_to(e))

    f_own = lax.rem(t, 8)

    def f_start(e):
        @pl.when(jnp.logical_not(f_self & (e == f_own)))
        def _():
            f_copy(e).start()

    loop(8, f_start)

    @pl.when(f_self)
    def _():
        n.f_recv[g] = n.f_send[f_own]

    def left_heads(buf, sem, more=0):
        @pl.when(relays)
        def _():
            left(buf, 15 + more, sem)

        @pl.when(jnp.logical_not(relays))
        def _():
            left(buf, 16 + more, sem)

    @pl.when(relays)
    def _():
        left(n.down_half, 7, n.s_dn_sz.at[0])
        left(n.down_half, 16, n.s_dn_sy.at[0])

    @pl.when(jnp.logical_not(relays))
    def _():
        left(n.down_half, 8, n.s_dn_sz.at[0])

    left_heads(n.q_buf, n.s_q.at[0])
    left(n.n_buf, 3, n.s_n.at[0])
    for copy in pairs:
        copy.wait_send()
    bk.wait_send()
    pt.wait_send()
    left_heads(n.a_send, n.s_a.at[0])
    left_heads(n.l_send, n.s_l.at[0])
    left(n.d_recv2, 3, n.s_g2.at[0, 0])
    left(n.u_recv2, 3, n.s_g2.at[1, 0])
    left_heads(n.g_send3.at[0], n.s_g3.at[0, 0], 16)
    left(n.g_recv4.at[0], 7, n.s_g4.at[0, 0])

    first_col = 160 * t
    base = lax.div(first_col, 128) * 128
    up_cols = n.v_up[:, pl.ds(pl.multiple_of(base, 128), 256)]
    up_cols = pltpu.roll(up_cols, lax.rem(256 - (first_col - base), 256), 1)
    fu = up_cols - STEP_SCALE * summed(1)
    n.fu_pad[0:64, :] = jnp.zeros((64, 256), BF16)
    n.fu_pad[64:128, :] = fu.astype(BF16)

    arrived(n.o_recv2, 15, n.s_o2.at[1])
    n.o_recv2[i0] = n.o_send2[i0]
    total = lax.fori_loop(
        1, 16, lambda i, a: a + n.o_recv2[i].astype(F32), n.o_recv2[0].astype(F32)
    )
    low = jnp.where(lane < 64, 0.0, total[:, 128:]).astype(BF16)
    decoded = total + adapter_scale * dot(low, n.fu_pad[...])
    loads["live"].wait()
    wide_row = sublanes((16, 256))
    alive = (wide_row >> 2) < by_rollout(wide_row & 3, n.live)
    n.d_rows[...] = jnp.where(alive, decoded, 0.0)
    for s in range(4):
        n.w_dec[s] = n.d_rows[s * 4 : s * 4 + 4, 0:160].astype(BF16)
    results[0].start()

    @pl.when(f_self)
    def _():
        arrived(n.f_recv, 7, n.s_f.at[1])

    @pl.when(jnp.logical_not(f_self))
    def _():
        arrived(n.f_recv, 8, n.s_f.at[1])

    first_col = 640 * g + 20 * t
    base = jnp.minimum(lax.div(first_col, 128) * 128, 5120 - 256)
    up_cols = n.v_up[:, pl.ds(pl.multiple_of(base, 128), 256)]
    up_cols = pltpu.roll(up_cols, lax.rem(256 - (first_col - base), 256), 1)[:, :128]
    sums = jnp.concatenate([n.f_recv[j] for j in range(8)], axis=0)
    piece = up_cols - STEP_SCALE * sums
    n.w_fu[...] = jnp.concatenate([piece, piece], axis=0).T[0:20, 0:64]
    results[2].start()

    left_heads(n.g_send3.at[1], n.s_g3.at[1, 0], 16)
    left(n.g_recv4.at[1], 7, n.s_g4.at[1, 0])
    o1.wait_send()
    left(n.o_send2, 15, n.s_o2.at[0])

    @pl.when(f_self)
    def _():
        left(n.f_send, 7, n.s_f.at[0])

    @pl.when(jnp.logical_not(f_self))
    def _():
        left(n.f_send, 8, n.s_f.at[0])

    for copy in results:
        copy.wait()


def hand_out(dec, fd, fu, dec_out, fd_out, fu_out):
    dec_out[...] = dec[...]
    fd_out[...] = fd[...]
    fu_out[...] = fu[...]


def body(hid, cot, down, up, wo, wq, wk, wv, x, kc, vc, fill, start, live):
    hbm = pl.BlockSpec(memory_space=pl.ANY)
    vmem = pl.BlockSpec(memory_space=pltpu.VMEM)
    shapes = (
        jax.ShapeDtypeStruct((4, 4, 160), BF16),
        jax.ShapeDtypeStruct((64, 256), F32),
        jax.ShapeDtypeStruct((20, 64), F32),
    )
    results = pl.pallas_call(
        kernel,
        out_shape=shapes,
        in_specs=[hbm] * 14,
        out_specs=(hbm,) * 3,
        scratch_shapes=[pltpu.VMEM(shape, kind) for shape, kind in SCRATCH.values()]
        + [pltpu.SMEM((4,), jnp.int32)] * 3
        + [pltpu.SemaphoreType.DMA(shape) for shape in SEMS.values()],
        compiler_params=pltpu.CompilerParams(
            collective_id=0, has_side_effects=True, vmem_limit_bytes=56 * 2**20
        ),
        name="update_and_decode",
    )(hid, cot, down.T, up, wo, wq, wk.T, wv.T, x, kc, vc, fill, start, live)
    dec, fd, fu = pl.pallas_call(
        hand_out,
        out_shape=shapes,
        in_specs=[vmem] * 3,
        out_specs=(vmem,) * 3,
        compiler_params=pltpu.CompilerParams(vmem_limit_bytes=56 * 2**20),
        name="hand_out",
    )(*results)
    return dec, fd.T, fu.T


def solution(mesh):
    return jax.shard_map(
        body,
        mesh=mesh,
        in_specs=(
            P(("group", "tensor"), None),
            P(("group", "tensor"), None),
            P("tensor", None),
            P(),
            P("tensor", None),
            P(None, "tensor"),
            P(None, "tensor"),
            P(None, "tensor"),
            P(None, "group", None),
            P("group", "tensor", None),
            P("group", "tensor", None),
            P("group"),
            P("group"),
            P("group"),
        ),
        out_specs=(P(None, "group", "tensor"), P("tensor", None), P(None, ("group", "tensor"))),
        check_vma=False,
    )
```

```python
import math

import jax
import jax.numpy as jnp
from jax import lax
from jax.experimental import pallas as pl
from jax.experimental.pallas import tpu as pltpu
from jax.sharding import PartitionSpec as P

MESH = pl.DeviceIdType.MESH
F32 = jnp.float32
BF16 = jnp.bfloat16

adapter_scale = 0.01
rate_numerator = 50.0
rope_theta = 1000000.0
masked_score = -1e30

HD = 128
TOKENS = 32768
STEP_SCALE = adapter_scale * rate_numerator / math.sqrt(TOKENS)
INV_ROOT = 1.0 / math.sqrt(HD)

NN = (((1,), (0,)), ((), ()))
NT = (((1,), (1,)), ((), ()))


def dot(a, b, dims=NN):
    return lax.dot_general(a, b, dims, preferred_element_type=F32)


def rcopy(src, dst, ss, rs, dev):
    return pltpu.make_async_remote_copy(
        src_ref=src, dst_ref=dst, send_sem=ss, recv_sem=rs, device_id=dev, device_id_type=MESH
    )


def loop(n, fn, start=0):
    def step(k, carry):
        fn(k)
        return carry

    lax.fori_loop(start, n, step, 0)


def each(n, fn, start=0):
    for k in range(start, n):
        fn(k)


SCRATCH = dict(
    v_down=((64, 256), F32),
    v_x=((4, 4, 5120), BF16),
    x_rows=((16, 5120), F32),
    v_wq=((5120, 256), BF16),
    v_wkv=((64, 5120), BF16),
    v_up=((64, 5120), F32),
    v_cot=((128, 5120), BF16),
    cot2=((128, 2560), BF16),
    hid2=((2, 128, 4096), BF16),
    wo2=((2, 256, 2560), BF16),
    att2=((2, 16, 256), BF16),
    t_send=((16, 128), F32),
    t_recv=((16, 128), F32),
    kbuf=((2, 4, 128, 512), BF16),
    vbuf=((2, 4, 128, 512), BF16),
    down_own=((64, 256), BF16),
    down_half=((16, 64, 256), BF16),
    back2=((2, 64, 128), BF16),
    part_send=((64, 256), F32),
    part_recv=((64, 256), F32),
    q_rot0=((16, 128), F32),
    q_rot1=((16, 128), F32),
    q_rows=((32, 128), F32),
    q_send=((32, 128), BF16),
    q_buf=((16, 32, 128), BF16),
    n_buf=((4, 16, 128), BF16),
    n_send=((16, 128), BF16),
    a_send=((16, 32, 128), BF16),
    a_recv=((16, 32, 128), BF16),
    l_send=((16, 8, 128), F32),
    l_recv=((16, 8, 128), F32),
    d_send2=((8, 128, 256), BF16),
    d_recv2=((4, 2, 128, 256), BF16),
    u_send2=((8, 160, 128), BF16),
    u_recv2=((4, 2, 160, 128), BF16),
    g_send3=((2, 32, 16, 128), BF16),
    g_recv3=((2, 32, 16, 128), BF16),
    g_send4=((2, 16, 128), F32),
    g_recv4=((2, 8, 16, 128), F32),
    u_tmp=((64, 1280), F32),
    p_rows=((16, 2560), F32),
    fd_pad=((128, 256), BF16),
    fu_pad=((128, 256), BF16),
    o_keep=((16, 16, 256), F32),
    o_send2=((16, 16, 256), BF16),
    o_recv2=((16, 16, 256), BF16),
    d_rows=((16, 256), F32),
    f_send=((8, 8, 128), F32),
    f_recv=((8, 8, 128), F32),
    w_dec=((4, 4, 160), BF16),
    w_fd=((64, 256), F32),
    w_fu=((20, 64), F32),
)
SEMS = dict(
    load=(14,),
    dn_sz=(1,),
    dn_sy=(1,),
    dn_r=(16,),
    sib_s=(5,),
    sib_r=(5,),
    bk=(2,),
    pt=(2,),
    q=(2,),
    n=(2,),
    a=(2,),
    l=(2,),
    g2=(2, 2),
    g3=(2, 2),
    g4=(2, 2),
    at=(2,),
    tt=(2,),
    o2=(2,),
    f=(2,),
    out=(3,),
)


class Names:
    pass


def lanes(shape):
    return lax.broadcasted_iota(jnp.int32, shape, len(shape) - 1)


def sublanes(shape):
    return lax.broadcasted_iota(jnp.int32, shape, len(shape) - 2)


def by_rollout(rollout, ref):
    picked = jnp.where(rollout == 0, ref[0], ref[1])
    picked = jnp.where(rollout == 2, ref[2], picked)
    return jnp.where(rollout == 3, ref[3], picked)


def kernel(
    hid, cot, down, up, wo, wq, wk, wv, x, kc, vc, fill_in, start_in, live_in, dec_out, fd_out, fu_out, *refs
):
    n = Names()
    for name, ref in zip(list(SCRATCH) + ["start", "fill", "live"] + ["s_" + key for key in SEMS], refs):
        setattr(n, name, ref)
    t = lax.axis_index("tensor")
    g = lax.axis_index("group")
    c = lax.rem(t, 2)
    i0 = lax.div(t, 2)
    y = lax.div(t, 16)
    z = lax.rem(i0, 8)
    t16 = lax.rem(t, 16)
    sib = {"tensor": t + 1 - 2 * c}
    other_y = lax.rem(t + 16, 32)
    g_other = g + 1 - 2 * lax.rem(g, 2)
    gx = lax.div(g, 2)
    gy = lax.rem(g, 2)
    relays = c == y

    def tdev(index):
        return {"tensor": index}

    def gdev(index):
        return {"group": index}

    def far_z(k):
        return lax.rem(z + (4, 5, 3, 6, 2, 7, 1, 0)[k], 8)

    def far_core(k):
        return far_z(k // 2) * 2 + (c if k % 2 else 1 - c)

    def far_chip(k):
        return (y if k % 2 else 1 - y) * 8 + far_z(k // 2)

    def far_x(k):
        return lax.rem(gx + (2, 3, 1, 0)[k], 4)

    def far_group(k):
        return far_x(k % 4) * 2 + (1 - gy if k < 4 else gy)

    f_from = 4 * g + lax.div(t, 8)
    f_self = f_from == t

    def f_to(e):
        return {"group": lax.div(t, 4), "tensor": 8 * lax.rem(t, 4) + e}

    def half(size, which):
        return pl.ds(pl.multiple_of(size * which, size), size)

    loads = dict(
        down=(down, n.v_down),
        x=(x, n.v_x),
        wq=(wq, n.v_wq),
        wk=(wk, n.v_wkv.at[pl.ds(0, 32)]),
        wv=(wv, n.v_wkv.at[pl.ds(32, 32)]),
        up=(up, n.v_up),
        cot=(cot, n.v_cot),
        hid=(hid.at[:, half(4096, c)], n.hid2.at[0]),
        k=(kc.at[:, :, half(512, c)], n.kbuf.at[0]),
        v=(vc.at[:, :, half(512, c)], n.vbuf.at[0]),
        wo=(wo.at[:, half(2560, c)], n.wo2.at[0]),
        start=(start_in, n.start),
        fill=(fill_in, n.fill),
        live=(live_in, n.live),
    )
    loads = {
        key: pltpu.make_async_copy(src, dst, n.s_load.at[at])
        for at, (key, (src, dst)) in enumerate(loads.items())
    }
    for copy in loads.values():
        copy.start()

    def arrived(buf, count, sem):
        part = buf.at[pl.ds(0, count)]
        rcopy(part, part, sem, sem, sib).wait_recv()

    def left(buf, count, sem):
        part = buf.at[pl.ds(0, count)]
        rcopy(part, part, sem, sem, sib).wait_send()

    def arrived_heads(buf, sem, more=0):
        @pl.when(relays)
        def _():
            arrived(buf, 15 + more, sem)

        @pl.when(jnp.logical_not(relays))
        def _():
            arrived(buf, 16 + more, sem)

    barrier = pltpu.get_barrier_semaphore()
    each(
        32,
        lambda k: pl.semaphore_signal(
            barrier, inc=1, device_id=tdev(lax.rem(t + k, 32)), device_id_type=MESH
        ),
        1,
    )
    each(
        8,
        lambda k: pl.semaphore_signal(
            barrier, inc=1, device_id=gdev(lax.rem(g + k, 8)), device_id_type=MESH
        ),
        1,
    )

    pl.semaphore_signal(
        barrier,
        inc=1,
        device_id={"group": g_other, "tensor": other_y},
        device_id_type=MESH,
    )

    each(
        16,
        lambda k: pl.semaphore_signal(
            barrier,
            inc=1,
            device_id={"group": g_other, "tensor": 2 * k + y},
            device_id_type=MESH,
        ),
    )

    def f_greet(j):
        pl.semaphore_signal(
            barrier, inc=1, device_id={"group": j, "tensor": f_from}, device_id_type=MESH
        )

    each(8, lambda k: f_greet(lax.rem(g + k, 8)), 1)

    @pl.when(jnp.logical_not(f_self))
    def _():
        f_greet(g)

    loads["down"].wait()
    n.down_own[...] = n.v_down[...].astype(BF16)

    pl.semaphore_wait(barrier, 63 - f_self.astype(jnp.int32))

    def dn_z(k):
        to = y * 16 + far_z(k) * 2 + y
        return rcopy(
            n.down_own, n.down_half.at[t16], n.s_dn_sz.at[0], n.s_dn_r.at[t16], tdev(to)
        )

    def dn_y(slot, group):
        return rcopy(
            n.down_half.at[slot],
            n.down_half.at[slot],
            n.s_dn_sy.at[0],
            n.s_dn_r.at[slot],
            {"group": group, "tensor": other_y},
        )

    def dn_pass(z_of, core):
        dn_y(z_of * 2 + core, g + core * (g_other - g)).start()

    each(7, lambda k: dn_z(k).start())

    @pl.when(relays)
    def _():
        n.down_half[t16] = n.down_own[...]
        dn_pass(z, c)

    @pl.when(jnp.logical_not(relays))
    def _():
        dn_z(7).start()

    pairs = [
        rcopy(src, dst, n.s_sib_s.at[at], n.s_sib_r.at[at], sib)
        for at, (src, dst) in enumerate(
            (
                (hid.at[:, half(4096, 1 - c)], n.hid2.at[1]),
                (kc.at[:, :, half(512, 1 - c)], n.kbuf.at[1]),
                (vc.at[:, :, half(512, 1 - c)], n.vbuf.at[1]),
                (cot.at[:, half(2560, 1 - c)], n.cot2),
                (wo.at[:, half(2560, 1 - c)], n.wo2.at[1]),
            )
        )
    ]
    pairs[0].start()

    loads["x"].wait()
    for s in range(4):
        n.x_rows[s * 4 : s * 4 + 4, :] = n.v_x[s].astype(F32)
    xb = n.x_rows[...].astype(BF16)
    row = sublanes((16, HD))
    lane = lanes((16, HD))
    loads["start"].wait()
    position = (by_rollout(row & 3, n.start) + (row >> 2)).astype(F32)
    freq = jnp.exp((lane & 63).astype(F32) * (-math.log(rope_theta) * 2.0 / HD))
    angle = position * freq
    cosine = jnp.cos(angle)
    sine = jnp.where(lane < 64, -jnp.sin(angle), jnp.sin(angle))

    def rotate(v):
        v = v.astype(BF16).astype(F32)
        return v * cosine + pltpu.roll(v, 64, 1) * sine

    loads["wq"].wait()
    q = dot(xb, n.v_wq[...])
    for h, rows in enumerate((n.q_rot0, n.q_rot1)):
        rows[...] = rotate(q[:, h * HD : (h + 1) * HD])
        for r in range(4):
            n.q_rows[r * 8 + h * 4 : r * 8 + h * 4 + 4, :] = rows[pl.ds(r, 4, stride=4), :]
    n.q_send[...] = n.q_rows[...].astype(BF16)

    send2 = (n.d_send2, n.u_send2)
    recv2 = (n.d_recv2, n.u_recv2)

    def g2(u, part, k):
        to = far_x(k)
        size = (64, 80)[u]
        rows = pl.ds(part * size, size)
        return rcopy(
            send2[u].at[pl.ds(2 * to, 2), rows],
            recv2[u].at[gx, :, rows],
            n.s_g2.at[u, 0],
            n.s_g2.at[u, 1],
            gdev(2 * to + gy),
        )

    def g3(u, half, k):
        i = far_core(k)
        return rcopy(
            n.g_send3.at[u, half * 16 + i],
            n.g_recv3.at[u, gy * 16 + i0],
            n.s_g3.at[u, 0],
            n.s_g3.at[u, 1],
            {"group": 2 * gx + half, "tensor": 16 * c + i},
        )

    def g4(u, k):
        j = far_group(k)
        return rcopy(
            n.g_send4.at[u], n.g_recv4.at[u, g], n.s_g4.at[u, 0], n.s_g4.at[u, 1], gdev(j)
        )

    def stack8(first, second, j):
        rows = slice(j * 8, j * 8 + 8)
        return jnp.concatenate([first[rows], second[rows]], axis=0).astype(BF16)

    def stage3_out(u):
        arrived(recv2[u], 3, n.s_g2.at[u, 1])

        def total(half, row):
            rows = pl.ds(pl.multiple_of(row, 16), 16)
            sums = send2[u][2 * gx + half, rows, :].astype(F32)
            for dx in range(1, 4):
                sums = sums + recv2[u][lax.rem(gx + dx, 4), half, rows, :].astype(F32)
            return sums

        def send(i, low, high):
            n.g_send3[u, i] = jnp.concatenate([low, high], axis=0).astype(BF16)

        def down_sum(pair):
            for half in range(2):
                sums = total(half, pair * 16)
                for e in range(2):
                    piece = sums[e * 8 : e * 8 + 8]
                    send(half * 16 + pair * 2 + e, piece[:, :128], piece[:, 128:])

        def up_sum(part):
            for half in range(2):
                rest = total(half, part * 80 + 64)
                for pair in range(4):
                    sums = total(half, part * 80 + pair * 16)
                    high = pltpu.roll(rest, 128 - 32 * pair, 1) if pair else rest
                    for e in range(2):
                        rows = slice(e * 8, e * 8 + 8)
                        send(half * 16 + part * 8 + pair * 2 + e, sums[rows], high[rows])

        if u == 0:
            loop(8, down_sum)
        else:
            loop(2, up_sum)

        def both(k):
            g3(u, 1 - gy, k).start()
            g3(u, gy, k).start()

        each(15, both)
        g3(u, 1 - gy, 15).start()

        @pl.when(jnp.logical_not(relays))
        def _():
            g3(u, gy, 15).start()

    def stage4_out(u):
        arrived_heads(n.g_recv3.at[u], n.s_g3.at[u, 1], 16)

        @pl.when(relays)
        def _():
            n.g_recv3[u, gy * 16 + i0] = n.g_send3[u, gy * 16 + t16]

        sums = [n.g_recv3[u, i].astype(F32) for i in range(4)]
        for i in range(4, 32):
            sums[i % 4] = sums[i % 4] + n.g_recv3[u, i].astype(F32)
        total = (sums[0] + sums[1]) + (sums[2] + sums[3])
        n.g_send4[u] = total
        n.g_recv4[u, g] = total
        return total

    def stage4_send(u):
        each(7, lambda k: g4(u, k).start())

    def summed(u):
        arrived(n.g_recv4.at[u], 7, n.s_g4.at[u, 1])
        pieces = [n.g_recv4[u, j] for j in range(8)]
        return jnp.concatenate(
            [jnp.concatenate([p[:8], p[8:]], axis=1) for p in pieces], axis=0
        )

    loads["up"].wait()
    loads["cot"].wait()
    n.back2[0] = dot(n.v_up[...].astype(BF16), n.v_cot[...], NT).astype(BF16)
    bk = rcopy(n.back2.at[0], n.back2.at[1], n.s_bk.at[0], n.s_bk.at[1], sib)
    bk.start()

    loads["wk"].wait()
    loads["wv"].wait()
    nkv = dot(xb, n.v_wkv[...], NT)
    n.n_send[...] = jnp.concatenate([nkv, nkv], axis=1).astype(BF16)
    b4 = lax.rem(t, 4)

    def n_copy(k):
        to = t - b4 + lax.rem(b4 + k, 4)
        return rcopy(n.n_send, n.n_buf.at[b4], n.s_n.at[0], n.s_n.at[1], tdev(to))

    each(4, lambda k: n_copy(k).start(), 1)
    n.n_buf[b4] = n.n_send[...]

    loads["hid"].wait()
    pairs[0].wait_recv()
    bk.wait_recv()

    back = jnp.concatenate([n.back2[0], n.back2[1]], axis=1)

    def down_pair(pair):
        blocks = []
        for e in range(2):
            cols = pl.ds(pl.multiple_of((pair * 2 + e) * 256, 256), 256)
            both = jnp.concatenate([n.hid2[0, :, cols], n.hid2[1, :, cols]], axis=0)
            blocks.append(dot(back, both))
        rows = pl.ds(pl.multiple_of(pair * 16, 16), 16)
        for j in range(8):
            n.d_send2[j, rows, :] = stack8(*blocks, j)

    for part in range(2):
        loop(part * 4 + 4, down_pair, part * 4)
        each(3, lambda k: g2(0, part, k).start())

    def q_copy(k):
        to = 2 * far_chip(k) + y
        return rcopy(n.q_send, n.q_buf.at[t16], n.s_q.at[0], n.s_q.at[1], tdev(to))

    @pl.when(jnp.logical_not(relays))
    def _():
        q_copy(15).start()

    each(15, lambda k: q_copy(k).start())

    @pl.when(relays)
    def _():
        n.q_buf[t16] = n.q_send[...]

    for copy in pairs[1:]:
        copy.start()

    def dn_recv(slot):
        dn_y(slot, g).wait_recv()

    @pl.when(relays)
    def _():
        dn_recv(z * 2 + 1 - c)
        dn_pass(z, 1 - c)

        def pass_on(k):
            from_z = far_z(k)
            for core in range(2):
                dn_recv(from_z * 2 + core)
                dn_pass(from_z, core)

        each(7, pass_on)

    def reduce_slice(at, total):
        cols = pl.ds(pl.multiple_of(at * 256, 256), 256)
        both = jnp.concatenate([n.hid2[0, :, cols], n.hid2[1, :, cols]], axis=0)
        return total + dot(n.down_half[at], both, NT)

    pt = rcopy(n.part_send, n.part_recv, n.s_pt.at[0], n.s_pt.at[1], sib)

    @pl.when(relays)
    def _():
        total = jnp.zeros((64, 256), F32)
        for at in range(16):
            total = reduce_slice(at, total)
        n.part_send[...] = total
        pt.start()

    @pl.when(jnp.logical_not(relays))
    def _():
        total = jnp.zeros((64, 256), F32)
        for k in (7, 0, 1, 2, 3, 4, 5, 6):
            slices = [far_z(k) * 2 + core for core in range(2)]
            for at in slices:
                dn_recv(at)
            for at in slices:
                total = reduce_slice(at, total)
        n.part_send[...] = total
        pt.start()

    arrived_heads(n.q_buf, n.s_q.at[1])
    loads["fill"].wait()
    loads["k"].wait()
    loads["v"].wait()
    pairs[1].wait_recv()
    pairs[2].wait_recv()

    spot = lanes((64, 256))
    spot = jnp.where(spot < 128, t * 128 + spot, (t + 1 - 2 * c) * 128 + spot - 128)
    tile_lane = lanes((8, 128))

    def send_part(i):
        to = tdev(16 * c + i)
        stays = relays & (i == t16)

        @pl.when(jnp.logical_not(stays))
        def _():
            rcopy(n.a_send.at[i], n.a_recv.at[i0], n.s_a.at[0], n.s_a.at[1], to).start()
            rcopy(n.l_send.at[i], n.l_recv.at[i0], n.s_l.at[0], n.s_l.at[1], to).start()

        @pl.when(stays)
        def _():
            n.a_recv[i0] = n.a_send[i]
            n.l_recv[i0] = n.l_send[i]

    def pair_at(step):
        return lax.rem(step + 1 + lax.div(z, 4), 2)

    def send_parts(step):
        each(8, lambda j: send_part(pair_at(step) * 8 + j))

    def attend(step):
        pair = pair_at(step)
        cols = pl.ds(pl.multiple_of(pair * 256, 256), 256)
        qs = [n.q_buf[pair * 8 + j].astype(F32) for j in range(8)]
        none = jnp.zeros((32, 128), F32)
        outs, tops, sums = [], [], []
        for r in range(4):
            first, second = (
                jnp.concatenate([a[r * 8 : r * 8 + 8] for a in qs[h * 4 : h * 4 + 4]], axis=0)
                for h in range(2)
            )
            qr = jnp.concatenate(
                [
                    jnp.concatenate([first, none], axis=1),
                    jnp.concatenate([none, second], axis=1),
                ],
                axis=0,
            ).astype(BF16)
            keys = jnp.concatenate([n.kbuf[0, r, :, cols], n.kbuf[1, r, :, cols]], axis=0)
            values = jnp.concatenate([n.vbuf[0, r, :, cols], n.vbuf[1, r, :, cols]], axis=0)
            valid = spot < n.fill[r]
            scores = jnp.where(valid, dot(qr, keys, NT) * INV_ROOT, masked_score)
            top = jnp.max(scores, axis=1, keepdims=True)
            weights = jnp.where(valid, jnp.exp(scores - top), 0.0)
            tops.append(top)
            sums.append(jnp.sum(weights, axis=1, keepdims=True))
            outs.append(dot(weights.astype(BF16), values))
        for j in range(8):
            rows = slice(j * 8, j * 8 + 8)
            half = slice(j // 4 * 128, j // 4 * 128 + 128)
            n.a_send[pair * 8 + j] = jnp.concatenate(
                [o[rows, half] for o in outs], axis=0
            ).astype(BF16)
            tile = jnp.zeros((8, 128), F32)
            for r in range(4):
                tile = jnp.where(tile_lane == r, tops[r][rows], tile)
                tile = jnp.where(tile_lane == 64 + r, sums[r][rows], tile)
            n.l_send[pair * 8 + j] = tile

    loop(1, attend)

    stage3_out(0)
    send_parts(0)

    until = jnp.where(relays, 2, 1)
    def attend_and_send(step):
        attend(step)
        send_parts(step)

    loop(until, attend_and_send, 1)

    pt.wait_recv()
    pairs[3].wait_recv()
    reduced = jnp.concatenate(
        [
            n.part_send[:, :128] + n.part_recv[:, 128:],
            n.part_send[:, 128:] + n.part_recv[:, :128],
        ],
        axis=1,
    ).astype(BF16)

    def up_part(part):
        both = jnp.concatenate(
            [
                n.v_cot[:, pl.ds(pl.multiple_of(2560 * c + 1280 * part, 1280), 1280)],
                n.cot2[:, pl.ds(1280 * part, 1280)],
            ],
            axis=0,
        )
        n.u_tmp[...] = dot(reduced, both)
        rest = [jnp.zeros((64, 128), F32)] * 2
        quarter = lanes((64, 128)) >> 5
        for pair in range(4):
            low = []
            for e in range(2):
                first = 160 * (pair * 2 + e)
                at = first // 128 * 128
                window = n.u_tmp[:, at : at + 256]
                window = pltpu.roll(window, 256 - (first - at), 1) if first > at else window
                low.append(window[:, :128])
                high = pltpu.roll(window[:, 128:], 32 * pair, 1) if pair else window[:, 128:]
                rest[e] = jnp.where(quarter == pair, high, rest[e])
            rows = pl.ds(part * 80 + pair * 16, 16)
            for j in range(8):
                n.u_send2[j, rows, :] = stack8(*low, j)
        rows = pl.ds(part * 80 + 64, 16)
        for j in range(8):
            n.u_send2[j, rows, :] = stack8(*rest, j)
        each(3, lambda k: g2(1, part, k).start())

    each(2, up_part)

    loop(2, attend_and_send, until)

    arrived(n.n_buf, 3, n.s_n.at[1])
    fresh = [n.n_buf[j].astype(F32) for j in range(4)]
    quarter = lane >> 5
    new_k = fresh[0]
    new_v = pltpu.roll(fresh[0], 96, 1)
    for j in range(1, 4):
        new_k = jnp.where(quarter == j, pltpu.roll(fresh[j], 32 * j, 1), new_k)
        new_v = jnp.where(quarter == j, pltpu.roll(fresh[j], (32 * j + 96) % 128, 1), new_v)
    new_k = rotate(new_k).astype(BF16)
    new_v = new_v.astype(BF16)
    nrow = sublanes((32, 16))
    ncol = lanes((32, 16))
    new_valid = ((nrow >> 3) == (ncol & 3)) & ((ncol >> 2) <= (nrow & 3))
    new_scores = jnp.where(new_valid, dot(n.q_send[...], new_k, NT) * INV_ROOT, masked_score)
    new_top = jnp.max(new_scores, axis=1, keepdims=True)
    new_weights = jnp.where(new_valid, jnp.exp(new_scores - new_top), 0.0)
    new_sum = jnp.sum(new_weights, axis=1, keepdims=True)
    new_out = dot(new_weights.astype(BF16), new_v)
    new_tile = jnp.zeros((8, 128), F32)
    new_total = jnp.zeros((8, 128), F32)
    for r in range(4):
        rows = slice(r * 8, r * 8 + 8)
        new_tile = jnp.where(tile_lane == r, new_top[rows], new_tile)
        new_total = jnp.where(tile_lane == r, new_sum[rows], new_total)

    stage4_out(0)
    stage4_send(0)
    stage3_out(1)

    arrived_heads(n.a_recv, n.s_a.at[1])
    arrived_heads(n.l_recv, n.s_l.at[1])

    peak = lax.fori_loop(0, 16, lambda i, m: jnp.maximum(m, n.l_recv[i]), new_tile, unroll=True)
    scale = jnp.exp(new_tile - peak)

    def join(i, state):
        total, parts = state
        tile = n.l_recv[i]
        scale = jnp.exp(tile - peak)
        part = n.a_recv[i].astype(F32)
        return (
            total + scale * pltpu.roll(tile, 64, 1),
            [acc + part[r * 8 : r * 8 + 8] * scale[:, r : r + 1] for r, acc in enumerate(parts)],
        )

    total, parts = lax.fori_loop(
        0,
        16,
        join,
        (
            scale * new_total,
            [new_out[r * 8 : r * 8 + 8] * scale[:, r : r + 1] for r in range(4)],
        ),
        unroll=4,
    )
    for r in range(4):
        n.q_rows[r * 8 : r * 8 + 8, :] = parts[r] / total[:, r : r + 1]
    for h, rows in enumerate((n.q_rot0, n.q_rot1)):
        for r in range(4):
            rows[pl.ds(r, 4, stride=4), :] = n.q_rows[r * 8 + h * 4 : r * 8 + h * 4 + 4, :]
    att = jnp.concatenate([n.q_rot0[...], n.q_rot1[...]], axis=1).astype(BF16)
    n.att2[0] = att
    at = rcopy(n.att2.at[0], n.att2.at[1], n.s_at.at[0], n.s_at.at[1], sib)
    at.start()
    loads["wo"].wait()
    pairs[4].wait_recv()
    at.wait_recv()
    n.p_rows[...] = dot(n.att2[0], n.wo2[0]) + dot(n.att2[1], n.wo2[1])

    def out_part(part):
        for e in range(8):
            at = 160 * e // 128 * 128
            shift = 160 * e - at
            base = pl.multiple_of(part * 1280 + at, 128)
            window = n.p_rows[:, pl.ds(base, 256)]
            n.o_keep[part * 8 + e] = pltpu.roll(window, 256 - shift, 1) if shift else window

    loop(2, out_part)

    fd = n.v_down[...] - STEP_SCALE * summed(0)
    n.w_fd[...] = fd
    results = [
        pltpu.make_async_copy(src, dst, n.s_out.at[at])
        for at, (src, dst) in enumerate(
            ((n.w_dec, dec_out), (n.w_fd, fd_out), (n.w_fu, fu_out))
        )
    ]
    results[1].start()
    n.fd_pad[0:64, :] = jnp.zeros((64, 256), BF16)
    n.fd_pad[64:128, :] = fd.astype(BF16)
    n.t_send[...] = dot(att, n.fd_pad[...], NT)
    tt = rcopy(n.t_send, n.t_recv, n.s_tt.at[0], n.s_tt.at[1], sib)
    tt.start()

    def o2(k):
        i = far_core(k)
        return rcopy(
            n.o_send2.at[i], n.o_recv2.at[i0], n.s_o2.at[0], n.s_o2.at[1], tdev(16 * c + i)
        )

    tt.wait_recv()
    low = n.t_send[...] + n.t_recv[...]

    def out_sum(i):
        part = n.o_keep[i]
        n.o_send2[i] = jnp.concatenate(
            [part[:, :128], jnp.where(lane < 32, part[:, 128:], low)], axis=1
        ).astype(BF16)

    lax.fori_loop(0, 16, lambda i, a: (out_sum(i), a)[1], 0, unroll=4)
    each(15, lambda k: o2(k).start())

    @pl.when(jnp.logical_not(relays))
    def _():
        o2(15).start()

    up_total = stage4_out(1)
    up_total = jnp.concatenate([up_total[:8], up_total[8:]], axis=1)
    for e in range(8):
        n.f_send[e] = pltpu.roll(up_total, (256 - 20 * e) % 256, 1)[:, :128]

    def f_copy(e):
        return rcopy(n.f_send.at[e], n.f_recv.at[g], n.s_f.at[0], n.s_f.at[1], f_to(e))

    f_own = lax.rem(t, 8)

    def f_start(e):
        @pl.when(jnp.logical_not(f_self & (e == f_own)))
        def _():
            f_copy(e).start()

    each(8, f_start)

    @pl.when(f_self)
    def _():
        n.f_recv[g] = n.f_send[f_own]
    stage4_send(1)

    def left_heads(buf, sem, more=0):
        @pl.when(relays)
        def _():
            left(buf, 15 + more, sem)

        @pl.when(jnp.logical_not(relays))
        def _():
            left(buf, 16 + more, sem)

    @pl.when(relays)
    def _():
        left(n.down_half, 7, n.s_dn_sz.at[0])
        left(n.down_half, 16, n.s_dn_sy.at[0])

    @pl.when(jnp.logical_not(relays))
    def _():
        left(n.down_half, 8, n.s_dn_sz.at[0])

    left_heads(n.q_buf, n.s_q.at[0])
    left(n.n_buf, 3, n.s_n.at[0])
    for copy in pairs:
        copy.wait_send()
    bk.wait_send()
    pt.wait_send()
    left_heads(n.a_send, n.s_a.at[0])
    left_heads(n.l_send, n.s_l.at[0])
    left(n.d_recv2, 3, n.s_g2.at[0, 0])
    left(n.u_recv2, 3, n.s_g2.at[1, 0])
    left_heads(n.g_send3.at[0], n.s_g3.at[0, 0], 16)
    left(n.g_recv4.at[0], 7, n.s_g4.at[0, 0])

    first_col = 160 * t
    base = lax.div(first_col, 128) * 128
    up_cols = n.v_up[:, pl.ds(pl.multiple_of(base, 128), 256)]
    up_cols = pltpu.roll(up_cols, lax.rem(256 - (first_col - base), 256), 1)
    fu = up_cols - STEP_SCALE * summed(1)
    n.fu_pad[0:64, :] = jnp.zeros((64, 256), BF16)
    n.fu_pad[64:128, :] = fu.astype(BF16)

    arrived_heads(n.o_recv2, n.s_o2.at[1])
    @pl.when(relays)
    def _():
        n.o_recv2[i0] = n.o_send2[t16]

    total = lax.fori_loop(
        1, 16, lambda i, a: a + n.o_recv2[i].astype(F32), n.o_recv2[0].astype(F32), unroll=5
    )
    low = jnp.where(lane < 64, 0.0, total[:, 128:]).astype(BF16)
    decoded = total + adapter_scale * dot(low, n.fu_pad[...])
    loads["live"].wait()
    wide_row = sublanes((16, 256))
    alive = (wide_row >> 2) < by_rollout(wide_row & 3, n.live)
    n.d_rows[...] = jnp.where(alive, decoded, 0.0)
    for s in range(4):
        n.w_dec[s] = n.d_rows[s * 4 : s * 4 + 4, 0:160].astype(BF16)
    results[0].start()

    @pl.when(f_self)
    def _():
        arrived(n.f_recv, 7, n.s_f.at[1])

    @pl.when(jnp.logical_not(f_self))
    def _():
        arrived(n.f_recv, 8, n.s_f.at[1])

    first_col = 640 * g + 20 * t
    base = jnp.minimum(lax.div(first_col, 128) * 128, 5120 - 256)
    up_cols = n.v_up[:, pl.ds(pl.multiple_of(base, 128), 256)]
    up_cols = pltpu.roll(up_cols, lax.rem(256 - (first_col - base), 256), 1)[:, :128]
    sums = jnp.concatenate([n.f_recv[j] for j in range(8)], axis=0)
    piece = up_cols - STEP_SCALE * sums
    n.w_fu[...] = jnp.concatenate([piece, piece], axis=0).T[0:20, 0:64]
    results[2].start()

    left_heads(n.g_send3.at[1], n.s_g3.at[1, 0], 16)
    left(n.g_recv4.at[1], 7, n.s_g4.at[1, 0])
    at.wait_send()
    tt.wait_send()
    left_heads(n.o_send2, n.s_o2.at[0])

    @pl.when(f_self)
    def _():
        left(n.f_send, 7, n.s_f.at[0])

    @pl.when(jnp.logical_not(f_self))
    def _():
        left(n.f_send, 8, n.s_f.at[0])

    for copy in results:
        copy.wait()


def hand_out(dec, fd, fu, dec_out, fd_out, fu_out):
    dec_out[...] = dec[...]
    fd_out[...] = fd[...]
    fu_out[...] = fu[...]


def body(hid, cot, down, up, wo, wq, wk, wv, x, kc, vc, fill, start, live):
    hbm = pl.BlockSpec(memory_space=pl.ANY)
    vmem = pl.BlockSpec(memory_space=pltpu.VMEM)
    shapes = (
        jax.ShapeDtypeStruct((4, 4, 160), BF16),
        jax.ShapeDtypeStruct((64, 256), F32),
        jax.ShapeDtypeStruct((20, 64), F32),
    )
    results = pl.pallas_call(
        kernel,
        out_shape=shapes,
        in_specs=[hbm] * 14,
        out_specs=(hbm,) * 3,
        scratch_shapes=[pltpu.VMEM(shape, kind) for shape, kind in SCRATCH.values()]
        + [pltpu.SMEM((4,), jnp.int32)] * 3
        + [pltpu.SemaphoreType.DMA(shape) for shape in SEMS.values()],
        compiler_params=pltpu.CompilerParams(
            collective_id=0, has_side_effects=True, vmem_limit_bytes=56 * 2**20
        ),
        name="update_and_decode",
    )(hid, cot, down.T, up, wo, wq, wk.T, wv.T, x, kc, vc, fill, start, live)
    dec, fd, fu = pl.pallas_call(
        hand_out,
        out_shape=shapes,
        in_specs=[vmem] * 3,
        out_specs=(vmem,) * 3,
        compiler_params=pltpu.CompilerParams(vmem_limit_bytes=56 * 2**20),
        name="hand_out",
    )(*results)
    return dec, fd.T, fu.T


def solution(mesh):
    return jax.shard_map(
        body,
        mesh=mesh,
        in_specs=(
            P(("group", "tensor"), None),
            P(("group", "tensor"), None),
            P("tensor", None),
            P(),
            P("tensor", None),
            P(None, "tensor"),
            P(None, "tensor"),
            P(None, "tensor"),
            P(None, "group", None),
            P("group", "tensor", None),
            P("group", "tensor", None),
            P("group"),
            P("group"),
            P("group"),
        ),
        out_specs=(P(None, "group", "tensor"), P("tensor", None), P(None, ("group", "tensor"))),
        check_vma=False,
    )
```

```python
import math

import jax
import jax.numpy as jnp
from jax import lax
from jax.experimental import pallas as pl
from jax.experimental.pallas import tpu as pltpu
from jax.sharding import PartitionSpec as P

MESH = pl.DeviceIdType.MESH
F32 = jnp.float32
BF16 = jnp.bfloat16

adapter_scale = 0.01
rate_numerator = 50.0
rope_theta = 1000000.0
masked_score = -1e30

HD = 128
TOKENS = 32768
STEP_SCALE = adapter_scale * rate_numerator / math.sqrt(TOKENS)
INV_ROOT = 1.0 / math.sqrt(HD)

NN = (((1,), (0,)), ((), ()))
NT = (((1,), (1,)), ((), ()))


def dot(a, b, dims=NN):
    return lax.dot_general(a, b, dims, preferred_element_type=F32)


def rcopy(src, dst, ss, rs, dev):
    return pltpu.make_async_remote_copy(
        src_ref=src, dst_ref=dst, send_sem=ss, recv_sem=rs, device_id=dev, device_id_type=MESH
    )


def loop(n, fn, start=0):
    def step(k, carry):
        fn(k)
        return carry

    lax.fori_loop(start, n, step, 0)


def each(n, fn, start=0):
    for k in range(start, n):
        fn(k)


SCRATCH = dict(
    v_down=((64, 256), F32),
    v_x=((4, 4, 5120), BF16),
    x_rows=((16, 5120), F32),
    v_wq=((5120, 256), BF16),
    v_wkv=((64, 5120), BF16),
    v_up=((64, 5120), F32),
    v_cot=((128, 5120), BF16),
    cot2=((128, 2560), BF16),
    hid2=((2, 128, 4096), BF16),
    wo2=((2, 256, 2560), BF16),
    att2=((2, 16, 256), BF16),
    t_send=((16, 128), F32),
    t_recv=((16, 128), F32),
    kbuf=((2, 4, 128, 512), BF16),
    vbuf=((2, 4, 128, 512), BF16),
    down_own=((64, 256), BF16),
    down_half=((16, 64, 256), BF16),
    back2=((2, 64, 128), BF16),
    part_send=((64, 256), F32),
    part_recv=((64, 256), F32),
    q_rot0=((16, 128), F32),
    q_rot1=((16, 128), F32),
    q_rows=((32, 128), F32),
    q_send=((32, 128), BF16),
    q_buf=((16, 32, 128), BF16),
    n_buf=((4, 16, 128), BF16),
    n_send=((16, 128), BF16),
    a_send=((16, 32, 128), BF16),
    a_recv=((16, 32, 128), BF16),
    l_send=((16, 8, 128), F32),
    l_recv=((16, 8, 128), F32),
    d_send2=((8, 128, 256), BF16),
    d_recv2=((4, 2, 128, 256), BF16),
    u_send2=((8, 160, 128), BF16),
    u_recv2=((4, 2, 160, 128), BF16),
    g_send3=((2, 32, 16, 128), BF16),
    g_recv3=((2, 32, 16, 128), BF16),
    g_send4=((2, 16, 128), F32),
    g_recv4=((2, 8, 16, 128), F32),
    u_tmp=((64, 1280), F32),
    p_rows=((16, 2560), F32),
    fd_pad=((128, 256), BF16),
    fu_pad=((128, 256), BF16),
    o_keep=((16, 16, 256), F32),
    o_send2=((16, 16, 256), BF16),
    o_recv2=((16, 16, 256), BF16),
    d_rows=((16, 256), F32),
    f_send=((8, 8, 128), F32),
    f_recv=((8, 8, 128), F32),
    w_dec=((4, 4, 160), BF16),
    w_fd=((64, 256), F32),
    w_fu=((20, 64), F32),
)
SEMS = dict(
    load=(14,),
    dn_sz=(1,),
    dn_sy=(1,),
    dn_r=(16,),
    sib_s=(5,),
    sib_r=(5,),
    bk=(2,),
    pt=(2,),
    q=(2,),
    n=(2,),
    a=(2,),
    l=(2,),
    g2=(2, 2),
    g3=(2, 2),
    g4=(2, 2),
    at=(2,),
    tt=(2,),
    o2=(2,),
    f=(2,),
    out=(3,),
)


class Names:
    pass


def lanes(shape):
    return lax.broadcasted_iota(jnp.int32, shape, len(shape) - 1)


def sublanes(shape):
    return lax.broadcasted_iota(jnp.int32, shape, len(shape) - 2)


def by_rollout(rollout, ref):
    picked = jnp.where(rollout == 0, ref[0], ref[1])
    picked = jnp.where(rollout == 2, ref[2], picked)
    return jnp.where(rollout == 3, ref[3], picked)


def kernel(
    hid, cot, down, up, wo, wq, wk, wv, x, kc, vc, fill_in, start_in, live_in, dec_out, fd_out, fu_out, *refs
):
    n = Names()
    for name, ref in zip(list(SCRATCH) + ["start", "fill", "live"] + ["s_" + key for key in SEMS], refs):
        setattr(n, name, ref)
    t = lax.axis_index("tensor")
    g = lax.axis_index("group")
    c = lax.rem(t, 2)
    i0 = lax.div(t, 2)
    y = lax.div(t, 16)
    z = lax.rem(i0, 8)
    t16 = lax.rem(t, 16)
    sib = {"tensor": t + 1 - 2 * c}
    other_y = lax.rem(t + 16, 32)
    g_other = g + 1 - 2 * lax.rem(g, 2)
    gx = lax.div(g, 2)
    gy = lax.rem(g, 2)
    relays = c == y

    def tdev(index):
        return {"tensor": index}

    def gdev(index):
        return {"group": index}

    def far_z(k):
        return lax.rem(z + (4, 5, 3, 6, 2, 7, 1, 0)[k], 8)

    def far_core(k):
        return far_z(k // 2) * 2 + (c if k % 2 else 1 - c)

    def far_chip(k):
        return (y if k % 2 else 1 - y) * 8 + far_z(k // 2)

    def far_x(k):
        return lax.rem(gx + (2, 3, 1, 0)[k], 4)

    def far_group(k):
        return far_x(k % 4) * 2 + (1 - gy if k < 4 else gy)

    f_from = 4 * g + lax.div(t, 8)
    f_self = f_from == t

    def f_to(e):
        return {"group": lax.div(t, 4), "tensor": 8 * lax.rem(t, 4) + e}

    def half(size, which):
        return pl.ds(pl.multiple_of(size * which, size), size)

    loads = dict(
        down=(down, n.v_down),
        x=(x, n.v_x),
        wq=(wq, n.v_wq),
        wk=(wk, n.v_wkv.at[pl.ds(0, 32)]),
        wv=(wv, n.v_wkv.at[pl.ds(32, 32)]),
        up=(up, n.v_up),
        cot=(cot, n.v_cot),
        hid=(hid.at[:, half(4096, c)], n.hid2.at[0]),
        k=(kc.at[:, :, half(512, c)], n.kbuf.at[0]),
        v=(vc.at[:, :, half(512, c)], n.vbuf.at[0]),
        wo=(wo.at[:, half(2560, c)], n.wo2.at[0]),
        start=(start_in, n.start),
        fill=(fill_in, n.fill),
        live=(live_in, n.live),
    )
    loads = {
        key: pltpu.make_async_copy(src, dst, n.s_load.at[at])
        for at, (key, (src, dst)) in enumerate(loads.items())
    }
    for copy in loads.values():
        copy.start()

    def arrived(buf, count, sem):
        part = buf.at[pl.ds(0, count)]
        rcopy(part, part, sem, sem, sib).wait_recv()

    def left(buf, count, sem):
        part = buf.at[pl.ds(0, count)]
        rcopy(part, part, sem, sem, sib).wait_send()

    def arrived_heads(buf, sem, more=0):
        @pl.when(relays)
        def _():
            arrived(buf, 15 + more, sem)

        @pl.when(jnp.logical_not(relays))
        def _():
            arrived(buf, 16 + more, sem)

    barrier = pltpu.get_barrier_semaphore()
    def t_greet(k):
        pl.semaphore_signal(
            barrier, inc=1, device_id=tdev(lax.rem(t + k, 32)), device_id_type=MESH
        )

    near = (1, 31, 16, 15, 17)
    for k in near:
        t_greet(k)
    each(
        8,
        lambda k: pl.semaphore_signal(
            barrier, inc=1, device_id=gdev(lax.rem(g + k, 8)), device_id_type=MESH
        ),
        1,
    )

    pl.semaphore_signal(
        barrier,
        inc=1,
        device_id={"group": g_other, "tensor": other_y},
        device_id_type=MESH,
    )

    each(
        16,
        lambda k: pl.semaphore_signal(
            barrier,
            inc=1,
            device_id={"group": g_other, "tensor": 2 * k + y},
            device_id_type=MESH,
        ),
    )

    def f_greet(j):
        pl.semaphore_signal(
            barrier, inc=1, device_id={"group": j, "tensor": f_from}, device_id_type=MESH
        )

    each(8, lambda k: f_greet(lax.rem(g + k, 8)), 1)

    @pl.when(jnp.logical_not(f_self))
    def _():
        f_greet(g)

    for k in range(1, 32):
        if k not in near:
            t_greet(k)

    loads["down"].wait()
    n.down_own[...] = n.v_down[...].astype(BF16)

    pl.semaphore_wait(barrier, 63 - f_self.astype(jnp.int32))

    def dn_z(k):
        to = y * 16 + far_z(k) * 2 + y
        return rcopy(
            n.down_own, n.down_half.at[t16], n.s_dn_sz.at[0], n.s_dn_r.at[t16], tdev(to)
        )

    def dn_y(slot, group):
        return rcopy(
            n.down_half.at[slot],
            n.down_half.at[slot],
            n.s_dn_sy.at[0],
            n.s_dn_r.at[slot],
            {"group": group, "tensor": other_y},
        )

    def dn_pass(z_of, core):
        dn_y(z_of * 2 + core, g + core * (g_other - g)).start()

    each(7, lambda k: dn_z(k).start())

    @pl.when(relays)
    def _():
        n.down_half[t16] = n.down_own[...]
        dn_pass(z, c)

    @pl.when(jnp.logical_not(relays))
    def _():
        dn_z(7).start()

    pairs = [
        rcopy(src, dst, n.s_sib_s.at[at], n.s_sib_r.at[at], sib)
        for at, (src, dst) in enumerate(
            (
                (hid.at[:, half(4096, 1 - c)], n.hid2.at[1]),
                (kc.at[:, :, half(512, 1 - c)], n.kbuf.at[1]),
                (vc.at[:, :, half(512, 1 - c)], n.vbuf.at[1]),
                (cot.at[:, half(2560, 1 - c)], n.cot2),
                (wo.at[:, half(2560, 1 - c)], n.wo2.at[1]),
            )
        )
    ]
    pairs[0].start()

    loads["x"].wait()
    for s in range(4):
        n.x_rows[s * 4 : s * 4 + 4, :] = n.v_x[s].astype(F32)
    xb = n.x_rows[...].astype(BF16)
    row = sublanes((16, HD))
    lane = lanes((16, HD))
    loads["start"].wait()
    position = (by_rollout(row & 3, n.start) + (row >> 2)).astype(F32)
    freq = jnp.exp((lane & 63).astype(F32) * (-math.log(rope_theta) * 2.0 / HD))
    angle = position * freq
    cosine = jnp.cos(angle)
    sine = jnp.where(lane < 64, -jnp.sin(angle), jnp.sin(angle))

    def rotate(v):
        v = v.astype(BF16).astype(F32)
        return v * cosine + pltpu.roll(v, 64, 1) * sine

    loads["wq"].wait()
    q = dot(xb, n.v_wq[...])
    for h, rows in enumerate((n.q_rot0, n.q_rot1)):
        rows[...] = rotate(q[:, h * HD : (h + 1) * HD])
        for r in range(4):
            n.q_rows[r * 8 + h * 4 : r * 8 + h * 4 + 4, :] = rows[pl.ds(r, 4, stride=4), :]
    n.q_send[...] = n.q_rows[...].astype(BF16)

    send2 = (n.d_send2, n.u_send2)
    recv2 = (n.d_recv2, n.u_recv2)

    def g2(u, part, k):
        to = far_x(k)
        size = (64, 80)[u]
        rows = pl.ds(part * size, size)
        return rcopy(
            send2[u].at[pl.ds(2 * to, 2), rows],
            recv2[u].at[gx, :, rows],
            n.s_g2.at[u, 0],
            n.s_g2.at[u, 1],
            gdev(2 * to + gy),
        )

    def g3(u, half, k):
        i = far_core(k)
        return rcopy(
            n.g_send3.at[u, half * 16 + i],
            n.g_recv3.at[u, gy * 16 + i0],
            n.s_g3.at[u, 0],
            n.s_g3.at[u, 1],
            {"group": 2 * gx + half, "tensor": 16 * c + i},
        )

    def g4(u, k):
        j = far_group(k)
        return rcopy(
            n.g_send4.at[u], n.g_recv4.at[u, g], n.s_g4.at[u, 0], n.s_g4.at[u, 1], gdev(j)
        )

    def stack8(first, second, j):
        rows = slice(j * 8, j * 8 + 8)
        return jnp.concatenate([first[rows], second[rows]], axis=0).astype(BF16)

    def stage3_out(u):
        arrived(recv2[u], 3, n.s_g2.at[u, 1])

        def total(half, row):
            rows = pl.ds(pl.multiple_of(row, 16), 16)
            sums = send2[u][2 * gx + half, rows, :].astype(F32)
            for dx in range(1, 4):
                sums = sums + recv2[u][lax.rem(gx + dx, 4), half, rows, :].astype(F32)
            return sums

        def send(i, low, high):
            n.g_send3[u, i] = jnp.concatenate([low, high], axis=0).astype(BF16)

        def down_sum(pair):
            for half in range(2):
                sums = total(half, pair * 16)
                for e in range(2):
                    piece = sums[e * 8 : e * 8 + 8]
                    send(half * 16 + pair * 2 + e, piece[:, :128], piece[:, 128:])

        def up_sum(part):
            for half in range(2):
                rest = total(half, part * 80 + 64)
                for pair in range(4):
                    sums = total(half, part * 80 + pair * 16)
                    high = pltpu.roll(rest, 128 - 32 * pair, 1) if pair else rest
                    for e in range(2):
                        rows = slice(e * 8, e * 8 + 8)
                        send(half * 16 + part * 8 + pair * 2 + e, sums[rows], high[rows])

        if u == 0:
            loop(8, down_sum)
        else:
            loop(2, up_sum)

        def both(k):
            g3(u, 1 - gy, k).start()
            g3(u, gy, k).start()

        each(15, both)
        g3(u, 1 - gy, 15).start()

        @pl.when(jnp.logical_not(relays))
        def _():
            g3(u, gy, 15).start()

    def stage4_out(u):
        arrived_heads(n.g_recv3.at[u], n.s_g3.at[u, 1], 16)

        @pl.when(relays)
        def _():
            n.g_recv3[u, gy * 16 + i0] = n.g_send3[u, gy * 16 + t16]

        sums = [n.g_recv3[u, i].astype(F32) for i in range(4)]
        for i in range(4, 32):
            sums[i % 4] = sums[i % 4] + n.g_recv3[u, i].astype(F32)
        total = (sums[0] + sums[1]) + (sums[2] + sums[3])
        n.g_send4[u] = total
        n.g_recv4[u, g] = total
        return total

    def stage4_send(u):
        each(7, lambda k: g4(u, k).start())

    def summed(u):
        arrived(n.g_recv4.at[u], 7, n.s_g4.at[u, 1])
        pieces = [n.g_recv4[u, j] for j in range(8)]
        return jnp.concatenate(
            [jnp.concatenate([p[:8], p[8:]], axis=1) for p in pieces], axis=0
        )

    loads["up"].wait()
    loads["cot"].wait()
    n.back2[0] = dot(n.v_up[...].astype(BF16), n.v_cot[...], NT).astype(BF16)
    bk = rcopy(n.back2.at[0], n.back2.at[1], n.s_bk.at[0], n.s_bk.at[1], sib)
    bk.start()

    loads["wk"].wait()
    loads["wv"].wait()
    nkv = dot(xb, n.v_wkv[...], NT)
    n.n_send[...] = jnp.concatenate([nkv, nkv], axis=1).astype(BF16)
    b4 = lax.rem(t, 4)

    def n_copy(k):
        to = t - b4 + lax.rem(b4 + k, 4)
        return rcopy(n.n_send, n.n_buf.at[b4], n.s_n.at[0], n.s_n.at[1], tdev(to))

    each(4, lambda k: n_copy(k).start(), 1)
    n.n_buf[b4] = n.n_send[...]

    loads["hid"].wait()
    pairs[0].wait_recv()
    bk.wait_recv()

    back = jnp.concatenate([n.back2[0], n.back2[1]], axis=1)

    def down_pair(pair):
        blocks = []
        for e in range(2):
            cols = pl.ds(pl.multiple_of((pair * 2 + e) * 256, 256), 256)
            both = jnp.concatenate([n.hid2[0, :, cols], n.hid2[1, :, cols]], axis=0)
            blocks.append(dot(back, both))
        rows = pl.ds(pl.multiple_of(pair * 16, 16), 16)
        for j in range(8):
            n.d_send2[j, rows, :] = stack8(*blocks, j)

    for part in range(2):
        loop(part * 4 + 4, down_pair, part * 4)
        each(3, lambda k: g2(0, part, k).start())

    def q_copy(k):
        to = 2 * far_chip(k) + y
        return rcopy(n.q_send, n.q_buf.at[t16], n.s_q.at[0], n.s_q.at[1], tdev(to))

    @pl.when(jnp.logical_not(relays))
    def _():
        q_copy(15).start()

    each(15, lambda k: q_copy(k).start())

    @pl.when(relays)
    def _():
        n.q_buf[t16] = n.q_send[...]

    for copy in pairs[1:]:
        copy.start()

    def dn_recv(slot):
        dn_y(slot, g).wait_recv()

    @pl.when(relays)
    def _():
        dn_recv(z * 2 + 1 - c)
        dn_pass(z, 1 - c)

        def pass_on(k):
            from_z = far_z(k)
            for core in range(2):
                dn_recv(from_z * 2 + core)
                dn_pass(from_z, core)

        each(7, pass_on)

    def reduce_slice(at, total):
        cols = pl.ds(pl.multiple_of(at * 256, 256), 256)
        both = jnp.concatenate([n.hid2[0, :, cols], n.hid2[1, :, cols]], axis=0)
        return total + dot(n.down_half[at], both, NT)

    pt = rcopy(n.part_send, n.part_recv, n.s_pt.at[0], n.s_pt.at[1], sib)

    @pl.when(relays)
    def _():
        total = jnp.zeros((64, 256), F32)
        for at in range(16):
            total = reduce_slice(at, total)
        n.part_send[...] = total
        pt.start()

    @pl.when(jnp.logical_not(relays))
    def _():
        total = jnp.zeros((64, 256), F32)
        for k in (7, 0, 1, 2, 3, 4, 5, 6):
            slices = [far_z(k) * 2 + core for core in range(2)]
            for at in slices:
                dn_recv(at)
            for at in slices:
                total = reduce_slice(at, total)
        n.part_send[...] = total
        pt.start()

    arrived_heads(n.q_buf, n.s_q.at[1])
    loads["fill"].wait()
    loads["k"].wait()
    loads["v"].wait()
    pairs[1].wait_recv()
    pairs[2].wait_recv()

    spot = lanes((64, 256))
    spot = jnp.where(spot < 128, t * 128 + spot, (t + 1 - 2 * c) * 128 + spot - 128)
    tile_lane = lanes((8, 128))

    def send_part(i):
        to = tdev(16 * c + i)
        stays = relays & (i == t16)

        @pl.when(jnp.logical_not(stays))
        def _():
            rcopy(n.a_send.at[i], n.a_recv.at[i0], n.s_a.at[0], n.s_a.at[1], to).start()
            rcopy(n.l_send.at[i], n.l_recv.at[i0], n.s_l.at[0], n.s_l.at[1], to).start()

        @pl.when(stays)
        def _():
            n.a_recv[i0] = n.a_send[i]
            n.l_recv[i0] = n.l_send[i]

    def pair_at(step):
        return lax.rem(step + 1 + lax.div(z, 4), 2)

    def send_parts(step):
        each(8, lambda j: send_part(pair_at(step) * 8 + j))

    def attend(step):
        pair = pair_at(step)
        cols = pl.ds(pl.multiple_of(pair * 256, 256), 256)
        qs = [n.q_buf[pair * 8 + j].astype(F32) for j in range(8)]
        none = jnp.zeros((32, 128), F32)
        outs, tops, sums = [], [], []
        for r in range(4):
            first, second = (
                jnp.concatenate([a[r * 8 : r * 8 + 8] for a in qs[h * 4 : h * 4 + 4]], axis=0)
                for h in range(2)
            )
            qr = jnp.concatenate(
                [
                    jnp.concatenate([first, none], axis=1),
                    jnp.concatenate([none, second], axis=1),
                ],
                axis=0,
            ).astype(BF16)
            keys = jnp.concatenate([n.kbuf[0, r, :, cols], n.kbuf[1, r, :, cols]], axis=0)
            values = jnp.concatenate([n.vbuf[0, r, :, cols], n.vbuf[1, r, :, cols]], axis=0)
            valid = spot < n.fill[r]
            scores = jnp.where(valid, dot(qr, keys, NT) * INV_ROOT, masked_score)
            top = jnp.max(scores, axis=1, keepdims=True)
            weights = jnp.where(valid, jnp.exp(scores - top), 0.0)
            tops.append(top)
            sums.append(jnp.sum(weights, axis=1, keepdims=True))
            outs.append(dot(weights.astype(BF16), values))
        for j in range(8):
            rows = slice(j * 8, j * 8 + 8)
            half = slice(j // 4 * 128, j // 4 * 128 + 128)
            n.a_send[pair * 8 + j] = jnp.concatenate(
                [o[rows, half] for o in outs], axis=0
            ).astype(BF16)
            tile = jnp.zeros((8, 128), F32)
            for r in range(4):
                tile = jnp.where(tile_lane == r, tops[r][rows], tile)
                tile = jnp.where(tile_lane == 64 + r, sums[r][rows], tile)
            n.l_send[pair * 8 + j] = tile

    loop(1, attend)

    stage3_out(0)
    send_parts(0)

    until = jnp.where(relays, 2, 1)
    def attend_and_send(step):
        attend(step)
        send_parts(step)

    loop(until, attend_and_send, 1)

    pt.wait_recv()
    pairs[3].wait_recv()
    reduced = jnp.concatenate(
        [
            n.part_send[:, :128] + n.part_recv[:, 128:],
            n.part_send[:, 128:] + n.part_recv[:, :128],
        ],
        axis=1,
    ).astype(BF16)

    def up_part(part):
        both = jnp.concatenate(
            [
                n.v_cot[:, pl.ds(pl.multiple_of(2560 * c + 1280 * part, 1280), 1280)],
                n.cot2[:, pl.ds(1280 * part, 1280)],
            ],
            axis=0,
        )
        n.u_tmp[...] = dot(reduced, both)
        rest = [jnp.zeros((64, 128), F32)] * 2
        quarter = lanes((64, 128)) >> 5
        for pair in range(4):
            low = []
            for e in range(2):
                first = 160 * (pair * 2 + e)
                at = first // 128 * 128
                window = n.u_tmp[:, at : at + 256]
                window = pltpu.roll(window, 256 - (first - at), 1) if first > at else window
                low.append(window[:, :128])
                high = pltpu.roll(window[:, 128:], 32 * pair, 1) if pair else window[:, 128:]
                rest[e] = jnp.where(quarter == pair, high, rest[e])
            rows = pl.ds(part * 80 + pair * 16, 16)
            for j in range(8):
                n.u_send2[j, rows, :] = stack8(*low, j)
        rows = pl.ds(part * 80 + 64, 16)
        for j in range(8):
            n.u_send2[j, rows, :] = stack8(*rest, j)
        each(3, lambda k: g2(1, part, k).start())

    each(2, up_part)

    loop(2, attend_and_send, until)

    arrived(n.n_buf, 3, n.s_n.at[1])
    fresh = [n.n_buf[j].astype(F32) for j in range(4)]
    quarter = lane >> 5
    new_k = fresh[0]
    new_v = pltpu.roll(fresh[0], 96, 1)
    for j in range(1, 4):
        new_k = jnp.where(quarter == j, pltpu.roll(fresh[j], 32 * j, 1), new_k)
        new_v = jnp.where(quarter == j, pltpu.roll(fresh[j], (32 * j + 96) % 128, 1), new_v)
    new_k = rotate(new_k).astype(BF16)
    new_v = new_v.astype(BF16)
    nrow = sublanes((32, 16))
    ncol = lanes((32, 16))
    new_valid = ((nrow >> 3) == (ncol & 3)) & ((ncol >> 2) <= (nrow & 3))
    new_scores = jnp.where(new_valid, dot(n.q_send[...], new_k, NT) * INV_ROOT, masked_score)
    new_top = jnp.max(new_scores, axis=1, keepdims=True)
    new_weights = jnp.where(new_valid, jnp.exp(new_scores - new_top), 0.0)
    new_sum = jnp.sum(new_weights, axis=1, keepdims=True)
    new_out = dot(new_weights.astype(BF16), new_v)
    new_tile = jnp.zeros((8, 128), F32)
    new_total = jnp.zeros((8, 128), F32)
    for r in range(4):
        rows = slice(r * 8, r * 8 + 8)
        new_tile = jnp.where(tile_lane == r, new_top[rows], new_tile)
        new_total = jnp.where(tile_lane == r, new_sum[rows], new_total)

    stage3_out(1)

    stage4_out(0)
    stage4_send(0)
    arrived_heads(n.a_recv, n.s_a.at[1])
    arrived_heads(n.l_recv, n.s_l.at[1])

    peak = lax.fori_loop(0, 16, lambda i, m: jnp.maximum(m, n.l_recv[i]), new_tile, unroll=True)
    scale = jnp.exp(new_tile - peak)

    def join(i, state):
        total, parts = state
        tile = n.l_recv[i]
        scale = jnp.exp(tile - peak)
        part = n.a_recv[i].astype(F32)
        return (
            total + scale * pltpu.roll(tile, 64, 1),
            [acc + part[r * 8 : r * 8 + 8] * scale[:, r : r + 1] for r, acc in enumerate(parts)],
        )

    total, parts = lax.fori_loop(
        0,
        16,
        join,
        (
            scale * new_total,
            [new_out[r * 8 : r * 8 + 8] * scale[:, r : r + 1] for r in range(4)],
        ),
        unroll=4,
    )
    for r in range(4):
        n.q_rows[r * 8 : r * 8 + 8, :] = parts[r] / total[:, r : r + 1]
    for h, rows in enumerate((n.q_rot0, n.q_rot1)):
        for r in range(4):
            rows[pl.ds(r, 4, stride=4), :] = n.q_rows[r * 8 + h * 4 : r * 8 + h * 4 + 4, :]
    att = jnp.concatenate([n.q_rot0[...], n.q_rot1[...]], axis=1).astype(BF16)
    n.att2[0] = att
    at = rcopy(n.att2.at[0], n.att2.at[1], n.s_at.at[0], n.s_at.at[1], sib)
    at.start()
    loads["wo"].wait()
    pairs[4].wait_recv()
    at.wait_recv()
    n.p_rows[...] = dot(n.att2[0], n.wo2[0]) + dot(n.att2[1], n.wo2[1])

    def out_part(part):
        for e in range(8):
            at = 160 * e // 128 * 128
            shift = 160 * e - at
            base = pl.multiple_of(part * 1280 + at, 128)
            window = n.p_rows[:, pl.ds(base, 256)]
            n.o_keep[part * 8 + e] = pltpu.roll(window, 256 - shift, 1) if shift else window

    loop(2, out_part)

    fd = n.v_down[...] - STEP_SCALE * summed(0)
    n.w_fd[...] = fd
    results = [
        pltpu.make_async_copy(src, dst, n.s_out.at[at])
        for at, (src, dst) in enumerate(
            ((n.w_dec, dec_out), (n.w_fd, fd_out), (n.w_fu, fu_out))
        )
    ]
    results[1].start()
    n.fd_pad[0:64, :] = jnp.zeros((64, 256), BF16)
    n.fd_pad[64:128, :] = fd.astype(BF16)
    n.t_send[...] = dot(att, n.fd_pad[...], NT)
    tt = rcopy(n.t_send, n.t_recv, n.s_tt.at[0], n.s_tt.at[1], sib)
    tt.start()

    up_total = stage4_out(1)
    up_total = jnp.concatenate([up_total[:8], up_total[8:]], axis=1)
    for e in range(8):
        n.f_send[e] = pltpu.roll(up_total, (256 - 20 * e) % 256, 1)[:, :128]

    def f_copy(e):
        return rcopy(n.f_send.at[e], n.f_recv.at[g], n.s_f.at[0], n.s_f.at[1], f_to(e))

    f_own = lax.rem(t, 8)

    def f_start(e):
        @pl.when(jnp.logical_not(f_self & (e == f_own)))
        def _():
            f_copy(e).start()

    each(8, f_start)

    @pl.when(f_self)
    def _():
        n.f_recv[g] = n.f_send[f_own]
    stage4_send(1)

    def o2(k):
        i = far_core(k)
        return rcopy(
            n.o_send2.at[i], n.o_recv2.at[i0], n.s_o2.at[0], n.s_o2.at[1], tdev(16 * c + i)
        )

    tt.wait_recv()
    low = n.t_send[...] + n.t_recv[...]

    def out_sum(i):
        part = n.o_keep[i]
        n.o_send2[i] = jnp.concatenate(
            [part[:, :128], jnp.where(lane < 32, part[:, 128:], low)], axis=1
        ).astype(BF16)

    lax.fori_loop(0, 16, lambda i, a: (out_sum(i), a)[1], 0, unroll=4)
    each(15, lambda k: o2(k).start())

    @pl.when(jnp.logical_not(relays))
    def _():
        o2(15).start()

    def left_heads(buf, sem, more=0):
        @pl.when(relays)
        def _():
            left(buf, 15 + more, sem)

        @pl.when(jnp.logical_not(relays))
        def _():
            left(buf, 16 + more, sem)

    @pl.when(relays)
    def _():
        left(n.down_half, 7, n.s_dn_sz.at[0])
        left(n.down_half, 16, n.s_dn_sy.at[0])

    @pl.when(jnp.logical_not(relays))
    def _():
        left(n.down_half, 8, n.s_dn_sz.at[0])

    left_heads(n.q_buf, n.s_q.at[0])
    left(n.n_buf, 3, n.s_n.at[0])
    for copy in pairs:
        copy.wait_send()
    bk.wait_send()
    pt.wait_send()
    left_heads(n.a_send, n.s_a.at[0])
    left_heads(n.l_send, n.s_l.at[0])
    left(n.d_recv2, 3, n.s_g2.at[0, 0])
    left(n.u_recv2, 3, n.s_g2.at[1, 0])
    left_heads(n.g_send3.at[0], n.s_g3.at[0, 0], 16)
    left(n.g_recv4.at[0], 7, n.s_g4.at[0, 0])

    first_col = 160 * t
    base = lax.div(first_col, 128) * 128
    up_cols = n.v_up[:, pl.ds(pl.multiple_of(base, 128), 256)]
    up_cols = pltpu.roll(up_cols, lax.rem(256 - (first_col - base), 256), 1)
    fu = up_cols - STEP_SCALE * summed(1)
    n.fu_pad[0:64, :] = jnp.zeros((64, 256), BF16)
    n.fu_pad[64:128, :] = fu.astype(BF16)

    arrived_heads(n.o_recv2, n.s_o2.at[1])
    @pl.when(relays)
    def _():
        n.o_recv2[i0] = n.o_send2[t16]

    total = lax.fori_loop(
        1, 16, lambda i, a: a + n.o_recv2[i].astype(F32), n.o_recv2[0].astype(F32), unroll=5
    )
    low = jnp.where(lane < 64, 0.0, total[:, 128:]).astype(BF16)
    decoded = total + adapter_scale * dot(low, n.fu_pad[...])
    loads["live"].wait()
    wide_row = sublanes((16, 256))
    alive = (wide_row >> 2) < by_rollout(wide_row & 3, n.live)
    n.d_rows[...] = jnp.where(alive, decoded, 0.0)
    for s in range(4):
        n.w_dec[s] = n.d_rows[s * 4 : s * 4 + 4, 0:160].astype(BF16)
    results[0].start()

    @pl.when(f_self)
    def _():
        arrived(n.f_recv, 7, n.s_f.at[1])

    @pl.when(jnp.logical_not(f_self))
    def _():
        arrived(n.f_recv, 8, n.s_f.at[1])

    first_col = 640 * g + 20 * t
    base = jnp.minimum(lax.div(first_col, 128) * 128, 5120 - 256)
    up_cols = n.v_up[:, pl.ds(pl.multiple_of(base, 128), 256)]
    up_cols = pltpu.roll(up_cols, lax.rem(256 - (first_col - base), 256), 1)[:, :128]
    sums = jnp.concatenate([n.f_recv[j] for j in range(8)], axis=0)
    piece = up_cols - STEP_SCALE * sums
    n.w_fu[...] = jnp.concatenate([piece, piece], axis=0).T[0:20, 0:64]
    results[2].start()

    left_heads(n.g_send3.at[1], n.s_g3.at[1, 0], 16)
    left(n.g_recv4.at[1], 7, n.s_g4.at[1, 0])
    at.wait_send()
    tt.wait_send()
    left_heads(n.o_send2, n.s_o2.at[0])

    @pl.when(f_self)
    def _():
        left(n.f_send, 7, n.s_f.at[0])

    @pl.when(jnp.logical_not(f_self))
    def _():
        left(n.f_send, 8, n.s_f.at[0])

    for copy in results:
        copy.wait()


def hand_out(dec, fd, fu, dec_out, fd_out, fu_out):
    dec_out[...] = dec[...]
    fd_out[...] = fd[...]
    fu_out[...] = fu[...]


def body(hid, cot, down, up, wo, wq, wk, wv, x, kc, vc, fill, start, live):
    hbm = pl.BlockSpec(memory_space=pl.ANY)
    vmem = pl.BlockSpec(memory_space=pltpu.VMEM)
    shapes = (
        jax.ShapeDtypeStruct((4, 4, 160), BF16),
        jax.ShapeDtypeStruct((64, 256), F32),
        jax.ShapeDtypeStruct((20, 64), F32),
    )
    results = pl.pallas_call(
        kernel,
        out_shape=shapes,
        in_specs=[hbm] * 14,
        out_specs=(hbm,) * 3,
        scratch_shapes=[pltpu.VMEM(shape, kind) for shape, kind in SCRATCH.values()]
        + [pltpu.SMEM((4,), jnp.int32)] * 3
        + [pltpu.SemaphoreType.DMA(shape) for shape in SEMS.values()],
        compiler_params=pltpu.CompilerParams(
            collective_id=0, has_side_effects=True, vmem_limit_bytes=56 * 2**20
        ),
        name="update_and_decode",
    )(hid, cot, down.T, up, wo, wq, wk.T, wv.T, x, kc, vc, fill, start, live)
    dec, fd, fu = pl.pallas_call(
        hand_out,
        out_shape=shapes,
        in_specs=[vmem] * 3,
        out_specs=(vmem,) * 3,
        compiler_params=pltpu.CompilerParams(vmem_limit_bytes=56 * 2**20),
        name="hand_out",
    )(*results)
    return dec, fd.T, fu.T


def solution(mesh):
    return jax.shard_map(
        body,
        mesh=mesh,
        in_specs=(
            P(("group", "tensor"), None),
            P(("group", "tensor"), None),
            P("tensor", None),
            P(),
            P("tensor", None),
            P(None, "tensor"),
            P(None, "tensor"),
            P(None, "tensor"),
            P(None, "group", None),
            P("group", "tensor", None),
            P("group", "tensor", None),
            P("group"),
            P("group"),
            P("group"),
        ),
        out_specs=(P(None, "group", "tensor"), P("tensor", None), P(None, ("group", "tensor"))),
        check_vma=False,
    )
```

```python
import math

import jax
import jax.numpy as jnp
from jax import lax
from jax.experimental import pallas as pl
from jax.experimental.pallas import tpu as pltpu
from jax.sharding import PartitionSpec as P

MESH = pl.DeviceIdType.MESH
F32 = jnp.float32
BF16 = jnp.bfloat16

adapter_scale = 0.01
rate_numerator = 50.0
rope_theta = 1000000.0
masked_score = -1e30

HD = 128
TOKENS = 32768
STEP_SCALE = adapter_scale * rate_numerator / math.sqrt(TOKENS)
INV_ROOT = 1.0 / math.sqrt(HD)

NN = (((1,), (0,)), ((), ()))
NT = (((1,), (1,)), ((), ()))


def dot(a, b, dims=NN):
    return lax.dot_general(a, b, dims, preferred_element_type=F32)


def rcopy(src, dst, ss, rs, dev):
    return pltpu.make_async_remote_copy(
        src_ref=src, dst_ref=dst, send_sem=ss, recv_sem=rs, device_id=dev, device_id_type=MESH
    )


def loop(n, fn, start=0):
    def step(k, carry):
        fn(k)
        return carry

    lax.fori_loop(start, n, step, 0)


def each(n, fn, start=0):
    for k in range(start, n):
        fn(k)


SCRATCH = dict(
    v_down=((64, 256), F32),
    v_x=((4, 4, 5120), BF16),
    x_rows=((16, 5120), F32),
    v_wq=((5120, 256), BF16),
    v_wkv=((64, 5120), BF16),
    v_up=((64, 5120), F32),
    v_cot=((128, 5120), BF16),
    cot2=((128, 2560), BF16),
    hid2=((2, 128, 4096), BF16),
    wo2=((2, 256, 2560), BF16),
    att2=((2, 16, 256), BF16),
    t_send=((16, 128), F32),
    t_recv=((16, 128), F32),
    kbuf=((2, 4, 128, 512), BF16),
    vbuf=((2, 4, 128, 512), BF16),
    down_own=((64, 256), BF16),
    down_half=((16, 64, 256), BF16),
    back2=((2, 64, 128), BF16),
    part_send=((64, 256), F32),
    part_recv=((64, 256), F32),
    q_rot0=((16, 128), F32),
    q_rot1=((16, 128), F32),
    q_rows=((32, 128), F32),
    q_send=((32, 128), BF16),
    q_buf=((16, 32, 128), BF16),
    n_buf=((4, 16, 128), BF16),
    n_send=((16, 128), BF16),
    a_send=((16, 32, 128), BF16),
    a_recv=((16, 32, 128), BF16),
    l_send=((16, 8, 128), F32),
    l_recv=((16, 8, 128), F32),
    d_send2=((8, 128, 256), BF16),
    d_recv2=((4, 2, 128, 256), BF16),
    u_send2=((8, 160, 128), BF16),
    u_recv2=((4, 2, 160, 128), BF16),
    g_send3=((2, 32, 16, 128), BF16),
    g_recv3=((2, 32, 16, 128), BF16),
    g_send4=((2, 16, 128), F32),
    g_recv4=((2, 8, 16, 128), F32),
    u_tmp=((64, 1280), F32),
    p_rows=((16, 2560), F32),
    fd_pad=((128, 256), BF16),
    fu_pad=((128, 256), BF16),
    o_keep=((16, 16, 256), F32),
    o_send2=((16, 16, 256), BF16),
    o_recv2=((16, 16, 256), BF16),
    d_rows=((16, 256), F32),
    f_send=((8, 8, 128), F32),
    f_recv=((8, 8, 128), F32),
    w_dec=((4, 4, 160), BF16),
    w_fd=((64, 256), F32),
    w_fu=((20, 64), F32),
)
SEMS = dict(
    load=(14,),
    dn_sz=(1,),
    dn_sy=(1,),
    dn_r=(16,),
    sib_s=(5,),
    sib_r=(5,),
    bk=(2,),
    pt=(2,),
    q=(2,),
    n=(2,),
    a=(2,),
    l=(2,),
    g2=(2, 2),
    g3=(2, 2),
    g4=(2, 2),
    at=(2,),
    tt=(2,),
    o2=(2,),
    f=(2,),
    out=(3,),
)


class Names:
    pass


def lanes(shape):
    return lax.broadcasted_iota(jnp.int32, shape, len(shape) - 1)


def sublanes(shape):
    return lax.broadcasted_iota(jnp.int32, shape, len(shape) - 2)


def by_rollout(rollout, ref):
    picked = jnp.where(rollout == 0, ref[0], ref[1])
    picked = jnp.where(rollout == 2, ref[2], picked)
    return jnp.where(rollout == 3, ref[3], picked)


def kernel(
    hid, cot, down, up, wo, wq, wk, wv, x, kc, vc, fill_in, start_in, live_in, dec_out, fd_out, fu_out, *refs
):
    n = Names()
    for name, ref in zip(list(SCRATCH) + ["start", "fill", "live"] + ["s_" + key for key in SEMS], refs):
        setattr(n, name, ref)
    t = lax.axis_index("tensor")
    g = lax.axis_index("group")
    c = lax.rem(t, 2)
    i0 = lax.div(t, 2)
    y = lax.div(t, 16)
    z = lax.rem(i0, 8)
    t16 = lax.rem(t, 16)
    sib = {"tensor": t + 1 - 2 * c}
    other_y = lax.rem(t + 16, 32)
    g_other = g + 1 - 2 * lax.rem(g, 2)
    gx = lax.div(g, 2)
    gy = lax.rem(g, 2)
    relays = c == y

    def tdev(index):
        return {"tensor": index}

    def gdev(index):
        return {"group": index}

    def far_z(k):
        return lax.rem(z + (4, 5, 3, 6, 2, 7, 1, 0)[k], 8)

    def far_core(k):
        return far_z(k // 2) * 2 + (c if k % 2 else 1 - c)

    def far_chip(k):
        return (y if k % 2 else 1 - y) * 8 + far_z(k // 2)

    def far_x(k):
        return lax.rem(gx + (2, 3, 1, 0)[k], 4)

    def far_group(k):
        return far_x(k % 4) * 2 + (1 - gy if k < 4 else gy)

    f_from = 4 * g + lax.div(t, 8)
    f_self = f_from == t

    def f_to(e):
        return {"group": lax.div(t, 4), "tensor": 8 * lax.rem(t, 4) + e}

    def half(size, which):
        return pl.ds(pl.multiple_of(size * which, size), size)

    loads = dict(
        down=(down, n.v_down),
        x=(x, n.v_x),
        wq=(wq, n.v_wq),
        wk=(wk, n.v_wkv.at[pl.ds(0, 32)]),
        wv=(wv, n.v_wkv.at[pl.ds(32, 32)]),
        up=(up, n.v_up),
        cot=(cot, n.v_cot),
        hid=(hid.at[:, half(4096, c)], n.hid2.at[0]),
        k=(kc.at[:, :, half(512, c)], n.kbuf.at[0]),
        v=(vc.at[:, :, half(512, c)], n.vbuf.at[0]),
        wo=(wo.at[:, half(2560, c)], n.wo2.at[0]),
        start=(start_in, n.start),
        fill=(fill_in, n.fill),
        live=(live_in, n.live),
    )
    loads = {
        key: pltpu.make_async_copy(src, dst, n.s_load.at[at])
        for at, (key, (src, dst)) in enumerate(loads.items())
    }
    for copy in loads.values():
        copy.start()

    def arrived(buf, count, sem):
        part = buf.at[pl.ds(0, count)]
        rcopy(part, part, sem, sem, sib).wait_recv()

    def left(buf, count, sem):
        part = buf.at[pl.ds(0, count)]
        rcopy(part, part, sem, sem, sib).wait_send()

    def arrived_heads(buf, sem, more=0):
        @pl.when(relays)
        def _():
            arrived(buf, 15 + more, sem)

        @pl.when(jnp.logical_not(relays))
        def _():
            arrived(buf, 16 + more, sem)

    barrier = pltpu.get_barrier_semaphore()
    def t_greet(k):
        pl.semaphore_signal(
            barrier, inc=1, device_id=tdev(lax.rem(t + k, 32)), device_id_type=MESH
        )

    near = (1, 31, 16, 15, 17)
    for k in near:
        t_greet(k)
    each(
        8,
        lambda k: pl.semaphore_signal(
            barrier, inc=1, device_id=gdev(lax.rem(g + k, 8)), device_id_type=MESH
        ),
        1,
    )

    pl.semaphore_signal(
        barrier,
        inc=1,
        device_id={"group": g_other, "tensor": other_y},
        device_id_type=MESH,
    )

    each(
        16,
        lambda k: pl.semaphore_signal(
            barrier,
            inc=1,
            device_id={"group": g_other, "tensor": 2 * k + y},
            device_id_type=MESH,
        ),
    )

    def f_greet(j):
        pl.semaphore_signal(
            barrier, inc=1, device_id={"group": j, "tensor": f_from}, device_id_type=MESH
        )

    each(8, lambda k: f_greet(lax.rem(g + k, 8)), 1)

    @pl.when(jnp.logical_not(f_self))
    def _():
        f_greet(g)

    for k in range(1, 32):
        if k not in near:
            t_greet(k)

    loads["down"].wait()
    n.down_own[...] = n.v_down[...].astype(BF16)

    pl.semaphore_wait(barrier, 63 - f_self.astype(jnp.int32))

    def dn_z(k):
        to = y * 16 + far_z(k) * 2 + y
        return rcopy(
            n.down_own, n.down_half.at[t16], n.s_dn_sz.at[0], n.s_dn_r.at[t16], tdev(to)
        )

    def dn_y(slot, group):
        return rcopy(
            n.down_half.at[slot],
            n.down_half.at[slot],
            n.s_dn_sy.at[0],
            n.s_dn_r.at[slot],
            {"group": group, "tensor": other_y},
        )

    def dn_pass(z_of, core):
        dn_y(z_of * 2 + core, g + core * (g_other - g)).start()

    each(7, lambda k: dn_z(k).start())

    @pl.when(relays)
    def _():
        n.down_half[t16] = n.down_own[...]
        dn_pass(z, c)

    @pl.when(jnp.logical_not(relays))
    def _():
        dn_z(7).start()

    pairs = [
        rcopy(src, dst, n.s_sib_s.at[at], n.s_sib_r.at[at], sib)
        for at, (src, dst) in enumerate(
            (
                (hid.at[:, half(4096, 1 - c)], n.hid2.at[1]),
                (kc.at[:, :, half(512, 1 - c)], n.kbuf.at[1]),
                (vc.at[:, :, half(512, 1 - c)], n.vbuf.at[1]),
                (cot.at[:, half(2560, 1 - c)], n.cot2),
                (wo.at[:, half(2560, 1 - c)], n.wo2.at[1]),
            )
        )
    ]
    pairs[0].start()

    loads["x"].wait()
    for s in range(4):
        n.x_rows[s * 4 : s * 4 + 4, :] = n.v_x[s].astype(F32)
    xb = n.x_rows[...].astype(BF16)
    row = sublanes((16, HD))
    lane = lanes((16, HD))
    loads["start"].wait()
    position = (by_rollout(row & 3, n.start) + (row >> 2)).astype(F32)
    freq = jnp.exp((lane & 63).astype(F32) * (-math.log(rope_theta) * 2.0 / HD))
    angle = position * freq
    cosine = jnp.cos(angle)
    sine = jnp.where(lane < 64, -jnp.sin(angle), jnp.sin(angle))

    def rotate(v):
        v = v.astype(BF16).astype(F32)
        return v * cosine + pltpu.roll(v, 64, 1) * sine

    loads["wq"].wait()
    q = dot(xb, n.v_wq[...])
    for h, rows in enumerate((n.q_rot0, n.q_rot1)):
        rows[...] = rotate(q[:, h * HD : (h + 1) * HD])
        for r in range(4):
            n.q_rows[r * 8 + h * 4 : r * 8 + h * 4 + 4, :] = rows[pl.ds(r, 4, stride=4), :]
    n.q_send[...] = n.q_rows[...].astype(BF16)

    send2 = (n.d_send2, n.u_send2)
    recv2 = (n.d_recv2, n.u_recv2)

    def g2(u, part, k):
        to = far_x(k)
        size = (64, 80)[u]
        rows = pl.ds(part * size, size)
        return rcopy(
            send2[u].at[pl.ds(2 * to, 2), rows],
            recv2[u].at[gx, :, rows],
            n.s_g2.at[u, 0],
            n.s_g2.at[u, 1],
            gdev(2 * to + gy),
        )

    def g3(u, half, k):
        i = far_core(k)
        return rcopy(
            n.g_send3.at[u, half * 16 + i],
            n.g_recv3.at[u, gy * 16 + i0],
            n.s_g3.at[u, 0],
            n.s_g3.at[u, 1],
            {"group": 2 * gx + half, "tensor": 16 * c + i},
        )

    def g4(u, k):
        j = far_group(k)
        return rcopy(
            n.g_send4.at[u], n.g_recv4.at[u, g], n.s_g4.at[u, 0], n.s_g4.at[u, 1], gdev(j)
        )

    def stack8(first, second, j):
        rows = slice(j * 8, j * 8 + 8)
        return jnp.concatenate([first[rows], second[rows]], axis=0).astype(BF16)

    def stage3_out(u):
        arrived(recv2[u], 3, n.s_g2.at[u, 1])

        def total(half, row):
            rows = pl.ds(pl.multiple_of(row, 16), 16)
            sums = send2[u][2 * gx + half, rows, :].astype(F32)
            for dx in range(1, 4):
                sums = sums + recv2[u][lax.rem(gx + dx, 4), half, rows, :].astype(F32)
            return sums

        def send(i, low, high):
            n.g_send3[u, i] = jnp.concatenate([low, high], axis=0).astype(BF16)

        def down_sum(pair):
            for half in range(2):
                sums = total(half, pair * 16)
                for e in range(2):
                    piece = sums[e * 8 : e * 8 + 8]
                    send(half * 16 + pair * 2 + e, piece[:, :128], piece[:, 128:])

        def up_sum(part):
            for half in range(2):
                rest = total(half, part * 80 + 64)
                for pair in range(4):
                    sums = total(half, part * 80 + pair * 16)
                    high = pltpu.roll(rest, 128 - 32 * pair, 1) if pair else rest
                    for e in range(2):
                        rows = slice(e * 8, e * 8 + 8)
                        send(half * 16 + part * 8 + pair * 2 + e, sums[rows], high[rows])

        if u == 0:
            loop(8, down_sum)
        else:
            loop(2, up_sum)

        def both(k):
            g3(u, 1 - gy, k).start()
            g3(u, gy, k).start()

        each(15, both)
        g3(u, 1 - gy, 15).start()

        @pl.when(jnp.logical_not(relays))
        def _():
            g3(u, gy, 15).start()

    def stage4_out(u):
        arrived_heads(n.g_recv3.at[u], n.s_g3.at[u, 1], 16)

        @pl.when(relays)
        def _():
            n.g_recv3[u, gy * 16 + i0] = n.g_send3[u, gy * 16 + t16]

        sums = [n.g_recv3[u, i].astype(F32) for i in range(4)]
        for i in range(4, 32):
            sums[i % 4] = sums[i % 4] + n.g_recv3[u, i].astype(F32)
        total = (sums[0] + sums[1]) + (sums[2] + sums[3])
        n.g_send4[u] = total
        n.g_recv4[u, g] = total
        return total

    def stage4_send(u):
        each(7, lambda k: g4(u, k).start())

    def summed(u):
        arrived(n.g_recv4.at[u], 7, n.s_g4.at[u, 1])
        pieces = [n.g_recv4[u, j] for j in range(8)]
        return jnp.concatenate(
            [jnp.concatenate([p[:8], p[8:]], axis=1) for p in pieces], axis=0
        )

    loads["up"].wait()
    loads["cot"].wait()
    n.back2[0] = dot(n.v_up[...].astype(BF16), n.v_cot[...], NT).astype(BF16)
    bk = rcopy(n.back2.at[0], n.back2.at[1], n.s_bk.at[0], n.s_bk.at[1], sib)
    bk.start()

    loads["wk"].wait()
    loads["wv"].wait()
    nkv = dot(xb, n.v_wkv[...], NT)
    n.n_send[...] = jnp.concatenate([nkv, nkv], axis=1).astype(BF16)
    b4 = lax.rem(t, 4)

    def n_copy(k):
        to = t - b4 + lax.rem(b4 + k, 4)
        return rcopy(n.n_send, n.n_buf.at[b4], n.s_n.at[0], n.s_n.at[1], tdev(to))

    each(4, lambda k: n_copy(k).start(), 1)
    n.n_buf[b4] = n.n_send[...]

    loads["hid"].wait()
    pairs[0].wait_recv()
    bk.wait_recv()

    back = jnp.concatenate([n.back2[0], n.back2[1]], axis=1)

    def down_pair(pair):
        blocks = []
        for e in range(2):
            cols = pl.ds(pl.multiple_of((pair * 2 + e) * 256, 256), 256)
            both = jnp.concatenate([n.hid2[0, :, cols], n.hid2[1, :, cols]], axis=0)
            blocks.append(dot(back, both))
        rows = pl.ds(pl.multiple_of(pair * 16, 16), 16)
        for j in range(8):
            n.d_send2[j, rows, :] = stack8(*blocks, j)

    for part in range(2):
        loop(part * 4 + 4, down_pair, part * 4)
        each(3, lambda k: g2(0, part, k).start())

    def q_copy(k):
        to = 2 * far_chip(k) + y
        return rcopy(n.q_send, n.q_buf.at[t16], n.s_q.at[0], n.s_q.at[1], tdev(to))

    @pl.when(jnp.logical_not(relays))
    def _():
        q_copy(15).start()

    each(15, lambda k: q_copy(k).start())

    @pl.when(relays)
    def _():
        n.q_buf[t16] = n.q_send[...]

    for copy in pairs[1:]:
        copy.start()

    def dn_recv(slot):
        dn_y(slot, g).wait_recv()

    @pl.when(relays)
    def _():
        dn_recv(z * 2 + 1 - c)
        dn_pass(z, 1 - c)

        def pass_on(k):
            from_z = far_z(k)
            for core in range(2):
                dn_recv(from_z * 2 + core)
                dn_pass(from_z, core)

        each(7, pass_on)

    def reduce_slice(at, total):
        cols = pl.ds(pl.multiple_of(at * 256, 256), 256)
        both = jnp.concatenate([n.hid2[0, :, cols], n.hid2[1, :, cols]], axis=0)
        return total + dot(n.down_half[at], both, NT)

    pt = rcopy(n.part_send, n.part_recv, n.s_pt.at[0], n.s_pt.at[1], sib)

    @pl.when(relays)
    def _():
        total = jnp.zeros((64, 256), F32)
        for at in range(16):
            total = reduce_slice(at, total)
        n.part_send[...] = total
        pt.start()

    @pl.when(jnp.logical_not(relays))
    def _():
        total = jnp.zeros((64, 256), F32)
        for k in (7, 0, 1, 2, 3, 4, 5, 6):
            slices = [far_z(k) * 2 + core for core in range(2)]
            for at in slices:
                dn_recv(at)
            for at in slices:
                total = reduce_slice(at, total)
        n.part_send[...] = total
        pt.start()

    arrived_heads(n.q_buf, n.s_q.at[1])
    loads["fill"].wait()
    loads["k"].wait()
    loads["v"].wait()
    pairs[1].wait_recv()
    pairs[2].wait_recv()

    spot = lanes((64, 256))
    spot = jnp.where(spot < 128, t * 128 + spot, (t + 1 - 2 * c) * 128 + spot - 128)
    tile_lane = lanes((8, 128))

    def send_part(i):
        to = tdev(16 * c + i)
        stays = relays & (i == t16)

        @pl.when(jnp.logical_not(stays))
        def _():
            rcopy(n.a_send.at[i], n.a_recv.at[i0], n.s_a.at[0], n.s_a.at[1], to).start()
            rcopy(n.l_send.at[i], n.l_recv.at[i0], n.s_l.at[0], n.s_l.at[1], to).start()

        @pl.when(stays)
        def _():
            n.a_recv[i0] = n.a_send[i]
            n.l_recv[i0] = n.l_send[i]

    def pair_at(step):
        return lax.rem(step + 1 + lax.div(z, 4), 2)

    def send_parts(step):
        each(8, lambda j: send_part(pair_at(step) * 8 + j))

    def attend(step):
        pair = pair_at(step)
        cols = pl.ds(pl.multiple_of(pair * 256, 256), 256)
        qs = [n.q_buf[pair * 8 + j].astype(F32) for j in range(8)]
        none = jnp.zeros((32, 128), F32)
        outs, tops, sums = [], [], []
        for r in range(4):
            first, second = (
                jnp.concatenate([a[r * 8 : r * 8 + 8] for a in qs[h * 4 : h * 4 + 4]], axis=0)
                for h in range(2)
            )
            qr = jnp.concatenate(
                [
                    jnp.concatenate([first, none], axis=1),
                    jnp.concatenate([none, second], axis=1),
                ],
                axis=0,
            ).astype(BF16)
            keys = jnp.concatenate([n.kbuf[0, r, :, cols], n.kbuf[1, r, :, cols]], axis=0)
            values = jnp.concatenate([n.vbuf[0, r, :, cols], n.vbuf[1, r, :, cols]], axis=0)
            valid = spot < n.fill[r]
            scores = jnp.where(valid, dot(qr, keys, NT) * INV_ROOT, masked_score)
            top = jnp.max(scores, axis=1, keepdims=True)
            weights = jnp.where(valid, jnp.exp(scores - top), 0.0)
            tops.append(top)
            sums.append(jnp.sum(weights, axis=1, keepdims=True))
            outs.append(dot(weights.astype(BF16), values))
        for j in range(8):
            rows = slice(j * 8, j * 8 + 8)
            half = slice(j // 4 * 128, j // 4 * 128 + 128)
            n.a_send[pair * 8 + j] = jnp.concatenate(
                [o[rows, half] for o in outs], axis=0
            ).astype(BF16)
            tile = jnp.zeros((8, 128), F32)
            for r in range(4):
                tile = jnp.where(tile_lane == r, tops[r][rows], tile)
                tile = jnp.where(tile_lane == 64 + r, sums[r][rows], tile)
            n.l_send[pair * 8 + j] = tile

    first = jnp.where(relays, 1, 0)
    loop(first, attend)

    stage3_out(0)
    loop(first, send_parts)

    until = jnp.where(relays, 2, 1)
    def attend_and_send(step):
        attend(step)
        send_parts(step)

    loop(until, attend_and_send, first)

    pt.wait_recv()
    pairs[3].wait_recv()
    reduced = jnp.concatenate(
        [
            n.part_send[:, :128] + n.part_recv[:, 128:],
            n.part_send[:, 128:] + n.part_recv[:, :128],
        ],
        axis=1,
    ).astype(BF16)

    def up_part(part):
        both = jnp.concatenate(
            [
                n.v_cot[:, pl.ds(pl.multiple_of(2560 * c + 1280 * part, 1280), 1280)],
                n.cot2[:, pl.ds(1280 * part, 1280)],
            ],
            axis=0,
        )
        n.u_tmp[...] = dot(reduced, both)
        rest = [jnp.zeros((64, 128), F32)] * 2
        quarter = lanes((64, 128)) >> 5
        for pair in range(4):
            low = []
            for e in range(2):
                first = 160 * (pair * 2 + e)
                at = first // 128 * 128
                window = n.u_tmp[:, at : at + 256]
                window = pltpu.roll(window, 256 - (first - at), 1) if first > at else window
                low.append(window[:, :128])
                high = pltpu.roll(window[:, 128:], 32 * pair, 1) if pair else window[:, 128:]
                rest[e] = jnp.where(quarter == pair, high, rest[e])
            rows = pl.ds(part * 80 + pair * 16, 16)
            for j in range(8):
                n.u_send2[j, rows, :] = stack8(*low, j)
        rows = pl.ds(part * 80 + 64, 16)
        for j in range(8):
            n.u_send2[j, rows, :] = stack8(*rest, j)
        each(3, lambda k: g2(1, part, k).start())

    each(2, up_part)

    loop(2, attend_and_send, until)

    arrived(n.n_buf, 3, n.s_n.at[1])
    fresh = [n.n_buf[j].astype(F32) for j in range(4)]
    quarter = lane >> 5
    new_k = fresh[0]
    new_v = pltpu.roll(fresh[0], 96, 1)
    for j in range(1, 4):
        new_k = jnp.where(quarter == j, pltpu.roll(fresh[j], 32 * j, 1), new_k)
        new_v = jnp.where(quarter == j, pltpu.roll(fresh[j], (32 * j + 96) % 128, 1), new_v)
    new_k = rotate(new_k).astype(BF16)
    new_v = new_v.astype(BF16)
    nrow = sublanes((32, 16))
    ncol = lanes((32, 16))
    new_valid = ((nrow >> 3) == (ncol & 3)) & ((ncol >> 2) <= (nrow & 3))
    new_scores = jnp.where(new_valid, dot(n.q_send[...], new_k, NT) * INV_ROOT, masked_score)
    new_top = jnp.max(new_scores, axis=1, keepdims=True)
    new_weights = jnp.where(new_valid, jnp.exp(new_scores - new_top), 0.0)
    new_sum = jnp.sum(new_weights, axis=1, keepdims=True)
    new_out = dot(new_weights.astype(BF16), new_v)
    new_tile = jnp.zeros((8, 128), F32)
    new_total = jnp.zeros((8, 128), F32)
    for r in range(4):
        rows = slice(r * 8, r * 8 + 8)
        new_tile = jnp.where(tile_lane == r, new_top[rows], new_tile)
        new_total = jnp.where(tile_lane == r, new_sum[rows], new_total)

    stage4_out(0)
    stage4_send(0)
    stage3_out(1)

    arrived_heads(n.a_recv, n.s_a.at[1])
    arrived_heads(n.l_recv, n.s_l.at[1])

    peak = lax.fori_loop(0, 16, lambda i, m: jnp.maximum(m, n.l_recv[i]), new_tile, unroll=True)
    scale = jnp.exp(new_tile - peak)

    def join(i, state):
        total, parts = state
        tile = n.l_recv[i]
        scale = jnp.exp(tile - peak)
        part = n.a_recv[i].astype(F32)
        return (
            total + scale * pltpu.roll(tile, 64, 1),
            [acc + part[r * 8 : r * 8 + 8] * scale[:, r : r + 1] for r, acc in enumerate(parts)],
        )

    total, parts = lax.fori_loop(
        0,
        16,
        join,
        (
            scale * new_total,
            [new_out[r * 8 : r * 8 + 8] * scale[:, r : r + 1] for r in range(4)],
        ),
        unroll=4,
    )
    for r in range(4):
        n.q_rows[r * 8 : r * 8 + 8, :] = parts[r] / total[:, r : r + 1]
    for h, rows in enumerate((n.q_rot0, n.q_rot1)):
        for r in range(4):
            rows[pl.ds(r, 4, stride=4), :] = n.q_rows[r * 8 + h * 4 : r * 8 + h * 4 + 4, :]
    att = jnp.concatenate([n.q_rot0[...], n.q_rot1[...]], axis=1).astype(BF16)
    n.att2[0] = att
    at = rcopy(n.att2.at[0], n.att2.at[1], n.s_at.at[0], n.s_at.at[1], sib)
    at.start()
    loads["wo"].wait()
    pairs[4].wait_recv()
    at.wait_recv()
    n.p_rows[...] = dot(n.att2[0], n.wo2[0]) + dot(n.att2[1], n.wo2[1])

    def out_part(part):
        for e in range(8):
            at = 160 * e // 128 * 128
            shift = 160 * e - at
            base = pl.multiple_of(part * 1280 + at, 128)
            window = n.p_rows[:, pl.ds(base, 256)]
            n.o_keep[part * 8 + e] = pltpu.roll(window, 256 - shift, 1) if shift else window

    loop(2, out_part)

    fd = n.v_down[...] - STEP_SCALE * summed(0)
    n.w_fd[...] = fd
    results = [
        pltpu.make_async_copy(src, dst, n.s_out.at[at])
        for at, (src, dst) in enumerate(
            ((n.w_dec, dec_out), (n.w_fd, fd_out), (n.w_fu, fu_out))
        )
    ]
    results[1].start()
    n.fd_pad[0:64, :] = jnp.zeros((64, 256), BF16)
    n.fd_pad[64:128, :] = fd.astype(BF16)
    n.t_send[...] = dot(att, n.fd_pad[...], NT)
    tt = rcopy(n.t_send, n.t_recv, n.s_tt.at[0], n.s_tt.at[1], sib)
    tt.start()

    def o2(k):
        i = far_core(k)
        return rcopy(
            n.o_send2.at[i], n.o_recv2.at[i0], n.s_o2.at[0], n.s_o2.at[1], tdev(16 * c + i)
        )

    tt.wait_recv()
    low = n.t_send[...] + n.t_recv[...]

    def out_sum(i):
        part = n.o_keep[i]
        n.o_send2[i] = jnp.concatenate(
            [part[:, :128], jnp.where(lane < 32, part[:, 128:], low)], axis=1
        ).astype(BF16)

    lax.fori_loop(0, 16, lambda i, a: (out_sum(i), a)[1], 0, unroll=4)
    each(15, lambda k: o2(k).start())

    @pl.when(jnp.logical_not(relays))
    def _():
        o2(15).start()

    up_total = stage4_out(1)
    up_total = jnp.concatenate([up_total[:8], up_total[8:]], axis=1)
    for e in range(8):
        n.f_send[e] = pltpu.roll(up_total, (256 - 20 * e) % 256, 1)[:, :128]

    def f_copy(e):
        return rcopy(n.f_send.at[e], n.f_recv.at[g], n.s_f.at[0], n.s_f.at[1], f_to(e))

    f_own = lax.rem(t, 8)

    def f_start(e):
        @pl.when(jnp.logical_not(f_self & (e == f_own)))
        def _():
            f_copy(e).start()

    each(8, f_start)

    @pl.when(f_self)
    def _():
        n.f_recv[g] = n.f_send[f_own]
    stage4_send(1)

    def left_heads(buf, sem, more=0):
        @pl.when(relays)
        def _():
            left(buf, 15 + more, sem)

        @pl.when(jnp.logical_not(relays))
        def _():
            left(buf, 16 + more, sem)

    @pl.when(relays)
    def _():
        left(n.down_half, 7, n.s_dn_sz.at[0])
        left(n.down_half, 16, n.s_dn_sy.at[0])

    @pl.when(jnp.logical_not(relays))
    def _():
        left(n.down_half, 8, n.s_dn_sz.at[0])

    left_heads(n.q_buf, n.s_q.at[0])
    left(n.n_buf, 3, n.s_n.at[0])
    for copy in pairs:
        copy.wait_send()
    bk.wait_send()
    pt.wait_send()
    left_heads(n.a_send, n.s_a.at[0])
    left_heads(n.l_send, n.s_l.at[0])
    left(n.d_recv2, 3, n.s_g2.at[0, 0])
    left(n.u_recv2, 3, n.s_g2.at[1, 0])
    left_heads(n.g_send3.at[0], n.s_g3.at[0, 0], 16)
    left(n.g_recv4.at[0], 7, n.s_g4.at[0, 0])

    first_col = 160 * t
    base = lax.div(first_col, 128) * 128
    up_cols = n.v_up[:, pl.ds(pl.multiple_of(base, 128), 256)]
    up_cols = pltpu.roll(up_cols, lax.rem(256 - (first_col - base), 256), 1)
    fu = up_cols - STEP_SCALE * summed(1)
    n.fu_pad[0:64, :] = jnp.zeros((64, 256), BF16)
    n.fu_pad[64:128, :] = fu.astype(BF16)

    arrived_heads(n.o_recv2, n.s_o2.at[1])
    @pl.when(relays)
    def _():
        n.o_recv2[i0] = n.o_send2[t16]

    total = lax.fori_loop(
        1, 16, lambda i, a: a + n.o_recv2[i].astype(F32), n.o_recv2[0].astype(F32), unroll=5
    )
    low = jnp.where(lane < 64, 0.0, total[:, 128:]).astype(BF16)
    decoded = total + adapter_scale * dot(low, n.fu_pad[...])
    loads["live"].wait()
    wide_row = sublanes((16, 256))
    alive = (wide_row >> 2) < by_rollout(wide_row & 3, n.live)
    n.d_rows[...] = jnp.where(alive, decoded, 0.0)
    for s in range(4):
        n.w_dec[s] = n.d_rows[s * 4 : s * 4 + 4, 0:160].astype(BF16)
    results[0].start()

    @pl.when(f_self)
    def _():
        arrived(n.f_recv, 7, n.s_f.at[1])

    @pl.when(jnp.logical_not(f_self))
    def _():
        arrived(n.f_recv, 8, n.s_f.at[1])

    first_col = 640 * g + 20 * t
    base = jnp.minimum(lax.div(first_col, 128) * 128, 5120 - 256)
    up_cols = n.v_up[:, pl.ds(pl.multiple_of(base, 128), 256)]
    up_cols = pltpu.roll(up_cols, lax.rem(256 - (first_col - base), 256), 1)[:, :128]
    sums = jnp.concatenate([n.f_recv[j] for j in range(8)], axis=0)
    piece = up_cols - STEP_SCALE * sums
    n.w_fu[...] = jnp.concatenate([piece, piece], axis=0).T[0:20, 0:64]
    results[2].start()

    left_heads(n.g_send3.at[1], n.s_g3.at[1, 0], 16)
    left(n.g_recv4.at[1], 7, n.s_g4.at[1, 0])
    at.wait_send()
    tt.wait_send()
    left_heads(n.o_send2, n.s_o2.at[0])

    @pl.when(f_self)
    def _():
        left(n.f_send, 7, n.s_f.at[0])

    @pl.when(jnp.logical_not(f_self))
    def _():
        left(n.f_send, 8, n.s_f.at[0])

    for copy in results:
        copy.wait()


def hand_out(dec, fd, fu, dec_out, fd_out, fu_out):
    dec_out[...] = dec[...]
    fd_out[...] = fd[...]
    fu_out[...] = fu[...]


def body(hid, cot, down, up, wo, wq, wk, wv, x, kc, vc, fill, start, live):
    hbm = pl.BlockSpec(memory_space=pl.ANY)
    vmem = pl.BlockSpec(memory_space=pltpu.VMEM)
    shapes = (
        jax.ShapeDtypeStruct((4, 4, 160), BF16),
        jax.ShapeDtypeStruct((64, 256), F32),
        jax.ShapeDtypeStruct((20, 64), F32),
    )
    results = pl.pallas_call(
        kernel,
        out_shape=shapes,
        in_specs=[hbm] * 14,
        out_specs=(hbm,) * 3,
        scratch_shapes=[pltpu.VMEM(shape, kind) for shape, kind in SCRATCH.values()]
        + [pltpu.SMEM((4,), jnp.int32)] * 3
        + [pltpu.SemaphoreType.DMA(shape) for shape in SEMS.values()],
        compiler_params=pltpu.CompilerParams(
            collective_id=0, has_side_effects=True, vmem_limit_bytes=56 * 2**20
        ),
        name="update_and_decode",
    )(hid, cot, down.T, up, wo, wq, wk.T, wv.T, x, kc, vc, fill, start, live)
    dec, fd, fu = pl.pallas_call(
        hand_out,
        out_shape=shapes,
        in_specs=[vmem] * 3,
        out_specs=(vmem,) * 3,
        compiler_params=pltpu.CompilerParams(vmem_limit_bytes=56 * 2**20),
        name="hand_out",
    )(*results)
    return dec, fd.T, fu.T


def solution(mesh):
    return jax.shard_map(
        body,
        mesh=mesh,
        in_specs=(
            P(("group", "tensor"), None),
            P(("group", "tensor"), None),
            P("tensor", None),
            P(),
            P("tensor", None),
            P(None, "tensor"),
            P(None, "tensor"),
            P(None, "tensor"),
            P(None, "group", None),
            P("group", "tensor", None),
            P("group", "tensor", None),
            P("group"),
            P("group"),
            P("group"),
        ),
        out_specs=(P(None, "group", "tensor"), P("tensor", None), P(None, ("group", "tensor"))),
        check_vma=False,
    )
```
